32 devices in a mesh: item: 4 (over y, x), row: 4 (over z), pair: 2 (over core).
Axes of the slice: x: 2, y: 2, z: 4, core: 2. Of those that a mesh axis runs over, the one named last changes fastest.
Arguments:
- image: bfloat16 [4, 32, 512, 128], P('item', 'row', 'pair'), may hold values from -6 to 6
- land_mask: int32 [4, 32, 512], P('item', 'row', 'pair'), may hold values 0 or 1
- embedding: bfloat16 [4, 512], P('item'), may hold values from -6 to 6
- input_gain: float32 [128], replicated, may hold values from 0.5 to 1.5
- input_shift: float32 [128], replicated, may hold values from -3 to 3
- first_kernel: bfloat16 [3, 3, 128, 256], replicated, may hold values from -0.1875 to 0.1875
- first_bias: float32 [256], replicated, may hold values from -3 to 3
- film_weight: bfloat16 [512, 512], replicated, may hold values from -0.125 to 0.125
- film_bias: float32 [512], replicated, may hold values from -1.75 to 1.75
- middle_gain: float32 [256], replicated, may hold values from 0.5 to 1.5
- middle_shift: float32 [256], replicated, may hold values from -3 to 3
- second_kernel: bfloat16 [3, 3, 256, 256], replicated, may hold values from -0.125 to 0.125
- second_bias: float32 [256], replicated, may hold values from -3 to 3
- skip_weight: bfloat16 [128, 256], replicated, may hold values from -0.5 to 0.5
- skip_bias: float32 [256], replicated, may hold values from -3 to 3
- features: bfloat16 [4, 64, 64, 256], P('item', 'row', 'pair'), may hold values from -6 to 6
- token_land: int32 [4, 64, 64], P('item', 'row', 'pair'), may hold values 0 or 1
- attend_gain: float32 [256], replicated, may hold values from 0.5 to 1.5
- attend_shift: float32 [256], replicated, may hold values from -3 to 3
- mixing_weight: bfloat16 [256, 768], replicated, may hold values from -0.375 to 0.375
- mixing_bias: float32 [512], replicated, may hold values from -1.75 to 1.75
- output_weight: bfloat16 [256, 256], replicated, may hold values from -6 to 6
- output_bias: float32 [256], replicated, may hold values from -1.75 to 1.75
- grad_pooled: bfloat16 [4, 16, 256, 256], P('item', 'row', 'pair'), may hold values from -6 to 6
- grad_result: bfloat16 [4, 64, 64, 256], P('item', 'row', 'pair'), may hold values from -6 to 6
Outputs:
- pooled: bfloat16 [4, 16, 256, 256], P('item', 'row', 'pair')
- result: bfloat16 [4, 64, 64, 256], P('item', 'row', 'pair')
- image_grad: bfloat16 [4, 32, 512, 128], P('item', 'row', 'pair')
- features_grad: bfloat16 [4, 64, 64, 256], P('item', 'row', 'pair')
- input_gain_grad: float32 [128], replicated
- input_shift_grad: float32 [128], replicated
- first_kernel_grad: float32 [3, 3, 128, 256], replicated
- first_bias_grad: float32 [256], replicated
- film_weight_grad: float32 [512, 512], replicated
- film_bias_grad: float32 [512], replicated
- middle_gain_grad: float32 [256], replicated
- middle_shift_grad: float32 [256], replicated
- second_kernel_grad: float32 [3, 3, 256, 256], replicated
- second_bias_grad: float32 [256], replicated
- skip_weight_grad: float32 [128, 256], replicated
- skip_bias_grad: float32 [256], replicated
- attend_gain_grad: float32 [256], replicated
- attend_shift_grad: float32 [256], replicated
- mixing_weight_grad: float32 [256, 768], replicated
- mixing_bias_grad: float32 [512], replicated
- output_weight_grad: float32 [256, 256], replicated
- output_bias_grad: float32 [256], replicated
- rms_values: float32 [5], replicated
The draws below stay inside these ranges and needn't reach their ends.
All inputs are finite; a program needn't handle non-finite values. No bound on the sum of `land_mask` or of `token_land` on one device may be relied on, other than what follows from the above.
Results may differ from the reference program's by a relative error of at most 0.012.
The reference program's roundings to bfloat16 on the way count: a program that leaves them out, or rounds other values in their place, can miss the bound.
Values may be sent and summed in bfloat16 or wider, within the bound.
A program may use at most 128 MiB of HBM per device.

```python
import math
import jax
import jax.numpy as jnp
from jax import lax

C_IN = 128
C_OUT = 256
EMB = 512
GROUPS = 32
AH = 64
AW = 64
ITEMS = 4
H = 32
W = 512


def plant(drawn, own_key, smallest, top_value):
    longest = drawn.shape.index(max(drawn.shape))
    spots = []
    for shift in (0, 1):
        where = [jax.random.randint(jax.random.fold_in(own_key, axis), (), 0, length) for axis, length in enumerate(drawn.shape)]
        where[longest] = (where[longest] + shift) % drawn.shape[longest]
        spots.append(tuple(where))
    return drawn.at[spots[0]].set(smallest).at[spots[1]].set(top_value)


def levels(key, dims, pieces, low, top_value):
    def one(dim, parts):
        heights = jax.random.uniform(jax.random.fold_in(jax.random.fold_in(key, 6), dim), (parts,), jnp.float32, low / len(pieces), top_value / len(pieces))
        return jnp.repeat(jnp.exp(heights), dims[dim] // parts).reshape((-1,) + (1,) * (len(dims) - dim - 1))

    level = one(*pieces[0])
    for cut in pieces[1:]:
        level = level * one(*cut)
    return level


def noise(own_key, extent, scale, bound, cuts=(), kind=jnp.bfloat16):
    array = scale * jax.random.normal(own_key, extent, jnp.float32)
    if cuts:
        array = array * levels(own_key, extent, cuts, -0.22, 0.18)
    return jnp.clip(array, -bound, bound).astype(kind)


def setup_inputs(seed: int = 0) -> dict:
    streams_of = jax.random.split(jax.random.key(seed), 26)
    image = noise(streams_of[0], (ITEMS, H, W, C_IN), 1.0, 6.0, ((0, 4), (1, 4), (2, 2)))
    land_mask = plant((jax.random.randint(streams_of[1], (ITEMS, H, W), 0, 5) < 2).astype(jnp.int32), jax.random.fold_in(streams_of[1], 1), 0, 1)
    embedding = noise(streams_of[2], (ITEMS, EMB), 1.0, 6.0, ((0, 4),))
    input_gain = jnp.clip(1.0 + 0.1 * jax.random.normal(streams_of[3], (C_IN,), jnp.float32), 0.5, 1.5)
    input_shift = noise(streams_of[4], (C_IN,), 0.5, 3.0, (), jnp.float32)
    first_kernel = noise(streams_of[5], (3, 3, C_IN, C_OUT), (9 * C_IN) ** -0.5, 0.1875)
    first_bias = noise(streams_of[6], (C_OUT,), 0.5, 3.0, (), jnp.float32)
    film_weight = noise(streams_of[7], (EMB, 2 * C_OUT), (4 * EMB) ** -0.5, 0.125)
    film_bias = noise(streams_of[8], (2 * C_OUT,), 0.3, 1.75, (), jnp.float32)
    middle_gain = jnp.clip(1.0 + 0.1 * jax.random.normal(streams_of[9], (C_OUT,), jnp.float32), 0.5, 1.5)
    middle_shift = noise(streams_of[10], (C_OUT,), 0.5, 3.0, (), jnp.float32)
    second_kernel = noise(streams_of[11], (3, 3, C_OUT, C_OUT), (9 * C_OUT) ** -0.5, 0.125)
    second_bias = noise(streams_of[12], (C_OUT,), 0.5, 3.0, (), jnp.float32)
    skip_weight = noise(streams_of[13], (C_IN, C_OUT), C_IN ** -0.5, 0.5)
    skip_bias = noise(streams_of[14], (C_OUT,), 0.5, 3.0, (), jnp.float32)
    features = noise(streams_of[15], (ITEMS, AH, AW, C_OUT), 1.0, 6.0, ((0, 4), (1, 4), (2, 2)))
    token_land = plant((jax.random.randint(streams_of[16], (ITEMS, AH, AW), 0, 5) < 3).astype(jnp.int32), jax.random.fold_in(streams_of[16], 1), 0, 1)
    attend_gain = jnp.clip(1.0 + 0.1 * jax.random.normal(streams_of[17], (C_OUT,), jnp.float32), 0.5, 1.5)
    attend_shift = noise(streams_of[18], (C_OUT,), 0.5, 3.0, (), jnp.float32)
    mixing_weight = noise(streams_of[19], (C_OUT, 3 * C_OUT), C_OUT ** -0.5, 0.375)
    mixing_bias = noise(streams_of[20], (2 * C_OUT,), 0.3, 1.75, (), jnp.float32)
    output_weight = noise(streams_of[21], (C_OUT, C_OUT), 1 ** -0.5, 6.0)
    output_bias = noise(streams_of[22], (C_OUT,), 0.3, 1.75, (), jnp.float32)
    grad_pooled = noise(streams_of[23], (ITEMS, H // 2, W // 2, C_OUT), 1.0, 6.0, ((0, 4), (1, 4), (2, 2)))
    grad_result = noise(streams_of[24], (ITEMS, AH, AW, C_OUT), 1.0, 6.0, ((0, 4), (1, 4), (2, 2)))
    return dict(image=image, land_mask=land_mask, embedding=embedding, input_gain=input_gain, input_shift=input_shift, first_kernel=first_kernel, first_bias=first_bias, film_weight=film_weight, film_bias=film_bias, middle_gain=middle_gain, middle_shift=middle_shift, second_kernel=second_kernel, second_bias=second_bias, skip_weight=skip_weight, skip_bias=skip_bias, features=features, token_land=token_land, attend_gain=attend_gain, attend_shift=attend_shift, mixing_weight=mixing_weight, mixing_bias=mixing_bias, output_weight=output_weight, output_bias=output_bias, grad_pooled=grad_pooled, grad_result=grad_result)


@jax.custom_vjp
def low(v):
    return lax.optimization_barrier(v.astype(jnp.bfloat16)).astype(jnp.float32)

@jax.custom_vjp
def low_back(v):
    return v

def low_keep(v):
    return (low(v), None)

def low_pass(kept, grad):
    return (grad,)

def back_keep(v):
    return (v, None)

def back_low(kept, grad):
    return (low(grad),)
low.defvjp(low_keep, low_pass)
low_back.defvjp(back_keep, back_low)

def group_norm(value, landf, gain, shift):
    width = value.shape[-1] // GROUPS
    grouped = value.reshape(value.shape[:-1] + (GROUPS, width))
    weight = landf[..., None, None]
    count = jnp.maximum(jnp.sum(landf), 1.0) * width
    axes = tuple(range(landf.ndim)) + (landf.ndim + 1,)
    mean = lax.optimization_barrier(jnp.sum(grouped * weight, axis=axes)) / count
    square = lax.optimization_barrier(jnp.sum(grouped * grouped * weight, axis=axes)) / count
    scale_inv = lax.rsqrt(square - mean * mean + 1e-05)
    normed = ((grouped - mean[:, None]) * scale_inv[:, None]).reshape(value.shape)
    return normed * gain + shift

def conv_same(value, kernel):
    return lax.conv_general_dilated(value[None], kernel, (1, 1), 'SAME', dimension_numbers=('NHWC', 'HWIO', 'NHWC'), precision=lax.Precision.HIGHEST)[0]

def item_forward(params, image, features, landf, embed, keyland):
    input_gain, input_shift, first_kernel, first_bias, film_weight, film_bias, middle_gain, middle_shift, second_kernel, second_bias, skip_weight, skip_bias, attend_gain, attend_shift, mixing_weight, mixing_bias, output_weight, output_bias = params
    high = lax.Precision.HIGHEST
    act_one = low(jax.nn.silu(group_norm(image, landf, input_gain, input_shift)))
    hidden = low_back(conv_same(act_one, first_kernel) + first_bias)
    channels = hidden.shape[-1]
    film = jnp.dot(embed, film_weight, precision=high) + film_bias
    modulated = group_norm(hidden, landf, middle_gain, middle_shift) * (1.0 + film[:channels]) + film[channels:]
    act_two = low(jax.nn.silu(modulated))
    branch = conv_same(act_two, second_kernel) + second_bias
    skipped = jnp.einsum('hwc,cd->hwd', image, skip_weight, precision=high) + skip_bias
    stream = low_back(branch + skipped) * math.sqrt(0.5)
    height, span = (stream.shape[0], stream.shape[1])
    pooled = stream.reshape(height // 2, 2, span // 2, 2, channels).mean(axis=(1, 3))
    attend_in = low(group_norm(features, keyland, attend_gain, attend_shift)).reshape(-1, channels)
    keyflat = keyland.reshape(-1)
    bias_full = jnp.concatenate([mixing_bias[:channels], jnp.zeros((channels,), mixing_bias.dtype), mixing_bias[channels:]])
    mixed = low(low_back(jnp.dot(attend_in, mixing_weight, precision=high) + bias_full))
    query = mixed[:, :channels]
    key_part = mixed[:, channels:2 * channels]
    value_part = mixed[:, 2 * channels:]
    scores = low_back(jnp.dot(query, key_part.T, precision=high) * channels ** (-0.5))
    scores = jnp.where(keyflat[None, :] > 0.5, scores, -1000000000.0)
    probs = low(jax.nn.softmax(scores, axis=-1))
    attended = low(low_back(jnp.dot(probs, value_part, precision=high)))
    update = jnp.dot(attended, output_weight, precision=high) + output_bias
    result = features + update.reshape(features.shape)
    update_square = jnp.sum(update * update * keyflat[:, None])
    sums = jnp.stack([jnp.sum(image * image * landf[..., None]), jnp.sum(branch * branch * landf[..., None]), jnp.sum(stream * stream * landf[..., None]), update_square, jnp.sum(result * result * keyland[..., None]), jnp.sum(landf), jnp.sum(keyland)])
    return ((pooled, result), sums)

def reference(image, land_mask, embedding, input_gain, input_shift, first_kernel, first_bias, film_weight, film_bias, middle_gain, middle_shift, second_kernel, second_bias, skip_weight, skip_bias, features, token_land, attend_gain, attend_shift, mixing_weight, mixing_bias, output_weight, output_bias, grad_pooled, grad_result):
    params = tuple((p.astype(jnp.float32) for p in (input_gain, input_shift, first_kernel, first_bias, film_weight, film_bias, middle_gain, middle_shift, second_kernel, second_bias, skip_weight, skip_bias, attend_gain, attend_shift, mixing_weight, mixing_bias, output_weight, output_bias)))

    def one_item(item):
        img, fts, lnd, emb, kland, gpool, gres = item

        def forward(params_in, img_in, fts_in):
            return item_forward(params_in, img_in, fts_in, lnd, emb, kland)
        outs, pull, sums = jax.vjp(forward, params, img, fts, has_aux=True)
        grads, dimg, dfts = pull((gpool, gres))
        return (outs, grads, dimg, dfts, sums)
    items = (image.astype(jnp.float32), features.astype(jnp.float32), land_mask.astype(jnp.float32), embedding.astype(jnp.float32), token_land.astype(jnp.float32), grad_pooled.astype(jnp.float32), grad_result.astype(jnp.float32))
    (pooled, result), grads, dimg, dfts, sums = lax.map(one_item, items)
    grads = tuple((lax.optimization_barrier(jnp.sum(g, axis=0)) for g in grads))
    totals = lax.optimization_barrier(jnp.sum(sums, axis=0))
    land_count = jnp.maximum(totals[5], 1.0)
    token_count = jnp.maximum(totals[6], 1.0)
    denom = jnp.stack([land_count * C_IN, land_count * C_OUT, land_count * C_OUT, token_count * C_OUT, token_count * C_OUT])
    rms_values = jnp.sqrt(totals[:5] / denom)
    return (pooled.astype(jnp.bfloat16), result.astype(jnp.bfloat16), dimg.astype(jnp.bfloat16), dfts.astype(jnp.bfloat16), grads[0], grads[1], grads[2], grads[3], grads[4], grads[5], grads[6], grads[7], grads[8], grads[9], grads[10], grads[11], grads[12], grads[13], grads[14], grads[15], grads[16], grads[17], rms_values)
```

```python
import functools
import math
from types import SimpleNamespace

import jax
import jax.numpy as jnp
from jax import lax
from jax.experimental import pallas as pl
from jax.experimental.pallas import tpu as pltpu
from jax.sharding import PartitionSpec as P

GROUPS = 32
EPS = 1e-05
MASKED = -1000000000.0
LOG2E = 1.4426950408889634
F32 = jnp.float32
BF16 = jnp.bfloat16
MESH = pl.DeviceIdType.MESH
HIGHEST = lax.Precision.HIGHEST


def mm(left, right):
    return jnp.dot(left, right, preferred_element_type=F32)


def mm_t(left, right):
    return lax.dot_general(left, right, (((1,), (1,)), ((), ())), preferred_element_type=F32)


def iota(shape, dim):
    return lax.broadcasted_iota(jnp.int32, shape, dim)


def fold(value):
    rows, width = value.shape
    return jnp.sum(value.reshape(rows // 8, 8, width), axis=0)


def total(value):
    return jnp.sum(value, axis=0, keepdims=True)


def group_total(rows, width):
    channels = rows.shape[-1]
    left = jnp.floor(iota((channels, channels), 0).astype(F32) * (1.0 / width))
    right = jnp.floor(iota((channels, channels), 1).astype(F32) * (1.0 / width))
    same = (left == right).astype(F32)
    padded = jnp.concatenate([rows, jnp.zeros((8 - rows.shape[0], channels), F32)], axis=0)
    return jnp.dot(padded, same, precision=HIGHEST, preferred_element_type=F32)


def sigmoid(value):
    return 0.5 * jnp.tanh(0.5 * value) + 0.5


INPUTS = (
    "image", "land", "embedding", "gain1", "shift1", "kernel1", "bias1", "film_w", "film_b",
    "gain2", "shift2", "kernel2", "bias2", "skip_w", "skip_b", "features", "token", "gain3",
    "shift3", "mix_w", "mix_b", "out_w", "out_b", "gpool", "gres",
)
RESULTS = ("pooled", "result", "image_grad", "features_grad", "sum_a", "sum_b", "sum_c", "vectors")


class Links:
    def __init__(self, ref, n_item, n_row):
        self.ref = ref
        self.n_item, self.n_row, self.n_group = n_item, n_row, n_row * 2
        self.item, self.row, self.pair = (lax.axis_index(a) for a in ("item", "row", "pair"))
        self.sibling = 1 - self.pair
        self.slot = self.row * 2 + self.pair
        self.sends = 0
        self.recvs = 0
        self.pending = []

    def new_send(self):
        self.sends += 1
        return self.sends - 1

    def new_recv(self, count=1):
        self.recvs += count
        return self.recvs - count

    def send(self, source, target, device, recv, when=None):
        index = self.new_send()

        def make():
            return pltpu.make_async_remote_copy(
                src_ref=source,
                dst_ref=target,
                send_sem=self.ref.send_sem.at[index],
                recv_sem=self.ref.recv_sem.at[recv],
                device_id=device,
                device_id_type=MESH,
            )

        if when is None:
            make().start()
        else:
            pl.when(when)(lambda: make().start())
        self.pending.append((make, when))

    def arrived(self, target, recv, when=None):
        def wait():
            pltpu.make_async_remote_copy(
                src_ref=target,
                dst_ref=target,
                send_sem=self.ref.send_sem.at[0],
                recv_sem=self.ref.recv_sem.at[recv],
                device_id=(self.item, self.row, self.sibling),
                device_id_type=MESH,
            ).wait_recv()

        if when is None:
            wait()
        else:
            pl.when(when)(wait)

    def finish(self):
        for make, when in self.pending:
            if when is None:
                make().wait_send()
            else:
                pl.when(when)(lambda make=make: make().wait_send())

    def barrier(self):
        sem = pltpu.get_barrier_semaphore()
        count = 0
        for step in range(1, self.n_group):
            other = lax.rem(self.slot + step, self.n_group)
            device = (self.item, lax.div(other, 2), lax.rem(other, 2))
            pl.semaphore_signal(sem, inc=1, device_id=device, device_id_type=MESH)
            count += 1
        for step in range(1, self.n_item):
            device = (lax.rem(self.item + step, self.n_item), self.row, self.pair)
            pl.semaphore_signal(sem, inc=1, device_id=device, device_id_type=MESH)
            count += 1
        pl.semaphore_wait(sem, count)

    def share(self, slots, source=None):
        base = self.new_recv(self.n_group)
        mine = slots.at[self.slot]
        for step in range(1, self.n_group):
            other = lax.rem(self.slot + step, self.n_group)
            device = (self.item, lax.div(other, 2), lax.rem(other, 2))
            self.send(mine if source is None else source, mine, device, base + self.slot)

        def wait():
            for step in range(1, self.n_group):
                other = lax.rem(self.slot + step, self.n_group)
                self.arrived(slots.at[other], base + other)

        return wait

    def edge_rows(self, first, last, above, below):
        has_above, has_below = self.row > 0, self.row < self.n_row - 1
        from_above, from_below = self.new_recv(), self.new_recv()
        self.send(first, below, (self.item, self.row - 1, self.pair), from_below, has_above)
        self.send(last, above, (self.item, self.row + 1, self.pair), from_above, has_below)

        def wait():
            self.arrived(above, from_above, has_above)
            self.arrived(below, from_below, has_below)

            @pl.when(self.row == 0)
            def _():
                above[...] = jnp.zeros(above.shape, above.dtype)

            @pl.when(self.row == self.n_row - 1)
            def _():
                below[...] = jnp.zeros(below.shape, below.dtype)

        return wait

    def edge_columns(self, column, columns):
        has_above, has_below = self.row > 0, self.row < self.n_row - 1
        base = self.new_recv(3)
        self.send(column, columns.at[1], (self.item, self.row, self.sibling), base + 1)
        self.send(column, columns.at[2], (self.item, self.row - 1, self.sibling), base + 2, has_above)
        self.send(column, columns.at[0], (self.item, self.row + 1, self.sibling), base, has_below)

        def wait():
            self.arrived(columns.at[1], base + 1)
            self.arrived(columns.at[0], base, has_above)
            self.arrived(columns.at[2], base + 2, has_below)

            @pl.when(self.row == 0)
            def _():
                columns[0] = jnp.zeros(columns.shape[1:], columns.dtype)

            @pl.when(self.row == self.n_row - 1)
            def _():
                columns[2] = jnp.zeros(columns.shape[1:], columns.dtype)

        return wait

    def all_sum(self, part, recv1, sum1, recv2, recv3, out):
        blocks = part.shape[0]
        half = blocks // 2
        quarter = half // self.n_item
        chunk = quarter // self.n_row
        item_at, row_at = self.item * quarter, self.row * chunk
        own = self.pair * half + item_at + row_at

        def span(ref, start, size):
            return ref.at[pl.ds(start, size)]

        def stage1():
            sem = self.new_recv()
            self.send(span(part, self.sibling * half, half), recv1, (self.item, self.row, self.sibling), sem)

            def stage2():
                self.arrived(recv1, sem)
                sum1[...] = (part[pl.ds(self.pair * half, half)].astype(F32) + recv1[...].astype(F32)).astype(BF16)
                base = self.new_recv(self.n_item - 1)
                for step in range(1, self.n_item):
                    other = lax.rem(self.item + step, self.n_item)
                    self.send(
                        span(sum1, other * quarter, quarter), recv2.at[step - 1],
                        (other, self.row, self.pair), base + step - 1,
                    )

                def stage3():
                    value = sum1[pl.ds(item_at, quarter)].astype(F32)
                    for step in range(1, self.n_item):
                        self.arrived(recv2.at[step - 1], base + step - 1)
                        value = value + recv2[step - 1].astype(F32)
                    sum1[pl.ds(item_at, quarter)] = value.astype(BF16)
                    base3 = self.new_recv(self.n_row - 1)
                    for step in range(1, self.n_row):
                        other = lax.rem(self.row + step, self.n_row)
                        self.send(
                            span(sum1, item_at + other * chunk, chunk), recv3.at[step - 1],
                            (self.item, other, self.pair), base3 + step - 1,
                        )

                    def stage4():
                        value = sum1[pl.ds(item_at + row_at, chunk)].astype(F32)
                        for step in range(1, self.n_row):
                            self.arrived(recv3.at[step - 1], base3 + step - 1)
                            value = value + recv3[step - 1].astype(F32)
                        out[pl.ds(own, chunk)] = value.astype(BF16)
                        base4 = self.new_recv(self.n_row)
                        for step in range(1, self.n_row):
                            other = lax.rem(self.row + step, self.n_row)
                            self.send(
                                span(out, own, chunk), span(out, own, chunk),
                                (self.item, other, self.pair), base4 + self.row,
                            )

                        def stage5():
                            for step in range(1, self.n_row):
                                other = lax.rem(self.row + step, self.n_row)
                                self.arrived(
                                    span(out, self.pair * half + item_at + other * chunk, chunk), base4 + other
                                )
                            base5 = self.new_recv(self.n_item)
                            mine = span(out, self.pair * half + item_at, quarter)
                            for step in range(1, self.n_item):
                                other = lax.rem(self.item + step, self.n_item)
                                self.send(mine, mine, (other, self.row, self.pair), base5 + self.item)

                            def stage6():
                                for step in range(1, self.n_item):
                                    other = lax.rem(self.item + step, self.n_item)
                                    self.arrived(
                                        span(out, self.pair * half + other * quarter, quarter), base5 + other
                                    )
                                sem6 = self.new_recv()
                                whole = span(out, self.pair * half, half)
                                self.send(whole, whole, (self.item, self.row, self.sibling), sem6)

                                def stage7():
                                    self.arrived(span(out, self.sibling * half, half), sem6)

                                return stage7

                            return stage6

                        return stage5

                    return stage4

                return stage3

            return stage2

        return stage1()


def norm_terms(sums, squares, count, width):
    size = jnp.maximum(count, 1.0) * width
    grouped = group_total(jnp.concatenate([sums, squares], axis=0), width)
    mean = grouped[0:1] / size
    return mean, lax.rsqrt(grouped[1:2] / size - mean * mean + EPS), size


def main_kernel(n_item, n_row, *refs):
    names = INPUTS + RESULTS + SCRATCH
    ref = SimpleNamespace(**dict(zip(names, refs)))
    link = Links(ref, n_item, n_row)
    height, span, c_in = ref.image.shape
    channels = ref.bias1.shape[-1]
    half = span // 2
    tokens = ref.features.shape[0]
    n_group = link.n_group
    low, high = height // 2, half
    side = link.pair.astype(F32)
    width1, width2 = c_in // GROUPS, channels // GROUPS
    slot = link.slot
    factor = channels ** (-0.5)

    link.barrier()

    wait_token = link.share(ref.flags, ref.token)
    wait_image_rows = link.edge_rows(ref.image.at[0], ref.image.at[height - 1], ref.image_up, ref.image_down)
    wait_pool_rows = link.edge_rows(ref.gpool.at[0], ref.gpool.at[low - 1], ref.pool_up, ref.pool_down)
    feature_sem = link.new_recv(n_group)
    link.send(ref.features, ref.raw.at[slot], (link.item, link.row, link.sibling), feature_sem + slot)
    for step in range(1, n_row):
        other = lax.rem(link.row + step, n_row)
        link.send(ref.features, ref.raw.at[slot], (link.item, other, link.pair), feature_sem + slot)
    ref.flags[slot] = ref.token[...]
    ref.raw[slot] = ref.features[...]

    ones = jnp.ones((span, 128), BF16)
    place = iota((span, span), 0)
    place = jnp.where(place < half, 2 * place, 2 * (place - half) + 1)
    spread = place == iota((span, span), 1)

    def land_row(y, carry):
        line = jnp.broadcast_to(ref.land[pl.ds(y, 1), :].astype(F32), (span, span))
        ref.mask[y] = mm(jnp.where(spread, line, 0.0).astype(BF16), ones)
        return carry

    lax.fori_loop(0, height, land_row, 0)

    rows_t, cols_t = ref.token.shape

    def token_mask(flags):
        pick = iota((rows_t, cols_t, rows_t), 0) == iota((rows_t, cols_t, rows_t), 2)
        lines = mm(pick.reshape(tokens, rows_t).astype(BF16), flags.astype(F32).astype(BF16))
        keep = (iota((rows_t, cols_t, cols_t), 1) == iota((rows_t, cols_t, cols_t), 2)).reshape(tokens, cols_t)
        return mm(jnp.where(keep, lines, 0.0).astype(BF16), jnp.ones((cols_t, 128), BF16))

    ref.token_mask[...] = token_mask(ref.token[...])

    def split_row(y, row):
        ref.line[...] = row.astype(F32)
        even = ref.line[pl.ds(0, half, stride=2), :]
        odd = ref.line[pl.ds(1, half, stride=2), :]
        ref.normed1[y, 0:half] = even
        ref.normed1[y, half:span] = odd
        return even, odd

    def image_row(y, carry):
        sums, squares, count = carry
        even, odd = split_row(y + 1, ref.image[y])
        value = jnp.concatenate([even, odd], axis=0)
        ref.image_low[y] = value.astype(BF16)
        ref.column1[pl.ds(y, 1), :] = jnp.where(side > 0.5, even[0:1], odd[half - 1 : half])
        mask = ref.mask[y]
        masked = value * mask
        return sums + fold(masked), squares + fold(masked * value), count + fold(mask)

    zero1 = jnp.zeros((8, c_in), F32)
    zero2 = jnp.zeros((8, channels), F32)
    sums1, squares1, count1 = lax.fori_loop(0, height, image_row, (zero1, zero1, jnp.zeros((8, 128), F32)))
    wait_image_columns = link.edge_columns(ref.column1, ref.columns1)
    raw = ref.features[...].astype(F32)
    tmask = ref.token_mask[...]
    tmask2 = jnp.concatenate([tmask] * (channels // 128), axis=1)
    masked = raw * tmask2
    ref.stats1[slot] = jnp.zeros((8, channels), F32)
    ref.stats1[slot, 0:1, 0:c_in] = total(sums1)
    ref.stats1[slot, 0:1, c_in:channels] = total(squares1)
    ref.stats1[slot, 1:2, :] = total(masked)
    ref.stats1[slot, 2:3, :] = total(masked * raw)
    ref.stats1[slot, 3:4, 0:128] = total(count1)
    ref.stats1[slot, 3:4, 128:256] = total(tmask)
    wait_stats1 = link.share(ref.stats1)

    for i in range(low):
        value = (ref.gpool[i].astype(F32) * 0.25 * math.sqrt(0.5)).astype(BF16)
        ref.gpre[i] = value
        ref.gpre_t[:, i * half : (i + 1) * half] = value.T
        wide = value.astype(F32)
        ref.column2[i : i + 1, :] = jnp.where(side > 0.5, wide[0:1], wide[half - 1 : half])
    wait_pool_columns = link.edge_columns(ref.column2, ref.columns2)
    gpre_sum = zero2
    for i in range(low):
        gpre_sum = gpre_sum + fold(ref.gpre[i].astype(F32))

    coarse = ref.probs if n_group >= 8 and tokens >= 2 * channels else ref.coarse

    upper, lower = {0: (2,), 1: (1, 2)}, {0: (0, 1), 1: (0,)}
    for u in range(2):
        for line, row_taps in enumerate((upper[u], lower[u])):
            tall = []
            for b in range(3):
                tile = sum(ref.kernel2[a, b * channels : (b + 1) * channels, :].astype(F32) for a in row_taps)
                tall.append(tile)
            for v in range(2):
                for place_x, column_taps in enumerate((upper[v], lower[v])):
                    tile = sum(tall[b] for b in column_taps)
                    coarse[u * 4 + v * 2 + line, 0:channels, place_x * channels : (place_x + 1) * channels] = tile.astype(BF16)

    wait_pool_rows()
    wait_pool_columns()
    first_row = iota((half, channels), 0) == 0
    last_row = iota((half, channels), 0) == half - 1
    for i in range(low + 2):
        if i == 0:
            value, edge = ref.pool_up[...], ref.columns2[0, low - 1 : low, :]
        elif i == low + 1:
            value, edge = ref.pool_down[...], ref.columns2[2, 0:1, :]
        else:
            value, edge = ref.gpre[i - 1], ref.columns2[1, i - 1 : i, :]
        if i in (0, low + 1):
            value = (value.astype(F32) * 0.25 * math.sqrt(0.5)).astype(BF16)
        wide = value.astype(F32)
        left = jnp.where(first_row, edge * side, pltpu.roll(wide, 1, 0))
        right = jnp.where(last_row, edge * (1.0 - side), pltpu.roll(wide, half - 1, 0))
        ref.padded_g[i, :, 0:channels] = left.astype(BF16)
        ref.padded_g[i, :, channels : 2 * channels] = value
        ref.padded_g[i, :, 2 * channels : 3 * channels] = right.astype(BF16)
    for u in range(2):
        for v in range(2):
            value = 0.0
            for line in range(2):
                rows = ref.padded_g[u + line : u + line + low, :, v * channels : (v + 2) * channels]
                value = value + mm_t(rows.reshape(low * half, 2 * channels), coarse[u * 4 + v * 2 + line, 0:channels, 0 : 2 * channels])
            for i in range(low):
                ref.grad2[2 * i + u, v * half : (v + 1) * half, :] = value[i * half : (i + 1) * half]

    wait_image_rows()
    wait_image_columns()
    wait_stats1()
    stats = ref.stats1[0]
    for other in range(1, n_group):
        stats = stats + ref.stats1[other]
    count_land = jnp.concatenate([stats[3:4, 0:128]] * (channels // 128), axis=1)
    count_token = jnp.concatenate([stats[3:4, 128:256]] * (channels // 128), axis=1)
    mean1, inv1, size1 = norm_terms(stats[0:1, 0:c_in], stats[0:1, c_in:channels], count_land[:, 0:c_in], width1)
    mean3, inv3, size3 = norm_terms(stats[1:2], stats[2:3], count_token, width2)
    split_row(0, ref.image_up[...])
    split_row(height + 1, ref.image_down[...])
    gain1, shift1 = ref.gain1[...], ref.shift1[...]

    def write_shifted(target, y, even, odd, edge, size):
        top = iota((half, size), 0) == 0
        end = iota((half, size), 0) == half - 1
        before = jnp.where(top, edge * side, pltpu.roll(odd, 1, 0)).astype(BF16)
        after = jnp.where(end, edge * (1.0 - side), pltpu.roll(even, half - 1, 0)).astype(BF16)
        even, odd = even.astype(BF16), odd.astype(BF16)
        target[y, 0:half, 0:size] = before
        target[y, 0:half, size : 2 * size] = even
        target[y, 0:half, 2 * size : 3 * size] = odd
        target[y, half:span, 0:size] = even
        target[y, half:span, size : 2 * size] = odd
        target[y, half:span, 2 * size : 3 * size] = after

    def act1(value):
        normed = (value - mean1) * inv1
        affine = normed * gain1 + shift1
        gate = sigmoid(affine)
        return normed, affine, gate

    def edge_act(rows):
        _, affine, gate = act1(rows)
        return affine * gate

    has_up = (link.row > 0).astype(F32)
    has_down = (link.row < n_row - 1).astype(F32)
    ref.columns1[0] = edge_act(ref.columns1[0]) * has_up
    ref.columns1[1] = edge_act(ref.columns1[1])
    ref.columns1[2] = edge_act(ref.columns1[2]) * has_down

    def act1_edge_row(y, edge, exists):
        _, affine, gate = act1(ref.normed1[y])
        act = affine * gate * exists
        write_shifted(ref.padded1, y, act[0:half], act[half:span], edge, c_in)

    act1_edge_row(0, ref.columns1[0, height - 1 : height, :], has_up)
    act1_edge_row(height + 1, ref.columns1[2, 0:1, :], has_down)

    def act1_row(y, carry):
        normed, affine, gate = act1(ref.normed1[y + 1])
        act = affine * gate
        ref.normed1[y + 1] = normed
        ref.slope1[y] = gate * (1.0 + affine * (1.0 - gate))
        write_shifted(ref.padded1, y + 1, act[0:half], act[half:span], ref.columns1[1, pl.ds(y, 1), :], c_in)
        return carry

    lax.fori_loop(0, height, act1_row, 0)

    def wide_mask(y):
        mask = ref.mask[y]
        return jnp.concatenate([mask] * (channels // 128), axis=1)

    def conv1_row(y, carry):
        sums, squares = carry
        value = mm(ref.padded1[y], ref.kernel1[0])
        value = value + mm(ref.padded1[y + 1], ref.kernel1[1])
        value = value + mm(ref.padded1[y + 2], ref.kernel1[2])
        value = value + ref.bias1[...]
        ref.hidden[y] = value
        masked = value * wide_mask(y)
        return sums + fold(masked), squares + fold(masked * value)

    sums2, squares2 = lax.fori_loop(0, height, conv1_row, (zero2, zero2))
    ref.stats2[slot] = jnp.zeros((8, channels), F32)
    ref.stats2[slot, 0:1, :] = total(sums2)
    ref.stats2[slot, 1:2, :] = total(squares2)
    wait_stats2 = link.share(ref.stats2)

    gain3, shift3 = ref.gain3[...], ref.shift3[...]
    scale3 = inv3 * gain3

    def normalize(index):
        value = ((ref.raw[index].astype(F32) - mean3) * scale3 + shift3).astype(BF16)
        ref.tokens[index] = value
        ref.tokens_t[index] = value.T

    normalize(slot)
    mine = ref.tokens[slot]
    w_query = ref.mix_w[:, 0:channels]
    w_key = ref.mix_w[:, channels : 2 * channels]
    w_value = ref.mix_w[:, 2 * channels : 3 * channels]
    ref.query[...] = (mm(mine, w_query) + ref.mix_b[:, 0:channels]).astype(BF16)
    ref.query_t[...] = (mm_t(w_key, ref.query[...]) * (factor * LOG2E)).astype(BF16)
    alive = (count_token > 0.0).astype(F32) * factor
    ref.query_k[...] = (mm_t(ref.query[...], w_key) * alive).astype(BF16)
    ref.grad_att[...] = mm_t(ref.gres[...], ref.out_w[...]).astype(BF16)
    ref.grad_t[...] = mm_t(w_value, ref.grad_att[...])

    lines = jnp.broadcast_to(ref.embedding[...], (8, ref.embedding.shape[-1]))
    film = mm(lines, ref.film_w[...])[0:1] + ref.film_b[...]
    film_scale = 1.0 + film[:, 0:channels]
    film_shift = film[:, channels:]

    wait_stats2()
    stats = ref.stats2[0]
    for other in range(1, n_group):
        stats = stats + ref.stats2[other]
    mean2, inv2, size2 = norm_terms(stats[0:1], stats[1:2], count_land, width2)
    slope_m = ref.gain2[...] * film_scale
    shift_m = ref.shift2[...] * film_scale + film_shift

    def mid_row(y, carry):
        grad_sum, grad_dot = carry
        normed = (ref.hidden[y] - mean2) * inv2
        affine = normed * slope_m + shift_m
        gate = sigmoid(affine)
        act = affine * gate
        grad = ref.grad2[y] * (gate * (1.0 + affine * (1.0 - gate)))
        ref.hidden[y] = normed
        ref.grad2[y] = grad
        ref.act2[y] = act.astype(BF16)
        edge = jnp.where(side > 0.5, act[0:1], act[span - 1 : span])
        ref.column3[pl.ds(y, 1), :] = edge
        return grad_sum + fold(grad), grad_dot + fold(grad * normed)

    grad_sum2, grad_dot2 = lax.fori_loop(0, height, mid_row, (zero2, zero2))
    ref.stats3[slot] = jnp.zeros((8, channels), F32)
    ref.stats3[slot, 0:1, :] = total(grad_sum2)
    ref.stats3[slot, 1:2, :] = total(grad_dot2)
    wait_stats3 = link.share(ref.stats3)
    wait_act_rows = link.edge_rows(ref.act2.at[0], ref.act2.at[height - 1], ref.act_up, ref.act_down)
    wait_act_columns = link.edge_columns(ref.column3, ref.columns3)

    for a in range(3):
        for b in range(3):
            ref.kernel1_t[2 - a, :, (2 - b) * channels : (3 - b) * channels] = ref.kernel1[
                a, b * c_in : (b + 1) * c_in, :
            ]

    wait_stats3()
    stats = ref.stats3[0]
    for other in range(1, n_group):
        stats = stats + ref.stats3[other]
    grad_sum2, grad_dot2 = stats[0:1], stats[1:2]
    grouped = group_total(jnp.concatenate([grad_sum2 * slope_m, grad_dot2 * slope_m], axis=0), width2)
    first2, second2 = grouped[0:1] / size2, grouped[1:2] / size2

    def hidden_row(y, carry):
        normed = ref.hidden[y]
        grad = ref.grad2[y] * slope_m - wide_mask(y) * (first2 + normed * second2)
        grad = (grad * inv2).astype(BF16)
        ref.grad_hidden[y] = grad
        ref.grad_hidden_t[y] = grad.T
        wide = grad.astype(F32)
        ref.column4[pl.ds(y, 1), :] = jnp.where(side > 0.5, wide[0:1], wide[span - 1 : span])
        return carry + fold(wide)

    bias1_sum = lax.fori_loop(0, height, hidden_row, zero2)
    wait_hidden_rows = link.edge_rows(
        ref.grad_hidden.at[0], ref.grad_hidden.at[height - 1], ref.hidden_up, ref.hidden_down
    )
    wait_hidden_columns = link.edge_columns(ref.column4, ref.columns4)

    def pad_rows(target, source, up, down, columns):
        def edge_row(y, row, edge):
            row = row.astype(F32)
            write_shifted(target, y, row[0:half], row[half:span], edge, channels)

        edge_row(0, up[...], columns[0, height - 1 : height, :])
        edge_row(height + 1, down[...], columns[2, 0:1, :])

        def body(y, carry):
            edge_row(y + 1, source[y], columns[1, pl.ds(y, 1), :])
            return carry

        lax.fori_loop(0, height, body, 0)

    wait_act_rows()
    wait_act_columns()
    pad_rows(ref.padded2, ref.act2, ref.act_up, ref.act_down, ref.columns3)

    def box_row(i, carry):
        for a in range(3):
            value = 0.0
            for dy in range(2):
                for side_x in range(2):
                    row = ref.padded2[2 * i + a + dy, side_x * half : (side_x + 1) * half, :]
                    value = value + row.astype(F32)
            ref.boxes[a, i] = value.astype(BF16)
        value = 0.0
        for dy in range(2):
            for side_x in range(2):
                value = value + ref.image_low[2 * i + dy, side_x * half : (side_x + 1) * half, :].astype(F32)
        ref.image_box[i] = value.astype(BF16)
        return carry

    lax.fori_loop(0, low, box_row, 0)

    def kernel2_grad(a, carry):
        value = mm(ref.gpre_t[...], ref.boxes[a].reshape(low * half, 3 * channels)).T
        rows = 3 * channels // 16
        for lane in range(channels // 128):
            piece = value[:, lane * 128 : (lane + 1) * 128].astype(BF16).reshape(rows, 16, 128)
            ref.part_a[pl.ds(lane * 3 * rows + a * rows, rows)] = piece
        return carry

    lax.fori_loop(0, 3, kernel2_grad, 0)
    next_a = link.all_sum(ref.part_a, ref.recv1_a, ref.sum1_a, ref.recv2_a, ref.recv3_a, ref.sum_a)

    rows_c = 10 * c_in // 16

    def kernel1_grad(a, carry):
        value = 0.0
        for y in range(height):
            value = value + mm(ref.grad_hidden_t[y], ref.padded1[a + y])
        value = value.T
        rows = 3 * c_in // 16
        for lane in range(channels // 128):
            piece = value[:, lane * 128 : (lane + 1) * 128].astype(BF16).reshape(rows, 16, 128)
            ref.part_c[pl.ds(lane * rows_c + a * rows, rows)] = piece
        return carry

    lax.fori_loop(0, 3, kernel1_grad, 0)
    value = mm(ref.gpre_t[...], ref.image_box[...].reshape(low * half, c_in)).T
    for lane in range(channels // 128):
        piece = value[:, lane * 128 : (lane + 1) * 128].astype(BF16).reshape(c_in // 16, 16, 128)
        ref.part_c[pl.ds(lane * rows_c + 9 * c_in // 16, c_in // 16)] = piece
    next_c = link.all_sum(ref.part_c, ref.recv1_c, ref.sum1_c, ref.recv2_c, ref.recv3_c, ref.sum_c)

    def conv2_rows(i, carry):
        branch_sum, stream_sum = carry
        pooled = 0.0
        for u in range(2):
            y = 2 * i + u
            branch = mm(ref.padded2[y], ref.kernel2[0])
            branch = branch + mm(ref.padded2[y + 1], ref.kernel2[1])
            branch = branch + mm(ref.padded2[y + 2], ref.kernel2[2])
            branch = branch + ref.bias2[...]
            stream = (branch + mm(ref.image_low[y], ref.skip_w[...]) + ref.skip_b[...]) * math.sqrt(0.5)
            mask = wide_mask(y)
            branch_sum = branch_sum + fold(branch * branch * mask)
            stream_sum = stream_sum + fold(stream * stream * mask)
            pooled = pooled + stream[0:half] + stream[half:span]
        ref.pooled[i] = (pooled * 0.25).astype(BF16)
        return branch_sum, stream_sum

    branch_sum, stream_sum = lax.fori_loop(0, low, conv2_rows, (zero2, zero2))

    wait_hidden_rows()
    wait_hidden_columns()
    pad_rows(ref.padded2, ref.grad_hidden, ref.hidden_up, ref.hidden_down, ref.columns4)

    def back1_row(y, carry):
        grad_sum, grad_dot = carry
        value = mm_t(ref.padded2[y], ref.kernel1_t[0])
        value = value + mm_t(ref.padded2[y + 1], ref.kernel1_t[1])
        value = value + mm_t(ref.padded2[y + 2], ref.kernel1_t[2])
        value = value * ref.slope1[y]
        ref.slope1[y] = value
        return grad_sum + fold(value), grad_dot + fold(value * ref.normed1[y + 1])

    grad_sum1, grad_dot1 = lax.fori_loop(0, height, back1_row, (zero1, zero1))
    ref.stats4[slot] = jnp.zeros((8, channels), F32)
    ref.stats4[slot, 0:1, 0:c_in] = total(grad_sum1)
    ref.stats4[slot, 0:1, c_in:channels] = total(grad_dot1)
    wait_stats4 = link.share(ref.stats4)
    next_a = next_a()
    next_c = next_c()

    for step in range(1, n_row):
        other = lax.rem(link.row + step, n_row) * 2 + link.pair
        link.arrived(ref.raw.at[other], feature_sem + other)
        link.send(ref.raw.at[other], ref.raw.at[other], (link.item, link.row, link.sibling), feature_sem + other)
    wait_token()

    next_a = next_a()
    next_c = next_c()

    wait_stats4()
    stats = ref.stats4[0]
    for other in range(1, n_group):
        stats = stats + ref.stats4[other]
    grad_sum1, grad_dot1 = stats[0:1, 0:c_in], stats[0:1, c_in:channels]
    grouped = group_total(jnp.concatenate([grad_sum1 * gain1, grad_dot1 * gain1], axis=0), width1)
    first1, second1 = grouped[0:1] / size1, grouped[1:2] / size1

    def image_grad_rows(i, carry):
        skip = mm_t(ref.gpre[i], ref.skip_w[...])
        skip = jnp.concatenate([skip, skip], axis=0)
        for u in range(2):
            y = 2 * i + u
            value = ref.slope1[y] * gain1 - ref.mask[y] * (first1 + ref.normed1[y + 1] * second1)
            value = value * inv1 + skip
            ref.line[pl.ds(0, half, stride=2), :] = value[0:half]
            ref.line[pl.ds(1, half, stride=2), :] = value[half:span]
            ref.image_grad[y] = ref.line[...].astype(BF16)
        return carry

    lax.fori_loop(0, low, image_grad_rows, 0)
    next_a = next_a()
    next_c = next_c()

    for step in range(n_row):
        other = lax.rem(link.row + step, n_row) * 2 + link.sibling
        link.arrived(ref.raw.at[other], feature_sem + other)

    def score_block(index, carry):
        normalize(index)
        mask = token_mask(ref.flags[index])
        mask = jnp.concatenate([mask] * (tokens // 128), axis=1) if tokens > 128 else mask[:, 0:tokens]
        scores = mm(ref.tokens[index], ref.query_t[...])
        scores = jnp.where(mask > 0.5, scores, MASKED * LOG2E)
        ref.scores[index] = scores
        return jnp.maximum(carry, jnp.max(scores.reshape(tokens // 8, 8, tokens), axis=0))

    top = lax.fori_loop(0, n_group, score_block, jnp.full((8, tokens), -3e38, F32))
    top = jnp.max(top, axis=0, keepdims=True)
    ref.mixed_t[...] = jnp.zeros((channels, tokens), F32)

    def probs_block(index, carry):
        probs = jnp.exp2(ref.scores[index] - top)
        low_probs = probs.astype(BF16)
        ref.probs[index] = low_probs
        ref.mixed_t[...] += mm(ref.tokens_t[index], low_probs)
        return carry + fold(probs)

    norm = lax.fori_loop(0, n_group, probs_block, jnp.zeros((8, tokens), F32))
    norm = 1.0 / total(norm)
    next_a = next_a()
    next_c = next_c()
    mixed_t = ref.mixed_t[...] * norm
    ref.mixed_t[...] = mixed_t
    attended = (mm(mixed_t.T.astype(BF16), w_value) + ref.mix_b[:, channels:]).astype(BF16)
    update = mm(attended, ref.out_w[...]) + ref.out_b[...]
    result = ref.features[...].astype(F32) + update
    ref.result[...] = result.astype(BF16)
    tmask2 = jnp.concatenate([ref.token_mask[...]] * (channels // 128), axis=1)
    update_sum = fold(update * update * tmask2)
    result_sum = fold(result * result * tmask2)

    def part_b(lane, value):
        for tile in range(channels // 128):
            piece = value[:, tile * 128 : (tile + 1) * 128].astype(BF16)
            ref.part_b[pl.ds((lane + tile) * (channels // 16), channels // 16)] = piece.reshape(channels // 16, 16, 128)

    part_b(6, mm(attended.T, ref.gres[...]))
    part_b(4, mm(mixed_t.astype(BF16), ref.grad_att[...]))

    grad_t = (ref.grad_t[...] * norm).astype(BF16)
    delta = total(grad_t.astype(F32) * mixed_t)
    ref.grad_low_t[...] = grad_t
    ref.grad_low[...] = grad_t.T
    ref.grad_query_t[...] = jnp.zeros((channels, tokens), F32)

    def back_block(index, carry):
        grad_sum, grad_dot = carry
        probs = ref.probs[index]
        grad = mm(ref.tokens[index], ref.grad_low_t[...])
        grad = (probs.astype(F32) * (grad - delta)).astype(BF16)
        value = mm(grad, ref.query_k[...]) + mm(probs, ref.grad_low[...])
        ref.grad_tokens[index] = value.astype(BF16)
        ref.grad_query_t[...] += mm(ref.tokens_t[index], grad)
        return grad_sum + fold(value), grad_dot + fold(value * ref.raw[index].astype(F32))

    grad_sum3, grad_dot3 = zero2, zero2
    pair_sem = link.new_recv(n_row)
    order = [lax.rem(link.row + step, n_row) for step in range(1, n_row)] + [link.row]
    for step, other in enumerate(order):
        grad_sum3, grad_dot3 = back_block(other * 2 + link.sibling, (grad_sum3, grad_dot3))
        link.send(
            ref.grad_tokens.at[other * 2 + link.sibling], ref.pair_grad.at[step],
            (link.item, link.row, link.sibling), pair_sem + step,
        )
        grad_sum3, grad_dot3 = back_block(other * 2 + link.pair, (grad_sum3, grad_dot3))
    row_sem = link.new_recv(n_row)
    for step, other in enumerate(order[:-1]):
        link.arrived(ref.pair_grad.at[step], pair_sem + step)
        value = ref.pair_grad[step].astype(F32) + ref.grad_tokens[other * 2 + link.pair].astype(F32)
        ref.chip_grad[step] = value.astype(BF16)
        link.send(ref.chip_grad.at[step], ref.row_grad.at[step], (link.item, other, link.pair), row_sem + step)

    grad_query_t = (ref.grad_query_t[...] * alive[0:1, 0:1]).astype(BF16)
    grad_query = mm(grad_query_t.T, w_key).astype(BF16)
    part_b(0, mm(ref.tokens_t[slot], grad_query))
    part_b(2, mm(grad_query_t, ref.query[...]))
    next_b = link.all_sum(ref.part_b, ref.recv1_b, ref.sum1_b, ref.recv2_b, ref.recv3_b, ref.sum_b)
    own_grad = mm_t(grad_query, w_query)
    raw = ref.features[...].astype(F32)
    grad_sum3 = total(grad_sum3 + fold(own_grad))
    grad_dot3 = total(grad_dot3 + fold(own_grad * raw))
    ref.stats5[slot] = jnp.zeros((16, channels), F32)
    for index, value in enumerate((
        grad_sum3,
        (grad_dot3 - mean3 * grad_sum3) * inv3,
        total(bias1_sum),
        4.0 * total(gpre_sum),
        total(fold(ref.gres[...].astype(F32))),
        total(fold(grad_query.astype(F32))),
        total(fold(ref.grad_att[...].astype(F32))),
        total(branch_sum),
        total(stream_sum),
        total(update_sum),
        total(result_sum),
    )):
        ref.stats5[slot, index : index + 1, :] = value
    wait_stats5 = link.share(ref.stats5)
    next_a = next_a()
    next_c = next_c()
    next_b = next_b()

    last = n_row - 1
    link.arrived(ref.pair_grad.at[last], pair_sem + last)
    own_grad = own_grad + ref.pair_grad[last].astype(F32) + ref.grad_tokens[slot].astype(F32)
    wait_stats5()
    stats = ref.stats5[0]
    for other in range(1, n_group):
        stats = stats + ref.stats5[other]
    item = link.item
    ref.vectors[item, 0:16, :] = stats
    ref.vectors[item, 16:24, :] = jnp.zeros((8, channels), F32)
    ref.vectors[item, 11:12, 0:c_in] = grad_dot1
    ref.vectors[item, 11:12, c_in:channels] = grad_sum1
    ref.vectors[item, 12:13, :] = grad_dot2 * film_scale
    ref.vectors[item, 13:14, :] = grad_sum2 * film_scale
    ref.vectors[item, 14:15, :] = grad_dot2 * ref.gain2[...] + grad_sum2 * ref.shift2[...]
    ref.vectors[item, 15:16, :] = grad_sum2
    ref.vectors[item, 16:17, :] = ref.embedding[:, 0:channels].astype(F32)
    ref.vectors[item, 17:18, :] = ref.embedding[:, channels : 2 * channels].astype(F32)
    stats1 = ref.stats1[0]
    for other in range(1, n_group):
        stats1 = stats1 + ref.stats1[other]
    ref.vectors[item, 18:19, 0:c_in] = stats1[0:1, c_in:channels]
    ref.vectors[item, 19:20, :] = stats1[3:4]
    item_sem = link.new_recv(n_item)
    for step in range(1, n_item):
        other = lax.rem(item + step, n_item)
        link.send(ref.vectors.at[item], ref.vectors.at[item], (other, link.row, link.pair), item_sem + item)

    grouped = group_total(jnp.concatenate([stats[0:1] * gain3, stats[1:2] * gain3], axis=0), width2)
    first3, second3 = grouped[0:1] / size3, grouped[1:2] / size3
    for step in range(n_row - 1):
        link.arrived(ref.row_grad.at[step], row_sem + step)
        own_grad = own_grad + ref.row_grad[step].astype(F32)
    normed = (raw - mean3) * inv3
    value = (own_grad * gain3 - tmask2 * (first3 + normed * second3)) * inv3
    ref.features_grad[...] = (ref.gres[...].astype(F32) + value).astype(BF16)
    next_a = next_a()
    next_c = next_c()
    for _ in range(5):
        next_b = next_b()
    for step in range(1, n_item):
        other = lax.rem(item + step, n_item)
        link.arrived(ref.vectors.at[other], item_sem + other)
    link.finish()
    assert link.sends <= ref.send_sem.shape[0] and link.recvs <= ref.recv_sem.shape[0]


SCRATCH = (
    "send_sem", "recv_sem", "flags", "raw", "image_up", "image_down", "pool_up", "pool_down", "mask",
    "token_mask", "line", "normed1", "image_low", "column1", "columns1", "stats1", "gpre", "gpre_t",
    "column2", "columns2", "coarse", "padded_g", "grad2", "slope1", "padded1", "hidden", "stats2",
    "tokens", "tokens_t", "query", "query_t", "query_k", "grad_att", "grad_t", "act2", "column3",
    "columns3", "stats3", "act_up", "act_down", "kernel1_t", "grad_hidden", "grad_hidden_t", "column4",
    "columns4", "hidden_up", "hidden_down", "padded2", "boxes", "image_box", "part_a", "recv1_a",
    "sum1_a", "recv2_a", "recv3_a", "part_b", "recv1_b", "sum1_b", "recv2_b", "recv3_b", "part_c",
    "recv1_c", "sum1_c", "recv2_c", "recv3_c", "stats4", "scores", "probs", "mixed_t",
    "grad_low_t", "grad_low", "grad_query_t", "grad_tokens", "pair_grad", "chip_grad", "row_grad", "stats5",
)


def last_kernel(n_item, *refs):
    (pooled, result, image_grad, features_grad, sum_a, sum_b, sum_c, vectors) = refs[:8]
    (o_pooled, o_result, o_image, o_features, o_gain1, o_shift1, o_kernel1, o_bias1, o_film_w, o_film_b,
     o_gain2, o_shift2, o_kernel2, o_bias2, o_skip_w, o_skip_b, o_gain3, o_shift3, o_mix_w, o_mix_b,
     o_out_w, o_out_b, o_rms) = refs[8:]
    o_pooled[...] = pooled[...]
    o_result[...] = result[...]
    o_image[...] = image_grad[...]
    o_features[...] = features_grad[...]
    channels = o_bias1.shape[-1]
    c_in = o_gain1.shape[-1]

    def blocks(ref, start, count):
        return ref[start : start + count].reshape(count * 16, 128).astype(F32)

    lanes = channels // 128
    n_a, n_c, n_k = 9 * channels // 16, 10 * c_in // 16, 9 * c_in // 16
    for lane in range(lanes):
        at = slice(lane * 128, (lane + 1) * 128)
        o_kernel2[:, at] = blocks(sum_a, lane * n_a, n_a)
        o_kernel1[:, at] = blocks(sum_c, lane * n_c, n_k)
        o_skip_w[:, at] = blocks(sum_c, lane * n_c + n_k, n_c - n_k)
    n_b = channels // 16
    for lane in range(3 * lanes):
        o_mix_w[:, lane * 128 : (lane + 1) * 128] = blocks(sum_b, lane * n_b, n_b)
    for lane in range(lanes):
        o_out_w[:, lane * 128 : (lane + 1) * 128] = blocks(sum_b, (3 * lanes + lane) * n_b, n_b)
    value = vectors[0]
    for item in range(1, n_item):
        value = value + vectors[item]
    o_shift3[...] = value[0:1]
    o_gain3[...] = value[1:2]
    o_bias1[...] = value[2:3]
    o_bias2[...] = value[3:4]
    o_skip_b[...] = value[3:4]
    o_out_b[...] = value[4:5]
    o_mix_b[:, 0:channels] = value[5:6]
    o_mix_b[:, channels:] = value[6:7]
    o_gain1[...] = value[11:12, 0:c_in]
    o_shift1[...] = value[11:12, c_in:channels]
    o_gain2[...] = value[12:13]
    o_shift2[...] = value[13:14]
    o_film_b[:, 0:channels] = value[14:15]
    o_film_b[:, channels:] = value[15:16]
    pad = jnp.zeros((8 - n_item, 2 * channels), F32)
    embedding = jnp.concatenate(
        [jnp.concatenate([vectors[i, 16:17, :], vectors[i, 17:18, :]], axis=1) for i in range(n_item)] + [pad], axis=0
    )
    grads = jnp.concatenate(
        [jnp.concatenate([vectors[i, 14:15, :], vectors[i, 15:16, :]], axis=1) for i in range(n_item)] + [pad], axis=0
    )
    o_film_w[...] = lax.dot_general(
        embedding, grads, (((0,), (0,)), ((), ())), precision=HIGHEST, preferred_element_type=F32
    )

    def lane_sum(row):
        return jnp.sum(row, axis=1, keepdims=True)

    land = jnp.maximum(value[19:20, 0:1], 1.0)
    token = jnp.maximum(value[19:20, 128:129], 1.0)
    place = iota((1, 5), 1)
    rms = jnp.zeros((1, 5), F32)
    for index, (square, count) in enumerate((
        (lane_sum(value[18:19, 0:c_in]), land * c_in),
        (lane_sum(value[7:8]), land * channels),
        (lane_sum(value[8:9]), land * channels),
        (lane_sum(value[9:10]), token * channels),
        (lane_sum(value[10:11]), token * channels),
    )):
        rms = jnp.where(place == index, jnp.sqrt(square / count), rms)
    o_rms[...] = rms


def on_device(mesh_shape, *args):
    names = INPUTS
    arg = SimpleNamespace(**dict(zip(names, args)))
    n_item, n_row = mesh_shape["item"], mesh_shape["row"]
    n_group = 2 * n_row
    _, height, span, c_in = arg.image.shape
    channels = arg.bias1.shape[-1]
    _, rows_t, cols_t, _ = arg.features.shape
    tokens = rows_t * cols_t
    low, half = height // 2, span // 2
    inputs = [
        arg.image.reshape(height, span, c_in),
        arg.land_mask.reshape(height, span) if hasattr(arg, "land_mask") else arg.land.reshape(height, span),
        arg.embedding,
        arg.gain1.reshape(1, c_in),
        arg.shift1.reshape(1, c_in),
        arg.kernel1.reshape(3, 3 * c_in, channels),
        arg.bias1.reshape(1, channels),
        arg.film_w,
        arg.film_b.reshape(1, 2 * channels),
        arg.gain2.reshape(1, channels),
        arg.shift2.reshape(1, channels),
        arg.kernel2.reshape(3, 3 * channels, channels),
        arg.bias2.reshape(1, channels),
        arg.skip_w,
        arg.skip_b.reshape(1, channels),
        arg.features.reshape(tokens, channels),
        arg.token.reshape(rows_t, cols_t),
        arg.gain3.reshape(1, channels),
        arg.shift3.reshape(1, channels),
        arg.mix_w,
        arg.mix_b.reshape(1, 2 * channels),
        arg.out_w,
        arg.out_b.reshape(1, channels),
        arg.gpool.reshape(low, half, channels),
        arg.gres.reshape(tokens, channels),
    ]
    share = 2 * n_item * n_row
    blocks_a = -(-9 * channels * channels // 2048 // share) * share
    blocks_b = -(-4 * channels * channels // 2048 // share) * share
    blocks_c = -(-10 * c_in * channels // 2048 // share) * share
    vmem = pltpu.VMEM

    def sums(blocks):
        unit = blocks // 2 // n_item
        return [
            vmem((blocks, 16, 128), BF16),
            vmem((blocks // 2, 16, 128), BF16),
            vmem((blocks // 2, 16, 128), BF16),
            vmem((n_item - 1, unit, 16, 128), BF16),
            vmem((n_row - 1, unit // n_row, 16, 128), BF16),
        ]

    scratch = [
        pltpu.SemaphoreType.DMA((100 + 12 * n_group,)),
        pltpu.SemaphoreType.DMA((100 + 12 * n_group,)),
        vmem((n_group, rows_t, cols_t), jnp.int32),
        vmem((n_group, tokens, channels), BF16),
        vmem((span, c_in), BF16),
        vmem((span, c_in), BF16),
        vmem((half, channels), BF16),
        vmem((half, channels), BF16),
        vmem((height, span, 128), F32),
        vmem((tokens, 128), F32),
        vmem((span, c_in), F32),
        vmem((height + 2, span, c_in), F32),
        vmem((height, span, c_in), BF16),
        vmem((8, c_in), F32),
        vmem((3, 8, c_in), F32),
        vmem((n_group, 8, channels), F32),
        vmem((low, half, channels), BF16),
        vmem((channels, low * half), BF16),
        vmem((8, channels), F32),
        vmem((3, 8, channels), F32),
        vmem((8, channels, 2 * channels) if n_group < 8 or tokens < 2 * channels else (8, 16, 128), BF16),
        vmem((low + 2, half, 3 * channels), BF16),
        vmem((height, span, channels), F32),
        vmem((height, span, c_in), F32),
        vmem((height + 2, span, 3 * c_in), BF16),
        vmem((height, span, channels), F32),
        vmem((n_group, 8, channels), F32),
        vmem((n_group, tokens, channels), BF16),
        vmem((n_group, channels, tokens), BF16),
        vmem((tokens, channels), BF16),
        vmem((channels, tokens), BF16),
        vmem((tokens, channels), BF16),
        vmem((tokens, channels), BF16),
        vmem((channels, tokens), F32),
        vmem((height, span, channels), BF16),
        vmem((8, channels), F32),
        vmem((3, 8, channels), F32),
        vmem((n_group, 8, channels), F32),
        vmem((span, channels), BF16),
        vmem((span, channels), BF16),
        vmem((3, c_in, 3 * channels), BF16),
        vmem((height, span, channels), BF16),
        vmem((height, channels, span), BF16),
        vmem((8, channels), F32),
        vmem((3, 8, channels), F32),
        vmem((span, channels), BF16),
        vmem((span, channels), BF16),
        vmem((height + 2, span, 3 * channels), BF16),
        vmem((3, low, half, 3 * channels), BF16),
        vmem((low, half, c_in), BF16),
        *sums(blocks_a),
        *sums(blocks_b),
        *sums(blocks_c),
        vmem((n_group, 8, channels), F32),
        vmem((n_group, tokens, tokens), F32),
        vmem((n_group, tokens, tokens), BF16),
        vmem((channels, tokens), F32),
        vmem((channels, tokens), BF16),
        vmem((tokens, channels), BF16),
        vmem((channels, tokens), F32),
        vmem((n_group, tokens, channels), BF16),
        vmem((n_row, tokens, channels), BF16),
        vmem((n_row - 1, tokens, channels), BF16),
        vmem((n_row - 1, tokens, channels), BF16),
        vmem((n_group, 16, channels), F32),
    ]
    shape = jax.ShapeDtypeStruct
    mid = [
        shape((low, half, channels), BF16),
        shape((tokens, channels), BF16),
        shape((height, span, c_in), BF16),
        shape((tokens, channels), BF16),
        shape((blocks_a, 16, 128), BF16),
        shape((blocks_b, 16, 128), BF16),
        shape((blocks_c, 16, 128), BF16),
        shape((n_item, 24, channels), F32),
    ]
    in_vmem = pl.BlockSpec(memory_space=vmem)
    parts = pl.pallas_call(
        functools.partial(main_kernel, n_item, n_row),
        out_shape=mid,
        in_specs=[in_vmem] * len(inputs),
        out_specs=[in_vmem] * len(mid),
        scratch_shapes=scratch,
        compiler_params=pltpu.CompilerParams(
            collective_id=0, has_side_effects=True, vmem_limit_bytes=int(63.9 * 1024 * 1024)
        ),
    )(*inputs)
    emb = arg.embedding.shape[-1]
    final = [
        *mid[:4],
        shape((1, c_in), F32),
        shape((1, c_in), F32),
        shape((9 * c_in, channels), F32),
        shape((1, channels), F32),
        shape((emb, 2 * channels), F32),
        shape((1, 2 * channels), F32),
        shape((1, channels), F32),
        shape((1, channels), F32),
        shape((9 * channels, channels), F32),
        shape((1, channels), F32),
        shape((c_in, channels), F32),
        shape((1, channels), F32),
        shape((1, channels), F32),
        shape((1, channels), F32),
        shape((channels, 3 * channels), F32),
        shape((1, 2 * channels), F32),
        shape((channels, channels), F32),
        shape((1, channels), F32),
        shape((1, 5), F32),
    ]
    outs = pl.pallas_call(
        functools.partial(last_kernel, n_item),
        out_shape=final,
        in_specs=[in_vmem] * len(mid),
        out_specs=[in_vmem] * len(final),
        compiler_params=pltpu.CompilerParams(vmem_limit_bytes=48 * 1024 * 1024),
    )(*parts)
    shapes = (
        (1, low, half, channels),
        (1, rows_t, cols_t, channels),
        (1, height, span, c_in),
        (1, rows_t, cols_t, channels),
        (c_in,),
        (c_in,),
        (3, 3, c_in, channels),
        (channels,),
        (emb, 2 * channels),
        (2 * channels,),
        (channels,),
        (channels,),
        (3, 3, channels, channels),
        (channels,),
        (c_in, channels),
        (channels,),
        (channels,),
        (channels,),
        (channels, 3 * channels),
        (2 * channels,),
        (channels, channels),
        (channels,),
        (5,),
    )
    return tuple(out.reshape(to) for out, to in zip(outs, shapes))


def solution(mesh):
    tiled = P("item", "row", "pair", None)
    mask = P("item", "row", "pair")
    in_specs = [P()] * len(INPUTS)
    for name in ("image", "features", "gpool", "gres"):
        in_specs[INPUTS.index(name)] = tiled
    for name in ("land", "token"):
        in_specs[INPUTS.index(name)] = mask
    in_specs[INPUTS.index("embedding")] = P("item", None)
    return jax.shard_map(
        functools.partial(on_device, dict(mesh.shape)),
        mesh=mesh,
        in_specs=tuple(in_specs),
        out_specs=(tiled,) * 4 + (P(),) * 19,
        check_vma=False,
    )
```

```python
import functools
import math
from types import SimpleNamespace

import jax
import jax.numpy as jnp
from jax import lax
from jax.experimental import pallas as pl
from jax.experimental.pallas import tpu as pltpu
from jax.sharding import PartitionSpec as P

GROUPS = 32
EPS = 1e-05
MASKED = -1000000000.0
LOG2E = 1.4426950408889634
F32 = jnp.float32
BF16 = jnp.bfloat16
MESH = pl.DeviceIdType.MESH
HIGHEST = lax.Precision.HIGHEST


def mm(left, right):
    return jnp.dot(left, right, preferred_element_type=F32)


def mm_t(left, right):
    return lax.dot_general(left, right, (((1,), (1,)), ((), ())), preferred_element_type=F32)


def iota(shape, dim):
    return lax.broadcasted_iota(jnp.int32, shape, dim)


def fold(value):
    rows, width = value.shape
    return jnp.sum(value.reshape(rows // 8, 8, width), axis=0)


def total(value):
    return jnp.sum(value, axis=0, keepdims=True)


def group_total(rows, width):
    channels = rows.shape[-1]
    left = jnp.floor(iota((channels, channels), 0).astype(F32) * (1.0 / width))
    right = jnp.floor(iota((channels, channels), 1).astype(F32) * (1.0 / width))
    same = (left == right).astype(F32)
    padded = jnp.concatenate([rows, jnp.zeros((8 - rows.shape[0], channels), F32)], axis=0)
    return jnp.dot(padded, same, precision=HIGHEST, preferred_element_type=F32)


def sigmoid(value):
    return 0.5 * jnp.tanh(0.5 * value) + 0.5


INPUTS = (
    "image", "land", "embedding", "gain1", "shift1", "kernel1", "bias1", "film_w", "film_b",
    "gain2", "shift2", "kernel2", "bias2", "skip_w", "skip_b", "features", "token", "gain3",
    "shift3", "mix_w", "mix_b", "out_w", "out_b", "gpool", "gres",
)
RESULTS = ("pooled", "result", "image_grad", "features_grad", "sum_a", "sum_b", "sum_c", "vectors")


class Links:
    def __init__(self, ref, n_item, n_row):
        self.ref = ref
        self.n_item, self.n_row, self.n_group = n_item, n_row, n_row * 2
        self.item, self.row, self.pair = (lax.axis_index(a) for a in ("item", "row", "pair"))
        self.sibling = 1 - self.pair
        self.slot = self.row * 2 + self.pair
        self.sends = 0
        self.recvs = 0
        self.pending = []

    def at(self, row=None, pair=None, item=None):
        return (
            self.item if item is None else item,
            self.row if row is None else row,
            self.pair if pair is None else pair,
        )

    def others_in_group(self):
        for step in range(1, self.n_group):
            other = lax.rem(self.slot + step, self.n_group)
            yield other, self.at(lax.div(other, 2), lax.rem(other, 2))

    def others_in_row(self):
        for step in range(1, self.n_row):
            other = lax.rem(self.row + step, self.n_row)
            yield other, self.at(row=other)

    def others_in_item(self):
        for step in range(1, self.n_item):
            other = lax.rem(self.item + step, self.n_item)
            yield other, self.at(item=other)

    def new_recv(self, count=1):
        self.recvs += count
        return self.recvs - count

    def copy(self, source, target, device, send, recv):
        return pltpu.make_async_remote_copy(
            src_ref=source,
            dst_ref=target,
            send_sem=self.ref.send_sem.at[send],
            recv_sem=self.ref.recv_sem.at[recv],
            device_id=device,
            device_id_type=MESH,
        )

    def send(self, source, target, device, recv, when=None):
        index = self.sends
        self.sends += 1

        def make():
            return self.copy(source, target, device, index, recv)

        if when is None:
            make().start()
        else:
            pl.when(when)(lambda: make().start())
        self.pending.append((make, when))

    def send_all(self, copies, size):
        index, recv = self.sends, self.new_recv()
        self.sends += 1
        for source, target, device in copies:
            self.copy(source, target, device, index, recv).start()
        whole = self.copy(size, size, self.at(pair=self.sibling), index, recv)
        self.pending.append((lambda: whole, None))
        return whole.wait_recv

    def arrived(self, target, recv, when=None):
        def wait():
            self.copy(target, target, self.at(pair=self.sibling), 0, recv).wait_recv()

        if when is None:
            wait()
        else:
            pl.when(when)(wait)

    def finish(self):
        for make, when in self.pending:
            if when is None:
                make().wait_send()
            else:
                pl.when(when)(lambda make=make: make().wait_send())

    def greet(self):
        barrier = pltpu.get_barrier_semaphore()
        devices = [d for _, d in self.others_in_group()] + [d for _, d in self.others_in_item()]
        for device in devices:
            pl.semaphore_signal(barrier, inc=1, device_id=device, device_id_type=MESH)
        return lambda: pl.semaphore_wait(barrier, len(devices))

    def share(self, slots):
        mine = slots.at[self.slot]
        copies = [(mine, mine, device) for _, device in self.others_in_group()]
        return self.send_all(copies, slots.at[pl.ds(0, self.n_group - 1)])

    def edge_rows(self, first, last, above, below):
        has_above, has_below = self.row > 0, self.row < self.n_row - 1
        from_above, from_below = self.new_recv(), self.new_recv()
        self.send(first, below, self.at(row=self.row - 1), from_below, has_above)
        self.send(last, above, self.at(row=self.row + 1), from_above, has_below)

        def wait():
            self.arrived(above, from_above, has_above)
            self.arrived(below, from_below, has_below)

            @pl.when(self.row == 0)
            def _():
                above[...] = jnp.zeros(above.shape, above.dtype)

            @pl.when(self.row == self.n_row - 1)
            def _():
                below[...] = jnp.zeros(below.shape, below.dtype)

        return wait

    def edge_columns(self, column, columns):
        has_above, has_below = self.row > 0, self.row < self.n_row - 1
        base = self.new_recv(3)
        self.send(column, columns.at[2], self.at(self.row - 1, self.sibling), base + 2, has_above)
        self.send(column, columns.at[0], self.at(self.row + 1, self.sibling), base, has_below)
        self.send(column, columns.at[1], self.at(pair=self.sibling), base + 1)

        def wait():
            self.arrived(columns.at[1], base + 1)
            self.arrived(columns.at[0], base, has_above)
            self.arrived(columns.at[2], base + 2, has_below)

            @pl.when(self.row == 0)
            def _():
                columns[0] = jnp.zeros(columns.shape[1:], columns.dtype)

            @pl.when(self.row == self.n_row - 1)
            def _():
                columns[2] = jnp.zeros(columns.shape[1:], columns.dtype)

        return wait

    def all_sum(self, part, recv1, recv2, recv3, out):
        half = part.shape[0] // 2
        quarter = half // self.n_item
        chunk = quarter // self.n_row
        mine = self.pair * half
        item_at = mine + self.item * quarter
        own = item_at + self.row * chunk

        def span(ref, start, size):
            return ref.at[pl.ds(start, size)]

        def grow(start, size, arrivals):
            value = part[pl.ds(start, size)].astype(F32)
            for arrival in arrivals:
                value = value + arrival.astype(F32)
            return value.astype(BF16)

        def stage2():
            wait1()
            part[pl.ds(mine, half)] = grow(mine, half, [recv1[...]])
            copies = [
                (span(part, mine + other * quarter, quarter), recv2.at[step], device)
                for step, (other, device) in enumerate(self.others_in_item())
            ]
            wait2 = self.send_all(copies, recv2)

            def stage3():
                wait2()
                part[pl.ds(item_at, quarter)] = grow(item_at, quarter, [recv2[k] for k in range(self.n_item - 1)])
                copies = [
                    (span(part, item_at + other * chunk, chunk), recv3.at[step], device)
                    for step, (other, device) in enumerate(self.others_in_row())
                ]
                wait3 = self.send_all(copies, recv3)

                def stage4():
                    wait3()
                    out[pl.ds(own, chunk)] = grow(own, chunk, [recv3[k] for k in range(self.n_row - 1)])
                    source = span(out, own, chunk)
                    copies = [(source, source, device) for _, device in self.others_in_row()]
                    wait4 = self.send_all(copies, span(out, 0, (self.n_row - 1) * chunk))

                    def stage5():
                        wait4()
                        source = span(out, item_at, quarter)
                        copies = [(source, source, device) for _, device in self.others_in_item()]
                        wait5 = self.send_all(copies, span(out, 0, (self.n_item - 1) * quarter))

                        def stage6():
                            wait5()
                            source = span(out, mine, half)
                            return self.send_all([(source, source, self.at(pair=self.sibling))], span(out, 0, half))

                        return stage6

                    return stage5

                return stage4

            return stage3

        wait1 = self.send_all([(span(part, self.sibling * half, half), recv1, self.at(pair=self.sibling))], recv1)
        return stage2


def norm_terms(sums, squares, count, width):
    size = jnp.maximum(count, 1.0) * width
    grouped = group_total(jnp.concatenate([sums, squares], axis=0), width)
    mean = grouped[0:1] / size
    return mean, lax.rsqrt(grouped[1:2] / size - mean * mean + EPS), size


def chain_order(n_row):
    orders = []
    for row in range(n_row):
        steps = [(row + s, 0, n_row - 1 - s, s) for s in range(n_row - 1) if n_row - 1 - s > row]
        steps += [(n_row - 1 - row + s, 1, s, s) for s in range(n_row - 1) if s < row]
        steps.sort()
        orders.append([(target, 1 - down, down * (n_row - 1) + s) for _, down, target, s in steps])
    return orders


def arrival_order(n_row):
    orders = []
    for row in range(n_row):
        found = [row]
        for step in range(1, n_row):
            found += [r for r in (row - step, row + step) if 0 <= r < n_row]
        orders.append(found)
    return orders


def pick(values, index):
    chosen = jnp.int32(0)
    for k, value in enumerate(values):
        chosen = chosen + jnp.where(index == k, jnp.int32(value), jnp.int32(0))
    return chosen


def main_kernel(n_item, n_row, *refs):
    names = INPUTS + RESULTS + SCRATCH
    ref = SimpleNamespace(**dict(zip(names, refs)))
    link = Links(ref, n_item, n_row)
    height, span, c_in = ref.image.shape
    channels = ref.bias1.shape[-1]
    half = span // 2
    tokens = ref.features.shape[0]
    n_group = link.n_group
    low = height // 2
    side = link.pair.astype(F32)
    width1, width2 = c_in // GROUPS, channels // GROUPS
    slot, item, row, pair, sibling = link.slot, link.item, link.row, link.pair, link.sibling
    factor = channels ** (-0.5)
    zero1 = jnp.zeros((8, c_in), F32)
    zero2 = jnp.zeros((8, channels), F32)

    def lanes(mask, width):
        if width <= mask.shape[1]:
            return mask[:, 0:width]
        return jnp.concatenate([mask] * (width // mask.shape[1]), axis=1)

    def slot_sum(slots):
        value = slots[0]
        for other in range(1, n_group):
            value = value + slots[other]
        return value

    met = link.greet()

    ones = jnp.ones((span, 128), BF16)
    place = iota((span, span), 0)
    place = jnp.where(place < half, 2 * place, 2 * (place - half) + 1)
    spread = place == iota((span, span), 1)

    def land_row(y, carry):
        line = jnp.broadcast_to(ref.land[pl.ds(y, 1), :].astype(F32), (span, span))
        ref.mask[y] = mm(jnp.where(spread, line, 0.0).astype(BF16), ones)
        return carry

    lax.fori_loop(0, height, land_row, 0)

    rows_t, cols_t = ref.token.shape

    def token_mask(flags):
        chosen = iota((rows_t, cols_t, rows_t), 0) == iota((rows_t, cols_t, rows_t), 2)
        lines = mm(chosen.reshape(tokens, rows_t).astype(BF16), flags.astype(F32).astype(BF16))
        keep = (iota((rows_t, cols_t, cols_t), 1) == iota((rows_t, cols_t, cols_t), 2)).reshape(tokens, cols_t)
        return mm(jnp.where(keep, lines, 0.0).astype(BF16), jnp.ones((cols_t, 128), BF16))

    ref.token_mask[...] = token_mask(ref.token[...])

    def split_row(y, line):
        ref.line[...] = line.astype(F32)
        even = ref.line[pl.ds(0, half, stride=2), :]
        odd = ref.line[pl.ds(1, half, stride=2), :]
        ref.normed1[y, 0:half] = even
        ref.normed1[y, half:span] = odd
        return even, odd

    def image_row(y, carry):
        sums, squares, count = carry
        even, odd = split_row(y + 1, ref.image[y])
        value = jnp.concatenate([even, odd], axis=0)
        ref.image_low[y] = value.astype(BF16)
        ref.column1[pl.ds(y, 1), :] = jnp.where(side > 0.5, even[0:1], odd[half - 1 : half])
        mask = ref.mask[y]
        masked = value * mask
        return sums + fold(masked), squares + fold(masked * value), count + fold(mask)

    sums1, squares1, count1 = lax.fori_loop(0, height, image_row, (zero1, zero1, jnp.zeros((8, 128), F32)))
    raw = ref.features[...].astype(F32)
    tmask = ref.token_mask[...]
    tmask2 = lanes(tmask, channels)
    masked = raw * tmask2
    ref.stats1[slot] = jnp.zeros((8, channels), F32)
    ref.stats1[slot, 0:1, 0:c_in] = total(sums1)
    ref.stats1[slot, 0:1, c_in:channels] = total(squares1)
    ref.stats1[slot, 1:2, :] = total(masked)
    ref.stats1[slot, 2:3, :] = total(masked * raw)
    ref.stats1[slot, 3:4, 0:128] = total(count1)
    ref.stats1[slot, 3:4, 128:256] = total(tmask)

    gpre_sum = zero2
    for i in range(low):
        value = (ref.gpool[i].astype(F32) * 0.25 * math.sqrt(0.5)).astype(BF16)
        ref.gpre[i] = value
        ref.gpre_t[:, i * half : (i + 1) * half] = value.T
        wide = value.astype(F32)
        ref.column2[i : i + 1, :] = jnp.where(side > 0.5, wide[0:1], wide[half - 1 : half])
        gpre_sum = gpre_sum + fold(wide)
    ref.flags[slot] = ref.token[...]
    ref.raw[slot] = ref.features[...]

    met()
    wait_stats1 = link.share(ref.stats1)
    wait_image_columns = link.edge_columns(ref.column1, ref.columns1)
    wait_pool_columns = link.edge_columns(ref.column2, ref.columns2)
    wait_image_rows = link.edge_rows(ref.image.at[0], ref.image.at[height - 1], ref.image_up, ref.image_down)
    wait_pool_rows = link.edge_rows(ref.gpool.at[0], ref.gpool.at[low - 1], ref.pool_up, ref.pool_down)
    wait_token = link.share(ref.flags)
    raw_sem = link.new_recv(n_group)

    def raw_send(block, device, when=None):
        index = block * 2 + pair
        link.send(ref.raw.at[index], ref.raw.at[index], device, raw_sem + index, when)

    raw_send(row, link.at(row=row + 1), row < n_row - 1)
    raw_send(row, link.at(row=row - 1), row > 0)
    raw_send(row, link.at(pair=sibling))

    def raw_step(step):
        below, above = row - step, row + step
        link.arrived(ref.raw.at[below * 2 + pair], raw_sem + below * 2 + pair, below >= 0)
        link.arrived(ref.raw.at[above * 2 + pair], raw_sem + above * 2 + pair, above < n_row)
        if step < n_row - 1:
            raw_send(below, link.at(row=row + 1), (below >= 0) & (row < n_row - 1))
            raw_send(above, link.at(row=row - 1), (above < n_row) & (row > 0))
        raw_send(below, link.at(pair=sibling), below >= 0)
        raw_send(above, link.at(pair=sibling), above < n_row)

    coarse = ref.probs if n_group >= 8 and tokens >= 2 * channels else ref.coarse
    upper, lower = {0: (2,), 1: (1, 2)}, {0: (0, 1), 1: (0,)}
    for u in range(2):
        for line, row_taps in enumerate((upper[u], lower[u])):
            tall = []
            for b in range(3):
                tile = sum(ref.kernel2[a, b * channels : (b + 1) * channels, :].astype(F32) for a in row_taps)
                tall.append(tile)
            for v in range(2):
                for place_x, column_taps in enumerate((upper[v], lower[v])):
                    tile = sum(tall[b] for b in column_taps)
                    at = slice(place_x * channels, (place_x + 1) * channels)
                    coarse[u * 4 + v * 2 + line, 0:channels, at] = tile.astype(BF16)

    wait_pool_rows()
    wait_pool_columns()
    first_row = iota((half, channels), 0) == 0
    last_row = iota((half, channels), 0) == half - 1
    for i in range(low + 2):
        if i == 0:
            value, edge = ref.pool_up[...], ref.columns2[0, low - 1 : low, :]
        elif i == low + 1:
            value, edge = ref.pool_down[...], ref.columns2[2, 0:1, :]
        else:
            value, edge = ref.gpre[i - 1], ref.columns2[1, i - 1 : i, :]
        if i in (0, low + 1):
            value = (value.astype(F32) * 0.25 * math.sqrt(0.5)).astype(BF16)
        wide = value.astype(F32)
        left = jnp.where(first_row, edge * side, pltpu.roll(wide, 1, 0))
        right = jnp.where(last_row, edge * (1.0 - side), pltpu.roll(wide, half - 1, 0))
        ref.padded_g[i, :, 0:channels] = left.astype(BF16)
        ref.padded_g[i, :, channels : 2 * channels] = value
        ref.padded_g[i, :, 2 * channels : 3 * channels] = right.astype(BF16)
    for u in range(2):
        for v in range(2):
            value = 0.0
            for line in range(2):
                rows = ref.padded_g[u + line : u + line + low, :, v * channels : (v + 2) * channels]
                taps = coarse[u * 4 + v * 2 + line, 0:channels, 0 : 2 * channels]
                value = value + mm_t(rows.reshape(low * half, 2 * channels), taps)
            for i in range(low):
                ref.grad2[2 * i + u, v * half : (v + 1) * half, :] = value[i * half : (i + 1) * half]

    wait_image_rows()
    wait_image_columns()
    wait_stats1()
    stats1 = slot_sum(ref.stats1)
    count_land = lanes(stats1[3:4, 0:128], channels)
    count_token = lanes(stats1[3:4, 128:256], channels)
    mean1, inv1, size1 = norm_terms(stats1[0:1, 0:c_in], stats1[0:1, c_in:channels], count_land[:, 0:c_in], width1)
    mean3, inv3, size3 = norm_terms(stats1[1:2], stats1[2:3], count_token, width2)
    split_row(0, ref.image_up[...])
    split_row(height + 1, ref.image_down[...])
    gain1, shift1 = ref.gain1[...], ref.shift1[...]

    def write_shifted(target, y, even, odd, edge, size):
        top = iota((half, size), 0) == 0
        end = iota((half, size), 0) == half - 1
        before = jnp.where(top, edge * side, pltpu.roll(odd, 1, 0)).astype(BF16)
        after = jnp.where(end, edge * (1.0 - side), pltpu.roll(even, half - 1, 0)).astype(BF16)
        even, odd = even.astype(BF16), odd.astype(BF16)
        target[y, 0:half, 0:size] = before
        target[y, 0:half, size : 2 * size] = even
        target[y, 0:half, 2 * size : 3 * size] = odd
        target[y, half:span, 0:size] = even
        target[y, half:span, size : 2 * size] = odd
        target[y, half:span, 2 * size : 3 * size] = after

    def act1(value):
        normed = (value - mean1) * inv1
        affine = normed * gain1 + shift1
        gate = sigmoid(affine)
        return normed, affine, gate

    def edge_act(rows):
        _, affine, gate = act1(rows)
        return affine * gate

    has_up = (row > 0).astype(F32)
    has_down = (row < n_row - 1).astype(F32)
    ref.columns1[0] = edge_act(ref.columns1[0]) * has_up
    ref.columns1[1] = edge_act(ref.columns1[1])
    ref.columns1[2] = edge_act(ref.columns1[2]) * has_down

    def act1_edge_row(y, edge, exists):
        _, affine, gate = act1(ref.normed1[y])
        act = affine * gate * exists
        write_shifted(ref.padded1, y, act[0:half], act[half:span], edge, c_in)

    act1_edge_row(0, ref.columns1[0, height - 1 : height, :], has_up)
    act1_edge_row(height + 1, ref.columns1[2, 0:1, :], has_down)

    def act1_row(y, carry):
        normed, affine, gate = act1(ref.normed1[y + 1])
        act = affine * gate
        ref.normed1[y + 1] = normed
        ref.slope1[y] = gate * (1.0 + affine * (1.0 - gate))
        write_shifted(ref.padded1, y + 1, act[0:half], act[half:span], ref.columns1[1, pl.ds(y, 1), :], c_in)
        return carry

    lax.fori_loop(0, height, act1_row, 0)
    raw_step(1)

    def wide_mask(y):
        return lanes(ref.mask[y], channels)

    def conv1_row(y, carry):
        sums, squares = carry
        value = mm(ref.padded1[y], ref.kernel1[0])
        value = value + mm(ref.padded1[y + 1], ref.kernel1[1])
        value = value + mm(ref.padded1[y + 2], ref.kernel1[2])
        value = value + ref.bias1[...]
        ref.hidden[y] = value
        masked = value * wide_mask(y)
        return sums + fold(masked), squares + fold(masked * value)

    sums2, squares2 = lax.fori_loop(0, height, conv1_row, (zero2, zero2))
    ref.stats2[slot] = jnp.zeros((8, channels), F32)
    ref.stats2[slot, 0:1, :] = total(sums2)
    ref.stats2[slot, 1:2, :] = total(squares2)
    wait_stats2 = link.share(ref.stats2)

    scale3 = inv3 * ref.gain3[...]
    shift3 = ref.shift3[...]

    def normalize(index):
        value = ((ref.raw[index].astype(F32) - mean3) * scale3 + shift3).astype(BF16)
        ref.tokens[index] = value
        ref.tokens_t[index] = value.T

    normalize(slot)
    w_query = ref.mix_w[:, 0:channels]
    w_key = ref.mix_w[:, channels : 2 * channels]
    w_value = ref.mix_w[:, 2 * channels : 3 * channels]
    ref.query[...] = (mm(ref.tokens[slot], w_query) + ref.mix_b[:, 0:channels]).astype(BF16)
    ref.query_t[...] = (mm_t(w_key, ref.query[...]) * (factor * LOG2E)).astype(BF16)
    alive = (count_token > 0.0).astype(F32) * factor
    ref.query_k[...] = (mm_t(ref.query[...], w_key) * alive).astype(BF16)
    ref.grad_att[...] = mm_t(ref.gres[...], ref.out_w[...]).astype(BF16)
    ref.grad_t[...] = mm_t(w_value, ref.grad_att[...])

    lines = jnp.broadcast_to(ref.embedding[...], (8, ref.embedding.shape[-1]))
    film = mm(lines, ref.film_w[...])[0:1] + ref.film_b[...]
    film_scale = 1.0 + film[:, 0:channels]
    film_shift = film[:, channels:]

    ref.mixed_t[...] = jnp.zeros((channels, tokens), F32)
    ref.top[...] = jnp.full((8, tokens), -3e38, F32)
    ref.norm[...] = jnp.zeros((8, tokens), F32)

    def attend_block(index):
        mask = lanes(token_mask(ref.flags[index]), tokens)
        scores = mm(ref.tokens[index], ref.query_t[...])
        scores = jnp.where(mask > 0.5, scores, MASKED * LOG2E)
        old = ref.top[0:1]
        new = jnp.max(scores.reshape(tokens // 8, 8, tokens), axis=0)
        new = jnp.maximum(old, jnp.max(new, axis=0, keepdims=True))
        probs = jnp.exp2(scores - new)
        low_probs = probs.astype(BF16)
        ref.probs[index] = low_probs
        ref.tops[index, 0:1] = new
        ref.top[0:1] = new
        shrink = jnp.exp2(old - new)
        ref.norm[0:1] = ref.norm[0:1] * shrink + total(fold(probs))
        ref.mixed_t[...] = ref.mixed_t[...] * shrink + mm(ref.tokens_t[index], low_probs)

    arrivals = arrival_order(n_row)

    def attend(position):
        block = pick([order[position] for order in arrivals], row)

        def body(lane, carry):
            mine = lane == 0
            index = block * 2 + jnp.where(mine, pair, sibling)

            @pl.when(lane == 1)
            def _():
                link.arrived(ref.raw.at[index], raw_sem + index)

            if position == 0:

                @pl.when(lane == 1)
                def _():
                    normalize(index)
            else:
                normalize(index)
            attend_block(index)
            return carry

        lax.fori_loop(0, 2, body, 0)

    wait_token()
    attend(0)
    raw_step(2) if n_row > 2 else None

    wait_stats2()
    stats = slot_sum(ref.stats2)
    mean2, inv2, size2 = norm_terms(stats[0:1], stats[1:2], count_land, width2)
    slope_m = ref.gain2[...] * film_scale
    shift_m = ref.shift2[...] * film_scale + film_shift

    def mid_row(y, carry):
        grad_sum, grad_dot = carry
        normed = (ref.hidden[y] - mean2) * inv2
        affine = normed * slope_m + shift_m
        gate = sigmoid(affine)
        act = affine * gate
        grad = ref.grad2[y] * (gate * (1.0 + affine * (1.0 - gate)))
        ref.hidden[y] = normed
        ref.grad2[y] = grad
        ref.act2[y] = act.astype(BF16)
        ref.column3[pl.ds(y, 1), :] = jnp.where(side > 0.5, act[0:1], act[span - 1 : span])
        return grad_sum + fold(grad), grad_dot + fold(grad * normed)

    grad_sum2, grad_dot2 = lax.fori_loop(0, height, mid_row, (zero2, zero2))
    ref.stats3[slot] = jnp.zeros((8, channels), F32)
    ref.stats3[slot, 0:1, :] = total(grad_sum2)
    ref.stats3[slot, 1:2, :] = total(grad_dot2)
    wait_stats3 = link.share(ref.stats3)
    wait_act_columns = link.edge_columns(ref.column3, ref.columns3)
    wait_act_rows = link.edge_rows(ref.act2.at[0], ref.act2.at[height - 1], ref.act_up, ref.act_down)

    for a in range(3):
        for b in range(3):
            at = slice((2 - b) * channels, (3 - b) * channels)
            ref.kernel1_t[2 - a, :, at] = ref.kernel1[a, b * c_in : (b + 1) * c_in, :]
    attend(1)

    wait_stats3()
    stats = slot_sum(ref.stats3)
    grad_sum2, grad_dot2 = stats[0:1], stats[1:2]
    grouped = group_total(jnp.concatenate([grad_sum2 * slope_m, grad_dot2 * slope_m], axis=0), width2)
    first2, second2 = grouped[0:1] / size2, grouped[1:2] / size2

    def hidden_row(y, carry):
        normed = ref.hidden[y]
        grad = ref.grad2[y] * slope_m - wide_mask(y) * (first2 + normed * second2)
        grad = (grad * inv2).astype(BF16)
        ref.grad_hidden[y] = grad
        ref.grad_hidden_t[y] = grad.T
        wide = grad.astype(F32)
        ref.column4[pl.ds(y, 1), :] = jnp.where(side > 0.5, wide[0:1], wide[span - 1 : span])
        return carry + fold(wide)

    bias1_sum = lax.fori_loop(0, height, hidden_row, zero2)
    wait_hidden_columns = link.edge_columns(ref.column4, ref.columns4)
    wait_hidden_rows = link.edge_rows(
        ref.grad_hidden.at[0], ref.grad_hidden.at[height - 1], ref.hidden_up, ref.hidden_down
    )
    for step in range(3, n_row):
        raw_step(step)

    def pad_rows(target, source, up, down, columns):
        def edge_row(y, line, edge):
            line = line.astype(F32)
            write_shifted(target, y, line[0:half], line[half:span], edge, channels)

        edge_row(0, up[...], columns[0, height - 1 : height, :])
        edge_row(height + 1, down[...], columns[2, 0:1, :])

        def body(y, carry):
            edge_row(y + 1, source[y], columns[1, pl.ds(y, 1), :])
            return carry

        lax.fori_loop(0, height, body, 0)

    wait_act_rows()
    wait_act_columns()
    pad_rows(ref.padded2, ref.act2, ref.act_up, ref.act_down, ref.columns3)

    def box_row(i, carry):
        for a in range(3):
            value = 0.0
            for dy in range(2):
                for side_x in range(2):
                    line = ref.padded2[2 * i + a + dy, side_x * half : (side_x + 1) * half, :]
                    value = value + line.astype(F32)
            ref.padded3[a * (low // 2) + lax.div(i, 2), pl.ds(lax.rem(i, 2) * half, half), :] = value.astype(BF16)
        value = 0.0
        for dy in range(2):
            for side_x in range(2):
                value = value + ref.image_low[2 * i + dy, side_x * half : (side_x + 1) * half, :].astype(F32)
        ref.image_box[i] = value.astype(BF16)
        return carry

    lax.fori_loop(0, low, box_row, 0)

    def put(target, start, stride, value):
        count = value.shape[0] // 16
        for lane in range(value.shape[1] // 128):
            piece = value[:, lane * 128 : (lane + 1) * 128].astype(BF16)
            target[pl.ds(start + lane * stride, count)] = piece.reshape(count, 16, 128)

    rows_a, rows_c = 9 * channels // 16, 10 * c_in // 16

    def kernel2_grad(a, carry):
        boxes = ref.padded3[pl.ds(a * (low // 2), low // 2)].reshape(low * half, 3 * channels)
        value = mm(ref.gpre_t[...], boxes).T
        put(ref.part_a, a * (rows_a // 3), rows_a, value)
        return carry

    lax.fori_loop(0, 3, kernel2_grad, 0)
    next_a = link.all_sum(ref.part_a, ref.recv1_a, ref.recv2_a, ref.recv3_a, ref.sum_a)

    def kernel1_grad(a, carry):
        value = 0.0
        for y in range(height):
            value = value + mm(ref.grad_hidden_t[y], ref.padded1[a + y])
        put(ref.part_c, a * (3 * c_in // 16), rows_c, value.T)
        return carry

    lax.fori_loop(0, 3, kernel1_grad, 0)
    value = mm(ref.gpre_t[...], ref.image_box[...].reshape(low * half, c_in)).T
    put(ref.part_c, 9 * c_in // 16, rows_c, value)
    next_c = link.all_sum(ref.part_c, ref.recv1_c, ref.recv2_c, ref.recv3_c, ref.sum_c)
    next_a = next_a()

    attend(2) if n_row > 2 else None
    next_c = next_c()
    for position in range(3, n_row):
        attend(position)
    next_a = next_a()

    norm = 1.0 / ref.norm[0:1]
    mixed_t = ref.mixed_t[...] * norm
    ref.mixed_t[...] = mixed_t
    grad_t = (ref.grad_t[...] * norm).astype(BF16)
    delta = total(grad_t.astype(F32) * mixed_t)
    ref.grad_low_t[...] = grad_t
    ref.grad_low[...] = grad_t.T
    ref.grad_query_t[...] = jnp.zeros((channels, tokens), F32)
    next_c = next_c()

    last_top = ref.top[0:1]

    def back_block(index, carry):
        grad_sum, grad_dot = carry
        probs = ref.probs[index].astype(F32) * jnp.exp2(ref.tops[index, 0:1] - last_top)
        grad = mm(ref.tokens[index], ref.grad_low_t[...])
        grad = (probs * (grad - delta)).astype(BF16)
        value = mm(grad, ref.query_k[...]) + mm(probs.astype(BF16), ref.grad_low[...])
        ref.grad_tokens[index] = value.astype(BF16)
        ref.grad_query_t[...] += mm(ref.tokens_t[index], grad)
        return grad_sum + fold(value), grad_dot + fold(value * ref.raw[index].astype(F32))

    orders = chain_order(n_row)
    pair_sem = link.new_recv(n_row)
    chain_sem = link.new_recv(2 * (n_row - 1))

    def chain_at(position):
        target, up, index = (pick([order[position][k] for order in orders], row) for k in range(3))
        has_before = jnp.where(up == 1, row, n_row - 1 - row) > 0
        return target, up, index, has_before

    def back(target, carry):
        def body(lane, carry):
            return back_block(target * 2 + jnp.where(lane == 0, sibling, pair), carry)

        carry = body(0, carry)
        index = target * 2 + sibling
        link.send(ref.grad_tokens.at[index], ref.pair_grad.at[target], link.at(pair=sibling), pair_sem + target)
        return body(1, carry)

    def chain_send(position):
        target, up, index, has_before = chain_at(position)
        link.arrived(ref.pair_grad.at[target], pair_sem + target)
        own = ref.pair_grad[target].astype(F32) + ref.grad_tokens[target * 2 + pair].astype(F32)
        ref.chip_grad[position] = own.astype(BF16)

        @pl.when(has_before)
        def _():
            link.arrived(ref.chain_grad.at[index], chain_sem + index)
            ref.chip_grad[position] = (own + ref.chain_grad[index].astype(F32)).astype(BF16)

        link.send(
            ref.chip_grad.at[position], ref.chain_grad.at[index], link.at(row=row + 2 * up - 1), chain_sem + index
        )

    sums3 = (zero2, zero2)
    for position in range(n_row - 1):
        sums3 = back(chain_at(position)[0], sums3)
        if position > 0:
            chain_send(position - 1)
    sums3 = back(row, sums3)
    chain_send(n_row - 2)
    next_a = next_a()

    grad_query_t = (ref.grad_query_t[...] * alive[0:1, 0:1]).astype(BF16)
    grad_query = mm(grad_query_t.T, w_key).astype(BF16)
    attended = (mm(mixed_t.T.astype(BF16), w_value) + ref.mix_b[:, channels:]).astype(BF16)
    rows_b = channels // 16
    put(ref.part_b, 6 * rows_b, rows_b, mm(attended.T, ref.gres[...]))
    put(ref.part_b, 4 * rows_b, rows_b, mm(mixed_t.astype(BF16), ref.grad_att[...]))
    put(ref.part_b, 0, rows_b, mm(ref.tokens_t[slot], grad_query))
    put(ref.part_b, 2 * rows_b, rows_b, mm(grad_query_t, ref.query[...]))
    next_b = link.all_sum(ref.part_b, ref.recv1_b, ref.recv2_b, ref.recv3_b, ref.sum_b)
    next_c = next_c()

    update = mm(attended, ref.out_w[...]) + ref.out_b[...]
    raw = ref.features[...].astype(F32)
    result = raw + update
    ref.result[...] = result.astype(BF16)
    tmask2 = lanes(ref.token_mask[...], channels)
    update_sum = fold(update * update * tmask2)
    result_sum = fold(result * result * tmask2)
    next_b = next_b()
    ref.grad_own[...] = mm_t(grad_query, w_query)
    own_grad = ref.grad_own[...]
    grad_sum3 = total(sums3[0] + fold(own_grad))
    grad_dot3 = total(sums3[1] + fold(own_grad * raw))

    def conv2_rows(i, carry):
        branch_sum, stream_sum = carry
        pooled = 0.0
        for u in range(2):
            y = 2 * i + u
            branch = mm(ref.padded2[y], ref.kernel2[0])
            branch = branch + mm(ref.padded2[y + 1], ref.kernel2[1])
            branch = branch + mm(ref.padded2[y + 2], ref.kernel2[2])
            branch = branch + ref.bias2[...]
            stream = (branch + mm(ref.image_low[y], ref.skip_w[...]) + ref.skip_b[...]) * math.sqrt(0.5)
            mask = wide_mask(y)
            branch_sum = branch_sum + fold(branch * branch * mask)
            stream_sum = stream_sum + fold(stream * stream * mask)
            pooled = pooled + stream[0:half] + stream[half:span]
        ref.pooled[i] = (pooled * 0.25).astype(BF16)
        return branch_sum, stream_sum

    branch_sum, stream_sum = lax.fori_loop(0, low, conv2_rows, (zero2, zero2))
    next_b = next_b()
    next_a = next_a()

    wait_hidden_rows()
    wait_hidden_columns()
    pad_rows(ref.padded3, ref.grad_hidden, ref.hidden_up, ref.hidden_down, ref.columns4)
    next_c = next_c()

    def back1_row(y, carry):
        grad_sum, grad_dot = carry
        value = mm_t(ref.padded3[y], ref.kernel1_t[0])
        value = value + mm_t(ref.padded3[y + 1], ref.kernel1_t[1])
        value = value + mm_t(ref.padded3[y + 2], ref.kernel1_t[2])
        value = value * ref.slope1[y]
        ref.slope1[y] = value
        return grad_sum + fold(value), grad_dot + fold(value * ref.normed1[y + 1])

    grad_sum1, grad_dot1 = lax.fori_loop(0, height, back1_row, (zero1, zero1))
    ref.stats4[slot] = jnp.zeros((16, channels), F32)
    ref.stats4[slot, 11:12, 0:c_in] = total(grad_dot1)
    ref.stats4[slot, 11:12, c_in:channels] = total(grad_sum1)
    for index, value in enumerate((
        grad_sum3,
        (grad_dot3 - mean3 * grad_sum3) * inv3,
        total(bias1_sum),
        4.0 * total(gpre_sum),
        total(fold(ref.gres[...].astype(F32))),
        total(fold(grad_query.astype(F32))),
        total(fold(ref.grad_att[...].astype(F32))),
        total(branch_sum),
        total(stream_sum),
        total(update_sum),
        total(result_sum),
    )):
        ref.stats4[slot, index : index + 1, :] = value
    wait_stats4 = link.share(ref.stats4)
    next_b = next_b()

    last = n_row - 1
    link.arrived(ref.pair_grad.at[row], pair_sem + row)
    ref.grad_own[...] += ref.pair_grad[row].astype(F32) + ref.grad_tokens[slot].astype(F32)
    for index, exists in ((last - row, row > 0), (last + row, row < last)):

        @pl.when(exists)
        def _(index=index):
            link.arrived(ref.chain_grad.at[index], chain_sem + index)
            ref.grad_own[...] += ref.chain_grad[index].astype(F32)

    wait_stats4()
    stats = slot_sum(ref.stats4)
    ref.vectors[item, 0:16, :] = stats
    ref.vectors[item, 16:24, :] = jnp.zeros((8, channels), F32)
    ref.vectors[item, 12:13, :] = grad_dot2 * film_scale
    ref.vectors[item, 13:14, :] = grad_sum2 * film_scale
    ref.vectors[item, 14:15, :] = grad_dot2 * ref.gain2[...] + grad_sum2 * ref.shift2[...]
    ref.vectors[item, 15:16, :] = grad_sum2
    ref.vectors[item, 16:17, :] = ref.embedding[:, 0:channels].astype(F32)
    ref.vectors[item, 17:18, :] = ref.embedding[:, channels : 2 * channels].astype(F32)
    ref.vectors[item, 18:19, 0:c_in] = stats1[0:1, c_in:channels]
    ref.vectors[item, 19:20, :] = stats1[3:4]
    mine = ref.vectors.at[item]
    wait_vectors = link.send_all(
        [(mine, mine, device) for _, device in link.others_in_item()], ref.vectors.at[pl.ds(0, n_item - 1)]
    )
    next_b = next_b()

    grad_sum1, grad_dot1 = stats[11:12, c_in:channels], stats[11:12, 0:c_in]
    grouped = group_total(jnp.concatenate([grad_sum1 * gain1, grad_dot1 * gain1], axis=0), width1)
    first1, second1 = grouped[0:1] / size1, grouped[1:2] / size1

    def image_grad_rows(i, carry):
        skip = mm_t(ref.gpre[i], ref.skip_w[...])
        skip = jnp.concatenate([skip, skip], axis=0)
        for u in range(2):
            y = 2 * i + u
            value = ref.slope1[y] * gain1 - ref.mask[y] * (first1 + ref.normed1[y + 1] * second1)
            value = value * inv1 + skip
            ref.line[pl.ds(0, half, stride=2), :] = value[0:half]
            ref.line[pl.ds(1, half, stride=2), :] = value[half:span]
            ref.image_grad[y] = ref.line[...].astype(BF16)
        return carry

    lax.fori_loop(0, low, image_grad_rows, 0)
    next_b = next_b()

    gain3 = ref.gain3[...]
    grouped = group_total(jnp.concatenate([stats[0:1] * gain3, stats[1:2] * gain3], axis=0), width2)
    first3, second3 = grouped[0:1] / size3, grouped[1:2] / size3
    normed = (ref.features[...].astype(F32) - mean3) * inv3
    value = (ref.grad_own[...] * gain3 - lanes(ref.token_mask[...], channels) * (first3 + normed * second3)) * inv3
    ref.features_grad[...] = (ref.gres[...].astype(F32) + value).astype(BF16)

    wait_vectors()
    for step in (next_a, next_c, next_b):
        while step is not None:
            step = step()
    link.finish()
    assert link.sends <= ref.send_sem.shape[0] and link.recvs <= ref.recv_sem.shape[0], (link.sends, link.recvs)


SCRATCH = (
    "send_sem", "recv_sem", "flags", "raw", "image_up", "image_down", "pool_up", "pool_down", "mask",
    "token_mask", "line", "normed1", "image_low", "column1", "columns1", "stats1", "gpre", "gpre_t",
    "column2", "columns2", "coarse", "padded_g", "grad2", "slope1", "padded1", "hidden", "stats2",
    "tokens", "tokens_t", "query", "query_t", "query_k", "grad_att", "grad_t", "act2", "column3",
    "columns3", "stats3", "act_up", "act_down", "kernel1_t", "grad_hidden", "grad_hidden_t", "column4",
    "columns4", "hidden_up", "hidden_down", "padded2", "image_box", "part_a", "recv1_a",
    "recv2_a", "recv3_a", "part_b", "recv1_b", "recv2_b", "recv3_b", "part_c", "recv1_c", "recv2_c",
    "recv3_c", "padded3", "stats4", "top", "tops", "norm", "probs", "mixed_t", "grad_low_t", "grad_low",
    "grad_query_t", "grad_tokens", "pair_grad", "chip_grad", "chain_grad", "grad_own",
)


def last_kernel(n_item, *refs):
    (pooled, result, image_grad, features_grad, sum_a, sum_b, sum_c, vectors) = refs[:8]
    (o_pooled, o_result, o_image, o_features, o_gain1, o_shift1, o_kernel1, o_bias1, o_film_w, o_film_b,
     o_gain2, o_shift2, o_kernel2, o_bias2, o_skip_w, o_skip_b, o_gain3, o_shift3, o_mix_w, o_mix_b,
     o_out_w, o_out_b, o_rms) = refs[8:]
    o_pooled[...] = pooled[...]
    o_result[...] = result[...]
    o_image[...] = image_grad[...]
    o_features[...] = features_grad[...]
    channels = o_bias1.shape[-1]
    c_in = o_gain1.shape[-1]

    def blocks(ref, start, count):
        return ref[start : start + count].reshape(count * 16, 128).astype(F32)

    lanes = channels // 128
    n_a, n_c, n_k = 9 * channels // 16, 10 * c_in // 16, 9 * c_in // 16
    for lane in range(lanes):
        at = slice(lane * 128, (lane + 1) * 128)
        o_kernel2[:, at] = blocks(sum_a, lane * n_a, n_a)
        o_kernel1[:, at] = blocks(sum_c, lane * n_c, n_k)
        o_skip_w[:, at] = blocks(sum_c, lane * n_c + n_k, n_c - n_k)
    n_b = channels // 16
    for lane in range(3 * lanes):
        o_mix_w[:, lane * 128 : (lane + 1) * 128] = blocks(sum_b, lane * n_b, n_b)
    for lane in range(lanes):
        o_out_w[:, lane * 128 : (lane + 1) * 128] = blocks(sum_b, (3 * lanes + lane) * n_b, n_b)
    value = vectors[0]
    for item in range(1, n_item):
        value = value + vectors[item]
    o_shift3[...] = value[0:1]
    o_gain3[...] = value[1:2]
    o_bias1[...] = value[2:3]
    o_bias2[...] = value[3:4]
    o_skip_b[...] = value[3:4]
    o_out_b[...] = value[4:5]
    o_mix_b[:, 0:channels] = value[5:6]
    o_mix_b[:, channels:] = value[6:7]
    o_gain1[...] = value[11:12, 0:c_in]
    o_shift1[...] = value[11:12, c_in:channels]
    o_gain2[...] = value[12:13]
    o_shift2[...] = value[13:14]
    o_film_b[:, 0:channels] = value[14:15]
    o_film_b[:, channels:] = value[15:16]
    pad = jnp.zeros((8 - n_item, 2 * channels), F32)
    embedding = jnp.concatenate(
        [jnp.concatenate([vectors[i, 16:17, :], vectors[i, 17:18, :]], axis=1) for i in range(n_item)] + [pad], axis=0
    )
    grads = jnp.concatenate(
        [jnp.concatenate([vectors[i, 14:15, :], vectors[i, 15:16, :]], axis=1) for i in range(n_item)] + [pad], axis=0
    )
    o_film_w[...] = lax.dot_general(
        embedding, grads, (((0,), (0,)), ((), ())), precision=HIGHEST, preferred_element_type=F32
    )

    def lane_sum(row):
        return jnp.sum(row, axis=1, keepdims=True)

    land = jnp.maximum(value[19:20, 0:1], 1.0)
    token = jnp.maximum(value[19:20, 128:129], 1.0)
    place = iota((1, 5), 1)
    rms = jnp.zeros((1, 5), F32)
    for index, (square, count) in enumerate((
        (lane_sum(value[18:19, 0:c_in]), land * c_in),
        (lane_sum(value[7:8]), land * channels),
        (lane_sum(value[8:9]), land * channels),
        (lane_sum(value[9:10]), token * channels),
        (lane_sum(value[10:11]), token * channels),
    )):
        rms = jnp.where(place == index, jnp.sqrt(square / count), rms)
    o_rms[...] = rms


def on_device(mesh_shape, *args):
    names = INPUTS
    arg = SimpleNamespace(**dict(zip(names, args)))
    n_item, n_row = mesh_shape["item"], mesh_shape["row"]
    n_group = 2 * n_row
    _, height, span, c_in = arg.image.shape
    channels = arg.bias1.shape[-1]
    _, rows_t, cols_t, _ = arg.features.shape
    tokens = rows_t * cols_t
    low, half = height // 2, span // 2
    inputs = [
        arg.image.reshape(height, span, c_in),
        arg.land_mask.reshape(height, span) if hasattr(arg, "land_mask") else arg.land.reshape(height, span),
        arg.embedding,
        arg.gain1.reshape(1, c_in),
        arg.shift1.reshape(1, c_in),
        arg.kernel1.reshape(3, 3 * c_in, channels),
        arg.bias1.reshape(1, channels),
        arg.film_w,
        arg.film_b.reshape(1, 2 * channels),
        arg.gain2.reshape(1, channels),
        arg.shift2.reshape(1, channels),
        arg.kernel2.reshape(3, 3 * channels, channels),
        arg.bias2.reshape(1, channels),
        arg.skip_w,
        arg.skip_b.reshape(1, channels),
        arg.features.reshape(tokens, channels),
        arg.token.reshape(rows_t, cols_t),
        arg.gain3.reshape(1, channels),
        arg.shift3.reshape(1, channels),
        arg.mix_w,
        arg.mix_b.reshape(1, 2 * channels),
        arg.out_w,
        arg.out_b.reshape(1, channels),
        arg.gpool.reshape(low, half, channels),
        arg.gres.reshape(tokens, channels),
    ]
    share = 2 * n_item * n_row
    blocks_a = -(-9 * channels * channels // 2048 // share) * share
    blocks_b = -(-4 * channels * channels // 2048 // share) * share
    blocks_c = -(-10 * c_in * channels // 2048 // share) * share
    vmem = pltpu.VMEM

    def sums(blocks):
        unit = blocks // 2 // n_item
        return [
            vmem((blocks, 16, 128), BF16),
            vmem((blocks // 2, 16, 128), BF16),
            vmem((n_item - 1, unit, 16, 128), BF16),
            vmem((n_row - 1, unit // n_row, 16, 128), BF16),
        ]

    scratch = [
        pltpu.SemaphoreType.DMA((52 + 6 * n_row,)),
        pltpu.SemaphoreType.DMA((44 + 5 * n_row,)),
        vmem((n_group, rows_t, cols_t), jnp.int32),
        vmem((n_group, tokens, channels), BF16),
        vmem((span, c_in), BF16),
        vmem((span, c_in), BF16),
        vmem((half, channels), BF16),
        vmem((half, channels), BF16),
        vmem((height, span, 128), F32),
        vmem((tokens, 128), F32),
        vmem((span, c_in), F32),
        vmem((height + 2, span, c_in), F32),
        vmem((height, span, c_in), BF16),
        vmem((8, c_in), F32),
        vmem((3, 8, c_in), F32),
        vmem((n_group, 8, channels), F32),
        vmem((low, half, channels), BF16),
        vmem((channels, low * half), BF16),
        vmem((8, channels), F32),
        vmem((3, 8, channels), F32),
        vmem((8, channels, 2 * channels) if n_group < 8 or tokens < 2 * channels else (8, 16, 128), BF16),
        vmem((low + 2, half, 3 * channels), BF16),
        vmem((height, span, channels), F32),
        vmem((height, span, c_in), F32),
        vmem((height + 2, span, 3 * c_in), BF16),
        vmem((height, span, channels), F32),
        vmem((n_group, 8, channels), F32),
        vmem((n_group, tokens, channels), BF16),
        vmem((n_group, channels, tokens), BF16),
        vmem((tokens, channels), BF16),
        vmem((channels, tokens), BF16),
        vmem((tokens, channels), BF16),
        vmem((tokens, channels), BF16),
        vmem((channels, tokens), F32),
        vmem((height, span, channels), BF16),
        vmem((8, channels), F32),
        vmem((3, 8, channels), F32),
        vmem((n_group, 8, channels), F32),
        vmem((span, channels), BF16),
        vmem((span, channels), BF16),
        vmem((3, c_in, 3 * channels), BF16),
        vmem((height, span, channels), BF16),
        vmem((height, channels, span), BF16),
        vmem((8, channels), F32),
        vmem((3, 8, channels), F32),
        vmem((span, channels), BF16),
        vmem((span, channels), BF16),
        vmem((height + 2, span, 3 * channels), BF16),
        vmem((low, half, c_in), BF16),
        *sums(blocks_a),
        *sums(blocks_b),
        *sums(blocks_c),
        vmem((height + 2, span, 3 * channels), BF16),
        vmem((n_group, 16, channels), F32),
        vmem((8, tokens), F32),
        vmem((n_group, 8, tokens), F32),
        vmem((8, tokens), F32),
        vmem((n_group, tokens, tokens), BF16),
        vmem((channels, tokens), F32),
        vmem((channels, tokens), BF16),
        vmem((tokens, channels), BF16),
        vmem((channels, tokens), F32),
        vmem((n_group, tokens, channels), BF16),
        vmem((n_row, tokens, channels), BF16),
        vmem((n_row - 1, tokens, channels), BF16),
        vmem((2 * (n_row - 1), tokens, channels), BF16),
        vmem((tokens, channels), F32),
    ]
    shape = jax.ShapeDtypeStruct
    mid = [
        shape((low, half, channels), BF16),
        shape((tokens, channels), BF16),
        shape((height, span, c_in), BF16),
        shape((tokens, channels), BF16),
        shape((blocks_a, 16, 128), BF16),
        shape((blocks_b, 16, 128), BF16),
        shape((blocks_c, 16, 128), BF16),
        shape((n_item, 24, channels), F32),
    ]
    in_vmem = pl.BlockSpec(memory_space=vmem)
    parts = pl.pallas_call(
        functools.partial(main_kernel, n_item, n_row),
        out_shape=mid,
        in_specs=[in_vmem] * len(inputs),
        out_specs=[in_vmem] * len(mid),
        scratch_shapes=scratch,
        compiler_params=pltpu.CompilerParams(
            collective_id=0, has_side_effects=True, vmem_limit_bytes=int(63.9 * 1024 * 1024)
        ),
    )(*inputs)
    emb = arg.embedding.shape[-1]
    final = [
        *mid[:4],
        shape((1, c_in), F32),
        shape((1, c_in), F32),
        shape((9 * c_in, channels), F32),
        shape((1, channels), F32),
        shape((emb, 2 * channels), F32),
        shape((1, 2 * channels), F32),
        shape((1, channels), F32),
        shape((1, channels), F32),
        shape((9 * channels, channels), F32),
        shape((1, channels), F32),
        shape((c_in, channels), F32),
        shape((1, channels), F32),
        shape((1, channels), F32),
        shape((1, channels), F32),
        shape((channels, 3 * channels), F32),
        shape((1, 2 * channels), F32),
        shape((channels, channels), F32),
        shape((1, channels), F32),
        shape((1, 5), F32),
    ]
    outs = pl.pallas_call(
        functools.partial(last_kernel, n_item),
        out_shape=final,
        in_specs=[in_vmem] * len(mid),
        out_specs=[in_vmem] * len(final),
        compiler_params=pltpu.CompilerParams(vmem_limit_bytes=int(63.9 * 1024 * 1024)),
    )(*parts)
    shapes = (
        (1, low, half, channels),
        (1, rows_t, cols_t, channels),
        (1, height, span, c_in),
        (1, rows_t, cols_t, channels),
        (c_in,),
        (c_in,),
        (3, 3, c_in, channels),
        (channels,),
        (emb, 2 * channels),
        (2 * channels,),
        (channels,),
        (channels,),
        (3, 3, channels, channels),
        (channels,),
        (c_in, channels),
        (channels,),
        (channels,),
        (channels,),
        (channels, 3 * channels),
        (2 * channels,),
        (channels, channels),
        (channels,),
        (5,),
    )
    return tuple(out.reshape(to) for out, to in zip(outs, shapes))


def solution(mesh):
    tiled = P("item", "row", "pair", None)
    mask = P("item", "row", "pair")
    in_specs = [P()] * len(INPUTS)
    for name in ("image", "features", "gpool", "gres"):
        in_specs[INPUTS.index(name)] = tiled
    for name in ("land", "token"):
        in_specs[INPUTS.index(name)] = mask
    in_specs[INPUTS.index("embedding")] = P("item", None)
    return jax.shard_map(
        functools.partial(on_device, dict(mesh.shape)),
        mesh=mesh,
        in_specs=tuple(in_specs),
        out_specs=(tiled,) * 4 + (P(),) * 19,
        check_vma=False,
    )
```

```python
import functools
import math
from types import SimpleNamespace
from typing import Any, NamedTuple

import jax
import jax.numpy as jnp
from jax import lax
from jax.experimental import pallas as pl
from jax.experimental.pallas import tpu as pltpu
from jax.sharding import PartitionSpec as P

GROUPS = 32
EPS = 1e-05
MASKED = -1000000000.0
LOG2E = 1.4426950408889634
F32 = jnp.float32
BF16 = jnp.bfloat16
MESH = pl.DeviceIdType.MESH
HIGHEST = lax.Precision.HIGHEST


def mm(left, right):
    return jnp.dot(left, right, preferred_element_type=F32)


def mm_t(left, right):
    return lax.dot_general(left, right, (((1,), (1,)), ((), ())), preferred_element_type=F32)


def iota(shape, dim):
    return lax.broadcasted_iota(jnp.int32, shape, dim)


def fold(value):
    rows, width = value.shape
    return jnp.sum(value.reshape(rows // 8, 8, width), axis=0)


def total(value):
    return jnp.sum(value, axis=0, keepdims=True)


def group_total(rows, width):
    channels = rows.shape[-1]
    left = jnp.floor(iota((channels, channels), 0).astype(F32) * (1.0 / width))
    right = jnp.floor(iota((channels, channels), 1).astype(F32) * (1.0 / width))
    same = (left == right).astype(F32)
    padded = jnp.concatenate([rows, jnp.zeros((8 - rows.shape[0], channels), F32)], axis=0)
    return jnp.dot(padded, same, precision=HIGHEST, preferred_element_type=F32)


def sigmoid(value):
    return 0.5 * jnp.tanh(0.5 * value) + 0.5


class Inputs(NamedTuple):
    image: Any
    land: Any
    embedding: Any
    gain1: Any
    shift1: Any
    kernel1: Any
    bias1: Any
    film_w: Any
    film_b: Any
    gain2: Any
    shift2: Any
    kernel2: Any
    bias2: Any
    skip_w: Any
    skip_b: Any
    features: Any
    token: Any
    gain3: Any
    shift3: Any
    mix_w: Any
    mix_b: Any
    out_w: Any
    out_b: Any
    gpool: Any
    gres: Any


class Results(NamedTuple):
    pooled: Any
    result: Any
    image_grad: Any
    features_grad: Any
    sum_a: Any
    sum_b: Any
    sum_c: Any
    vectors: Any


INPUTS, RESULTS = Inputs._fields, Results._fields
FETCHED = ("kernel2", "kernel1", "film_w", "mix_w", "out_w", "skip_w", "gres")


class Links:
    def __init__(self, ref, n_item, n_row):
        self.ref = ref
        self.n_item, self.n_row, self.n_group = n_item, n_row, n_row * 2
        self.item, self.row, self.pair = (lax.axis_index(a) for a in ("item", "row", "pair"))
        self.sibling = 1 - self.pair
        self.slot = self.row * 2 + self.pair
        self.sends = 0
        self.recvs = 0
        self.pending = []

    def at(self, row=None, pair=None, item=None):
        return (
            self.item if item is None else item,
            self.row if row is None else row,
            self.pair if pair is None else pair,
        )

    def others_in_group(self):
        for step in range(1, self.n_group):
            other = lax.rem(self.slot + step, self.n_group)
            yield other, self.at(lax.div(other, 2), lax.rem(other, 2))

    def others_in_row(self):
        for step in range(1, self.n_row):
            other = lax.rem(self.row + step, self.n_row)
            yield other, self.at(row=other)

    def others_in_item(self):
        for step in range(1, self.n_item):
            other = lax.rem(self.item + step, self.n_item)
            yield other, self.at(item=other)

    def new_recv(self, count=1):
        self.recvs += count
        return self.recvs - count

    def copy(self, source, target, device, send, recv):
        return pltpu.make_async_remote_copy(
            src_ref=source,
            dst_ref=target,
            send_sem=self.ref.send_sem.at[send],
            recv_sem=self.ref.recv_sem.at[recv],
            device_id=device,
            device_id_type=MESH,
        )

    def send(self, source, target, device, recv, when=None):
        index = self.sends
        self.sends += 1

        def make():
            return self.copy(source, target, device, index, recv)

        if when is None:
            make().start()
        else:
            pl.when(when)(lambda: make().start())
        self.pending.append((make, when))

    def send_all(self, copies, size):
        index, recv = self.sends, self.new_recv()
        self.sends += 1
        for source, target, device in copies:
            self.copy(source, target, device, index, recv).start()
        whole = self.copy(size, size, self.at(pair=self.sibling), index, recv)
        self.pending.append((lambda: whole, None))
        return whole.wait_recv

    def arrived(self, target, recv, when=None):
        def wait():
            self.copy(target, target, self.at(pair=self.sibling), 0, recv).wait_recv()

        if when is None:
            wait()
        else:
            pl.when(when)(wait)

    def finish(self):
        for make, when in self.pending:
            if when is None:
                make().wait_send()
            else:
                pl.when(when)(lambda make=make: make().wait_send())

    def greet(self):
        barrier = pltpu.get_barrier_semaphore()
        devices = [d for _, d in self.others_in_group()] + [d for _, d in self.others_in_item()]
        for device in devices:
            pl.semaphore_signal(barrier, inc=1, device_id=device, device_id_type=MESH)
        return lambda: pl.semaphore_wait(barrier, len(devices))

    def share(self, slots):
        mine = slots.at[self.slot]
        copies = [(mine, mine, device) for _, device in self.others_in_group()]
        return self.send_all(copies, slots.at[pl.ds(0, self.n_group - 1)])

    def edge_rows(self, first, last, above, below):
        has_above, has_below = self.row > 0, self.row < self.n_row - 1
        from_above, from_below = self.new_recv(), self.new_recv()
        self.send(first, below, self.at(row=self.row - 1), from_below, has_above)
        self.send(last, above, self.at(row=self.row + 1), from_above, has_below)

        def wait():
            self.arrived(above, from_above, has_above)
            self.arrived(below, from_below, has_below)

            @pl.when(self.row == 0)
            def _():
                above[...] = jnp.zeros(above.shape, above.dtype)

            @pl.when(self.row == self.n_row - 1)
            def _():
                below[...] = jnp.zeros(below.shape, below.dtype)

        return wait

    def edge_columns(self, column, columns):
        has_above, has_below = self.row > 0, self.row < self.n_row - 1
        base = self.new_recv(3)
        self.send(column, columns.at[2], self.at(self.row - 1, self.sibling), base + 2, has_above)
        self.send(column, columns.at[0], self.at(self.row + 1, self.sibling), base, has_below)
        self.send(column, columns.at[1], self.at(pair=self.sibling), base + 1)

        def wait():
            self.arrived(columns.at[1], base + 1)
            self.arrived(columns.at[0], base, has_above)
            self.arrived(columns.at[2], base + 2, has_below)

            @pl.when(self.row == 0)
            def _():
                columns[0] = jnp.zeros(columns.shape[1:], columns.dtype)

            @pl.when(self.row == self.n_row - 1)
            def _():
                columns[2] = jnp.zeros(columns.shape[1:], columns.dtype)

        return wait

    def all_sum(self, part, recv1, recv2, recv3, out):
        half = part.shape[0] // 2
        quarter = half // self.n_item
        chunk = quarter // self.n_row
        mine = self.pair * half
        item_at = mine + self.item * quarter
        own = item_at + self.row * chunk

        def span(ref, start, size):
            return ref.at[pl.ds(start, size)]

        def grow(start, size, arrivals):
            value = part[pl.ds(start, size)].astype(F32)
            for arrival in arrivals:
                value = value + arrival.astype(F32)
            return value.astype(BF16)

        def stage2():
            wait1()
            part[pl.ds(mine, half)] = grow(mine, half, [recv1[...]])
            copies = [
                (span(part, mine + other * quarter, quarter), recv2.at[step], device)
                for step, (other, device) in enumerate(self.others_in_item())
            ]
            wait2 = self.send_all(copies, recv2)

            def stage3():
                wait2()
                part[pl.ds(item_at, quarter)] = grow(item_at, quarter, [recv2[k] for k in range(self.n_item - 1)])
                copies = [
                    (span(part, item_at + other * chunk, chunk), recv3.at[step], device)
                    for step, (other, device) in enumerate(self.others_in_row())
                ]
                wait3 = self.send_all(copies, recv3)

                def stage4():
                    wait3()
                    out[pl.ds(own, chunk)] = grow(own, chunk, [recv3[k] for k in range(self.n_row - 1)])
                    source = span(out, own, chunk)
                    copies = [(source, source, device) for _, device in self.others_in_row()]
                    wait4 = self.send_all(copies, span(out, 0, (self.n_row - 1) * chunk))

                    def stage5():
                        wait4()
                        source = span(out, item_at, quarter)
                        copies = [(source, source, device) for _, device in self.others_in_item()]
                        wait5 = self.send_all(copies, span(out, 0, (self.n_item - 1) * quarter))

                        def stage6():
                            wait5()
                            source = span(out, mine, half)
                            return self.send_all([(source, source, self.at(pair=self.sibling))], span(out, 0, half))

                        return stage6

                    return stage5

                return stage4

            return stage3

        wait1 = self.send_all([(span(part, self.sibling * half, half), recv1, self.at(pair=self.sibling))], recv1)
        return stage2


def norm_terms(sums, squares, count, width):
    size = jnp.maximum(count, 1.0) * width
    grouped = group_total(jnp.concatenate([sums, squares], axis=0), width)
    mean = grouped[0:1] / size
    return mean, lax.rsqrt(grouped[1:2] / size - mean * mean + EPS), size


def chain_order(n_row):
    orders = []
    for row in range(n_row):
        steps = [(row + s, 0, n_row - 1 - s, s) for s in range(n_row - 1) if n_row - 1 - s > row]
        steps += [(n_row - 1 - row + s, 1, s, s) for s in range(n_row - 1) if s < row]
        steps.sort()
        orders.append([(target, 1 - down, down * (n_row - 1) + s) for _, down, target, s in steps])
    return orders


def arrival_order(n_row):
    orders = []
    for row in range(n_row):
        found = [row]
        for step in range(1, n_row):
            found += [r for r in (row - step, row + step) if 0 <= r < n_row]
        orders.append(found)
    return orders


def pick(values, index):
    chosen = jnp.int32(0)
    for k, value in enumerate(values):
        chosen = chosen + jnp.where(index == k, jnp.int32(value), jnp.int32(0))
    return chosen


def main_kernel(n_item, n_row, *refs):
    names = INPUTS + RESULTS + SCRATCH
    ref = SimpleNamespace(**dict(zip(names, refs)))
    fetches = []
    for index, name in enumerate(FETCHED):
        fetches.append(pltpu.make_async_copy(getattr(ref, name), getattr(ref, name + "_in"), ref.local_sem.at[index]))
        fetches[-1].start()
        setattr(ref, name, getattr(ref, name + "_in"))
    stores = []
    homes = {name: getattr(ref, name) for name in RESULTS}
    for name in RESULTS:
        setattr(ref, name, getattr(ref, name + "_out"))

    def store(name):
        copy = pltpu.make_async_copy(getattr(ref, name), homes[name], ref.local_sem.at[len(FETCHED) + len(stores)])
        copy.start()
        stores.append(copy)

    link = Links(ref, n_item, n_row)
    height, span, c_in = ref.image.shape
    channels = ref.bias1.shape[-1]
    half = span // 2
    tokens = ref.features.shape[0]
    n_group = link.n_group
    low = height // 2
    side = link.pair.astype(F32)
    width1, width2 = c_in // GROUPS, channels // GROUPS
    slot, item, row, pair, sibling = link.slot, link.item, link.row, link.pair, link.sibling
    has_up = (row > 0).astype(F32)
    has_down = (row < n_row - 1).astype(F32)
    factor = channels ** (-0.5)
    zero1 = jnp.zeros((8, c_in), F32)
    zero2 = jnp.zeros((8, channels), F32)
    rows_t, cols_t = ref.token.shape
    now = SimpleNamespace()

    def lanes(mask, width):
        if width <= mask.shape[1]:
            return mask[:, 0:width]
        return jnp.concatenate([mask] * (width // mask.shape[1]), axis=1)

    def wide_mask(y):
        return lanes(ref.mask[y], channels)

    def inner(y):
        return ((y > 0) & (y < height + 1)).astype(F32)

    def exists(y):
        return jnp.where(y == 0, has_up, jnp.where(y == height + 1, has_down, 1.0))

    def slot_sum(slots):
        value = slots[0]
        for other in range(1, n_group):
            value = value + slots[other]
        return value

    def land_line(line):
        place = iota((span, span), 0)
        place = jnp.where(place < half, 2 * place, 2 * (place - half) + 1)
        line = jnp.broadcast_to(line.astype(F32), (span, span))
        line = jnp.where(place == iota((span, span), 1), line, 0.0).astype(BF16)
        return mm(line, jnp.ones((span, 128), BF16))

    def token_mask(flags):
        chosen = iota((rows_t, cols_t, rows_t), 0) == iota((rows_t, cols_t, rows_t), 2)
        lines = mm(chosen.reshape(tokens, rows_t).astype(BF16), flags)
        keep = (iota((rows_t, cols_t, cols_t), 1) == iota((rows_t, cols_t, cols_t), 2)).reshape(tokens, cols_t)
        return mm(jnp.where(keep, lines, 0.0).astype(BF16), jnp.ones((cols_t, 128), BF16))

    def split_row(y, line):
        ref.line[...] = line.astype(F32)
        even = ref.line[pl.ds(0, half, stride=2), :]
        odd = ref.line[pl.ds(1, half, stride=2), :]
        ref.normed1[y, 0:half] = even
        ref.normed1[y, half:span] = odd
        return even, odd

    def write_shifted(target, y, even, odd, edge, size):
        top = iota((half, size), 0) == 0
        end = iota((half, size), 0) == half - 1
        before = jnp.where(top, edge * side, pltpu.roll(odd, 1, 0)).astype(BF16)
        after = jnp.where(end, edge * (1.0 - side), pltpu.roll(even, half - 1, 0)).astype(BF16)
        even, odd = even.astype(BF16), odd.astype(BF16)
        target[y, 0:half, 0:size] = before
        target[y, 0:half, size : 2 * size] = even
        target[y, 0:half, 2 * size : 3 * size] = odd
        target[y, half:span, 0:size] = even
        target[y, half:span, size : 2 * size] = odd
        target[y, half:span, 2 * size : 3 * size] = after

    def set_edges(target, edges):
        size = channels

        def body(y, carry):
            edge = edges[pl.ds(y, 1), :]

            @pl.when(pair == 1)
            def _():
                tile = target[y, 0:16, 0:size].astype(F32)
                target[y, 0:16, 0:size] = jnp.where(iota((16, size), 0) == 0, edge, tile).astype(BF16)

            @pl.when(pair == 0)
            def _():
                tile = target[y, span - 16 : span, 2 * size : 3 * size].astype(F32)
                tile = jnp.where(iota((16, size), 0) == 15, edge, tile).astype(BF16)
                target[y, span - 16 : span, 2 * size : 3 * size] = tile

            return carry

        lax.fori_loop(0, height + 2, body, 0)

    def put(target, start, stride, value):
        count = value.shape[0] // 16
        for lane in range(value.shape[1] // 128):
            piece = value[:, lane * 128 : (lane + 1) * 128].astype(BF16)
            target[pl.ds(start + lane * stride, count)] = piece.reshape(count, 16, 128)

    rows_a, rows_b, rows_c = 9 * channels // 16, channels // 16, 10 * c_in // 16

    def local():
        def land_row(y, carry):
            ref.mask[y + 1] = land_line(ref.land[pl.ds(y, 1), :])
            return carry

        lax.fori_loop(0, height, land_row, 0)
        ref.token_mask[...] = token_mask(ref.token[...].astype(F32).astype(BF16))

        def image_row(y, carry):
            sums, squares, count = carry
            even, odd = split_row(y + 2, ref.image[y])
            value = jnp.concatenate([even, odd], axis=0)
            ref.image_low[y] = value.astype(BF16)
            ref.column1[pl.ds(y, 1), :] = jnp.where(side > 0.5, even[0:1], odd[half - 1 : half])
            mask = ref.mask[y + 1]
            masked = value * mask
            return sums + fold(masked), squares + fold(masked * value), count + fold(mask)

        sums, squares, count = lax.fori_loop(0, height, image_row, (zero1, zero1, jnp.zeros((8, 128), F32)))
        raw = ref.features[...].astype(F32)
        tmask = ref.token_mask[...]
        masked = raw * lanes(tmask, channels)
        ref.stats1[slot, 0:1, 0:c_in] = total(sums)
        ref.stats1[slot, 0:1, c_in:channels] = total(squares)
        ref.stats1[slot, 1:2, :] = total(masked)
        ref.stats1[slot, 2:3, :] = total(masked * raw)
        ref.stats1[slot, 3:4, 0:128] = total(count)
        ref.stats1[slot, 3:4, 128:256] = total(tmask)
        now.gpre_sum = zero2
        for i in range(low):
            value = (ref.gpool[i].astype(F32) * 0.25 * math.sqrt(0.5)).astype(BF16)
            ref.gpre[i] = value
            ref.gpre_t[:, i * half : (i + 1) * half] = value.T
            wide = value.astype(F32)
            ref.column2[i : i + 1, :] = jnp.where(side > 0.5, wide[0:1], wide[half - 1 : half])
            now.gpre_sum = now.gpre_sum + fold(wide)
        ref.flags[slot, 0:rows_t] = ref.token[...].astype(F32).astype(BF16)
        ref.raw[slot] = ref.features[...]

    def raw_send(block, device, when=None):
        index = block * 2 + pair
        link.send(ref.raw.at[index], ref.raw.at[index], device, now.raw_sem + index, when)

    def first_sends():
        now.wait_stats1 = link.share(ref.stats1)
        now.wait_pool_columns = link.edge_columns(ref.column2, ref.columns2)
        now.wait_image_columns = link.edge_columns(ref.column1, ref.columns1)
        now.wait_pool_rows = link.edge_rows(ref.gpool.at[0], ref.gpool.at[low - 1], ref.pool_up, ref.pool_down)
        now.wait_image_rows = link.edge_rows(
            ref.image.at[pl.ds(0, 2)], ref.image.at[pl.ds(height - 2, 2)], ref.image_up, ref.image_down
        )
        now.wait_land_rows = link.edge_rows(ref.land, ref.land, ref.land_up, ref.land_down)
        now.wait_token = link.share(ref.flags)
        now.raw_sem = link.new_recv(n_group)
        raw_send(row, link.at(row=row + 1), row < n_row - 1)
        raw_send(row, link.at(row=row - 1), row > 0)
        raw_send(row, link.at(pair=sibling))

    def raw_step(step):
        below, above = row - step, row + step
        link.arrived(ref.raw.at[below * 2 + pair], now.raw_sem + below * 2 + pair, below >= 0)
        link.arrived(ref.raw.at[above * 2 + pair], now.raw_sem + above * 2 + pair, above < n_row)
        if step < n_row - 1:
            raw_send(below, link.at(row=row + 1), (below >= 0) & (row < n_row - 1))
            raw_send(above, link.at(row=row - 1), (above < n_row) & (row > 0))
        raw_send(below, link.at(pair=sibling), below >= 0)
        raw_send(above, link.at(pair=sibling), above < n_row)

    coarse = ref.probs if n_group >= 8 and tokens >= 2 * channels else ref.coarse

    def coarse_taps():
        for copy in fetches:
            copy.wait()
        upper, lower = {0: (2,), 1: (1, 2)}, {0: (0, 1), 1: (0,)}
        for u in range(2):
            for line, row_taps in enumerate((upper[u], lower[u])):
                tall = []
                for b in range(3):
                    at = slice(b * channels, (b + 1) * channels)
                    tall.append(sum(ref.kernel2[a, at, :].astype(F32) for a in row_taps))
                for v in range(2):
                    for place_x, column_taps in enumerate((upper[v], lower[v])):
                        tile = sum(tall[b] for b in column_taps)
                        at = slice(place_x * channels, (place_x + 1) * channels)
                        coarse[u * 4 + v * 2 + line, 0:channels, at] = tile.astype(BF16)

    def back2():
        now.wait_pool_rows()
        now.wait_pool_columns()
        first_row = iota((half, channels), 0) == 0
        last_row = iota((half, channels), 0) == half - 1
        for i in range(low + 2):
            if i == 0:
                value, edge = ref.pool_up[...], ref.columns2[0, low - 1 : low, :]
            elif i == low + 1:
                value, edge = ref.pool_down[...], ref.columns2[2, 0:1, :]
            else:
                value, edge = ref.gpre[i - 1], ref.columns2[1, i - 1 : i, :]
            if i in (0, low + 1):
                value = (value.astype(F32) * 0.25 * math.sqrt(0.5)).astype(BF16)
            wide = value.astype(F32)
            left = jnp.where(first_row, edge * side, pltpu.roll(wide, 1, 0))
            right = jnp.where(last_row, edge * (1.0 - side), pltpu.roll(wide, half - 1, 0))
            ref.padded_g[i, :, 0:channels] = left.astype(BF16)
            ref.padded_g[i, :, channels : 2 * channels] = value
            ref.padded_g[i, :, 2 * channels : 3 * channels] = right.astype(BF16)
        for u in range(2):
            for v in range(2):
                value = 0.0
                for line in range(2):
                    rows = ref.padded_g[line : line + low + 1, :, v * channels : (v + 2) * channels]
                    taps = coarse[u * 4 + v * 2 + line, 0:channels, 0 : 2 * channels]
                    value = value + mm_t(rows.reshape((low + 1) * half, 2 * channels), taps)
                for i in range(low + 1):
                    ref.grad2[2 * i + 1 - u, v * half : (v + 1) * half, :] = value[i * half : (i + 1) * half]

    def norm1():
        now.wait_stats1()
        stats = slot_sum(ref.stats1)
        now.stats1 = stats
        now.count_land = lanes(stats[3:4, 0:128], channels)
        now.count_token = lanes(stats[3:4, 128:256], channels)
        mean, inv, now.size1 = norm_terms(
            stats[0:1, 0:c_in], stats[0:1, c_in:channels], now.count_land[:, 0:c_in], width1
        )
        now.inv1 = inv
        now.mean3, now.inv3, now.size3 = norm_terms(stats[1:2], stats[2:3], now.count_token, width2)
        gain, shift = ref.gain1[...], ref.shift1[...]

        def act1(value):
            normed = (value - mean) * inv
            affine = normed * gain + shift
            return normed, affine, sigmoid(affine)

        def edge_act(rows):
            _, affine, gate = act1(rows)
            return affine * gate

        now.wait_image_columns()
        ref.columns1[0] = edge_act(ref.columns1[0]) * has_up
        ref.columns1[1] = edge_act(ref.columns1[1])
        ref.columns1[2] = edge_act(ref.columns1[2]) * has_down

        def edge_row(y, edge, there):
            _, affine, gate = act1(ref.normed1[y])
            act = affine * gate * there
            write_shifted(ref.padded1, y, act[0:half], act[half:span], edge, c_in)

        def act1_row(y, carry):
            normed, affine, gate = act1(ref.normed1[y + 2])
            act = affine * gate
            ref.normed1[y + 2] = normed
            ref.slope1[y] = gate * (1.0 + affine * (1.0 - gate))
            write_shifted(ref.padded1, y + 2, act[0:half], act[half:span], ref.columns1[1, pl.ds(y, 1), :], c_in)
            return carry

        lax.fori_loop(0, height, act1_row, 0)
        now.wait_image_rows()
        for k in range(2):
            split_row(k, ref.image_up[k])
            split_row(height + 2 + k, ref.image_down[k])
        for k in range(2):
            edge_row(k, ref.columns1[0, height - 2 + k : height - 1 + k, :], has_up)
            edge_row(height + 2 + k, ref.columns1[2, k : k + 1, :], has_down)

    def conv1():
        now.wait_land_rows()
        ref.mask[0] = land_line(ref.land_up[height - 1 : height, :])
        ref.mask[height + 1] = land_line(ref.land_down[0:1, :])

        def conv1_row(y, carry):
            sums, squares = carry
            value = mm(ref.padded1[y], ref.kernel1[0])
            value = value + mm(ref.padded1[y + 1], ref.kernel1[1])
            value = value + mm(ref.padded1[y + 2], ref.kernel1[2])
            value = value + ref.bias1[...]
            ref.hidden[y] = value
            masked = value * wide_mask(y)
            keep = inner(y)
            return sums + fold(masked) * keep, squares + fold(masked * value) * keep

        sums, squares = lax.fori_loop(0, height + 2, conv1_row, (zero2, zero2))
        ref.stats2[slot, 0:1, :] = total(sums)
        ref.stats2[slot, 1:2, :] = total(squares)
        now.wait_stats2 = link.share(ref.stats2)

    def normalize(index):
        scale = now.inv3 * ref.gain3[...]
        value = ((ref.raw[index].astype(F32) - now.mean3) * scale + ref.shift3[...]).astype(BF16)
        ref.tokens[index] = value
        ref.tokens_t[index] = value.T

    def weights(k):
        return ref.mix_w[:, k * channels : (k + 1) * channels]

    def queries():
        now.wait_token()
        normalize(slot)
        ref.query[...] = (mm(ref.tokens[slot], weights(0)) + ref.mix_b[:, 0:channels]).astype(BF16)
        ref.query_t[...] = (mm_t(weights(1), ref.query[...]) * (factor * LOG2E)).astype(BF16)
        now.alive = (now.count_token > 0.0).astype(F32) * factor
        ref.query_k[...] = (mm_t(ref.query[...], weights(1)) * now.alive).astype(BF16)
        ref.grad_att[...] = mm_t(ref.gres[...], ref.out_w[...]).astype(BF16)
        ref.grad_t[...] = mm_t(weights(2), ref.grad_att[...])
        ref.mixed_t[...] = jnp.zeros((channels, tokens), F32)
        ref.top[...] = jnp.full((8, tokens), -3e38, F32)
        ref.norm[...] = jnp.zeros((8, tokens), F32)

    def attend_block(index):
        mask = lanes(token_mask(ref.flags[index, 0:rows_t]), tokens)
        scores = mm(ref.tokens[index], ref.query_t[...])
        scores = jnp.where(mask > 0.5, scores, MASKED * LOG2E)
        old = ref.top[0:1]
        new = jnp.max(scores.reshape(tokens // 8, 8, tokens), axis=0)
        new = jnp.maximum(old, jnp.max(new, axis=0, keepdims=True))
        probs = jnp.exp2(scores - new)
        low_probs = probs.astype(BF16)
        ref.probs[index] = low_probs
        ref.tops[index, 0:1] = new
        ref.top[0:1] = new
        shrink = jnp.exp2(old - new)
        ref.norm[0:1] = ref.norm[0:1] * shrink + total(fold(probs))
        ref.mixed_t[...] = ref.mixed_t[...] * shrink + mm(ref.tokens_t[index], low_probs)

    arrivals = arrival_order(n_row)

    def attend(position):
        block = pick([order[position] for order in arrivals], row)

        def body(lane, carry):
            index = block * 2 + jnp.where(lane == 0, pair, sibling)

            @pl.when(lane == 1)
            def _():
                link.arrived(ref.raw.at[index], now.raw_sem + index)

            if position == 0:

                @pl.when(lane == 1)
                def _():
                    normalize(index)
            else:
                normalize(index)
            attend_block(index)
            return carry

        lax.fori_loop(0, 2, body, 0)

    def film():
        lines = jnp.broadcast_to(ref.embedding[...], (8, ref.embedding.shape[-1]))
        value = mm(lines, ref.film_w[...])[0:1] + ref.film_b[...]
        now.film_scale = 1.0 + value[:, 0:channels]
        now.slope_m = ref.gain2[...] * now.film_scale
        now.shift_m = ref.shift2[...] * now.film_scale + value[:, channels:]

    def mid():
        now.wait_stats2()
        stats = slot_sum(ref.stats2)
        mean, inv, now.size2 = norm_terms(stats[0:1], stats[1:2], now.count_land, width2)
        now.inv2 = inv
        slope_m, shift_m = now.slope_m, now.shift_m

        def mid_row(y, carry):
            grad_sum, grad_dot = carry
            normed = (ref.hidden[y] - mean) * inv
            affine = normed * slope_m + shift_m
            gate = sigmoid(affine)
            act = affine * gate
            grad = ref.grad2[y] * (gate * (1.0 + affine * (1.0 - gate)))
            ref.hidden[y] = normed
            ref.grad2[y] = grad
            act = act * exists(y)
            write_shifted(ref.padded2, y, act[0:half], act[half:span], 0.0, channels)
            ref.column3[pl.ds(y, 1), :] = jnp.where(side > 0.5, act[0:1], act[span - 1 : span])
            keep = inner(y)
            return grad_sum + fold(grad) * keep, grad_dot + fold(grad * normed) * keep

        grad_sum, grad_dot = lax.fori_loop(0, height + 2, mid_row, (zero2, zero2))
        ref.stats3[slot, 0:1, :] = total(grad_sum)
        ref.stats3[slot, 1:2, :] = total(grad_dot)
        now.wait_stats3 = link.share(ref.stats3)
        now.wait_act_column = link.send_all([(ref.column3, ref.edge3, link.at(pair=sibling))], ref.edge3)

    def kernel2_grad():
        now.wait_act_column()
        set_edges(ref.padded2, ref.edge3)

        def box_row(i, carry):
            for a in range(3):
                value = 0.0
                for dy in range(2):
                    for side_x in range(2):
                        line = ref.padded2[2 * i + a + dy, side_x * half : (side_x + 1) * half, :]
                        value = value + line.astype(F32)
                at = a * (low // 2) + lax.div(i, 2)
                ref.padded3[at, pl.ds(lax.rem(i, 2) * half, half), :] = value.astype(BF16)
            return carry

        lax.fori_loop(0, low, box_row, 0)

        def body(a, carry):
            boxes = ref.padded3[pl.ds(a * (low // 2), low // 2)].reshape(low * half, 3 * channels)
            value = mm(ref.gpre_t[...], boxes).T
            put(ref.part_a, a * (rows_a // 3), rows_a, value)
            return carry

        lax.fori_loop(0, 3, body, 0)
        now.sum_a = link.all_sum(ref.part_a, ref.recv1_a, ref.recv2_a, ref.recv3_a, ref.sum_a)

    def hidden():
        now.wait_stats3()
        stats = slot_sum(ref.stats3)
        now.grad_sum2, now.grad_dot2 = stats[0:1], stats[1:2]
        slope_m, inv = now.slope_m, now.inv2
        grouped = group_total(jnp.concatenate([now.grad_sum2 * slope_m, now.grad_dot2 * slope_m], axis=0), width2)
        first, second = grouped[0:1] / now.size2, grouped[1:2] / now.size2

        def hidden_row(y, carry):
            normed = ref.hidden[y]
            grad = ref.grad2[y] * slope_m - wide_mask(y) * (first + normed * second)
            grad = (grad * (inv * exists(y))).astype(BF16)
            wide = grad.astype(F32)
            write_shifted(ref.padded3, y, wide[0:half], wide[half:span], 0.0, channels)
            ref.column4[pl.ds(y, 1), :] = jnp.where(side > 0.5, wide[0:1], wide[span - 1 : span])

            @pl.when((y > 0) & (y < height + 1))
            def _():
                ref.grad_hidden_t[y - 1] = grad.T

            return carry + fold(wide) * inner(y)

        now.bias1_sum = lax.fori_loop(0, height + 2, hidden_row, zero2)
        now.wait_hidden_column = link.send_all([(ref.column4, ref.edge4, link.at(pair=sibling))], ref.edge4)

    def image_boxes():
        for i in range(low):
            value = 0.0
            for dy in range(2):
                for side_x in range(2):
                    at = slice(side_x * half, (side_x + 1) * half)
                    value = value + ref.image_low[2 * i + dy, at, :].astype(F32)
            ref.image_box[i] = value.astype(BF16)
        value = mm(ref.gpre_t[...], ref.image_box[...].reshape(low * half, c_in)).T
        put(ref.part_c, 9 * c_in // 16, rows_c, value)

    def kernel1_grad():
        def body(a, carry):
            value = 0.0
            for y in range(height):
                value = value + mm(ref.grad_hidden_t[y], ref.padded1[a + y + 1])
            put(ref.part_c, a * (3 * c_in // 16), rows_c, value.T)
            return carry

        lax.fori_loop(0, 3, body, 0)
        now.sum_c = link.all_sum(ref.part_c, ref.recv1_c, ref.recv2_c, ref.recv3_c, ref.sum_c)

    def attended():
        norm = 1.0 / ref.norm[0:1]
        mixed_t = ref.mixed_t[...] * norm
        ref.mixed_t[...] = mixed_t
        grad_t = (ref.grad_t[...] * norm).astype(BF16)
        now.delta = total(grad_t.astype(F32) * mixed_t)
        ref.grad_low_t[...] = grad_t
        ref.grad_low[...] = grad_t.T
        ref.grad_query_t[...] = jnp.zeros((channels, tokens), F32)
        now.last_top = ref.top[0:1]
        now.sums3 = (zero2, zero2)
        now.pair_sem = link.new_recv(n_row)
        now.chain_sem = link.new_recv(2 * (n_row - 1))
        now.chain_send_sem = link.sends
        link.sends += n_row - 1

    def back_block(index, carry):
        grad_sum, grad_dot = carry
        probs = ref.probs[index].astype(F32) * jnp.exp2(ref.tops[index, 0:1] - now.last_top)
        grad = mm(ref.tokens[index], ref.grad_low_t[...])
        grad = (probs * (grad - now.delta)).astype(BF16)
        value = mm(grad, ref.query_k[...]) + mm(probs.astype(BF16), ref.grad_low[...])
        ref.grad_tokens[index] = value.astype(BF16)
        ref.grad_query_t[...] += mm(ref.tokens_t[index], grad)
        return grad_sum + fold(value), grad_dot + fold(value * ref.raw[index].astype(F32))

    orders = chain_order(n_row)

    def chain_at(position):
        target, up, index = (pick([order[position][k] for order in orders], row) for k in range(3))
        has_before = jnp.where(up == 1, row, n_row - 1 - row) > 0
        return target, up, index, has_before

    def back(position):
        target = row if position == n_row - 1 else chain_at(position)[0]

        def body(lane, carry):
            return back_block(target * 2 + jnp.where(lane == 0, sibling, pair), carry)

        now.sums3 = body(0, now.sums3)
        index = target * 2 + sibling
        link.send(ref.grad_tokens.at[index], ref.pair_grad.at[target], link.at(pair=sibling), now.pair_sem + target)
        now.sums3 = body(1, now.sums3)

    def chain_send(position, first):
        target, up, index, has_before = chain_at(position)
        source, device = ref.chip_grad.at[position], link.at(row=row + 2 * up - 1)
        send_sem = now.chain_send_sem + position

        @pl.when(jnp.logical_not(has_before) if first else has_before)
        def _():
            link.arrived(ref.pair_grad.at[target], now.pair_sem + target)
            own = ref.pair_grad[target].astype(F32) + ref.grad_tokens[target * 2 + pair].astype(F32)
            if not first:
                link.arrived(ref.chain_grad.at[index], now.chain_sem + index)
                own = own + ref.chain_grad[index].astype(F32)
            ref.chip_grad[position] = own.astype(BF16)
            link.copy(source, ref.chain_grad.at[index], device, send_sem, now.chain_sem + index).start()

        if not first:
            link.pending.append((lambda: link.copy(source, source, device, send_sem, 0), None))

    def mix_grads():
        grad_query_t = (ref.grad_query_t[...] * now.alive[0:1, 0:1]).astype(BF16)
        now.grad_query = mm(grad_query_t.T, weights(1)).astype(BF16)
        mixed_t = ref.mixed_t[...]
        now.attended = (mm(mixed_t.T.astype(BF16), weights(2)) + ref.mix_b[:, channels:]).astype(BF16)
        put(ref.part_b, 6 * rows_b, rows_b, mm(now.attended.T, ref.gres[...]))
        put(ref.part_b, 4 * rows_b, rows_b, mm(mixed_t.astype(BF16), ref.grad_att[...]))
        put(ref.part_b, 0, rows_b, mm(ref.tokens_t[slot], now.grad_query))
        put(ref.part_b, 2 * rows_b, rows_b, mm(grad_query_t, ref.query[...]))
        now.sum_b = link.all_sum(ref.part_b, ref.recv1_b, ref.recv2_b, ref.recv3_b, ref.sum_b)

    def result():
        update = mm(now.attended, ref.out_w[...]) + ref.out_b[...]
        raw = ref.features[...].astype(F32)
        value = raw + update
        ref.result[...] = value.astype(BF16)
        store("result")
        tmask2 = lanes(ref.token_mask[...], channels)
        now.update_sum = fold(update * update * tmask2)
        now.result_sum = fold(value * value * tmask2)
        own_grad = mm_t(now.grad_query, weights(0))
        ref.grad_own[...] = own_grad
        now.grad_sum3 = total(now.sums3[0] + fold(own_grad))
        now.grad_dot3 = total(now.sums3[1] + fold(own_grad * raw))

    def conv2():
        def conv2_rows(i, carry):
            branch_sum, stream_sum = carry
            pooled = 0.0
            for u in range(2):
                y = 2 * i + u
                branch = mm(ref.padded2[y], ref.kernel2[0])
                branch = branch + mm(ref.padded2[y + 1], ref.kernel2[1])
                branch = branch + mm(ref.padded2[y + 2], ref.kernel2[2])
                branch = branch + ref.bias2[...]
                stream = (branch + mm(ref.image_low[y], ref.skip_w[...]) + ref.skip_b[...]) * math.sqrt(0.5)
                mask = wide_mask(y + 1)
                branch_sum = branch_sum + fold(branch * branch * mask)
                stream_sum = stream_sum + fold(stream * stream * mask)
                pooled = pooled + stream[0:half] + stream[half:span]
            ref.pooled[i] = (pooled * 0.25).astype(BF16)
            return branch_sum, stream_sum

        now.branch_sum, now.stream_sum = lax.fori_loop(0, low, conv2_rows, (zero2, zero2))
        store("pooled")

    def taps1():
        for a in range(3):
            for b in range(3):
                at = slice((2 - b) * channels, (3 - b) * channels)
                ref.kernel1_t[2 - a, :, at] = ref.kernel1[a, b * c_in : (b + 1) * c_in, :]

    def back1():
        now.wait_hidden_column()
        set_edges(ref.padded3, ref.edge4)

        def back1_row(y, carry):
            grad_sum, grad_dot = carry
            value = mm_t(ref.padded3[y], ref.kernel1_t[0])
            value = value + mm_t(ref.padded3[y + 1], ref.kernel1_t[1])
            value = value + mm_t(ref.padded3[y + 2], ref.kernel1_t[2])
            value = value * ref.slope1[y]
            ref.slope1[y] = value
            return grad_sum + fold(value), grad_dot + fold(value * ref.normed1[y + 2])

        now.grad_sum1, now.grad_dot1 = lax.fori_loop(0, height, back1_row, (zero1, zero1))

    def last_share():
        ref.stats4[slot, 11:12, 0:c_in] = total(now.grad_dot1)
        ref.stats4[slot, 11:12, c_in:channels] = total(now.grad_sum1)
        for index, value in enumerate((
            now.grad_sum3,
            (now.grad_dot3 - now.mean3 * now.grad_sum3) * now.inv3,
            total(now.bias1_sum),
            4.0 * total(now.gpre_sum),
            total(fold(ref.gres[...].astype(F32))),
            total(fold(now.grad_query.astype(F32))),
            total(fold(ref.grad_att[...].astype(F32))),
            total(now.branch_sum),
            total(now.stream_sum),
            total(now.update_sum),
            total(now.result_sum),
        )):
            ref.stats4[slot, index : index + 1, :] = value
        now.wait_stats4 = link.share(ref.stats4)

    def last_sums():
        now.wait_stats4()
        stats = slot_sum(ref.stats4)
        now.stats4 = stats
        ref.vectors[item, 0:12, :] = stats
        ref.vectors[item, 12:13, :] = now.grad_dot2 * now.film_scale
        ref.vectors[item, 13:14, :] = now.grad_sum2 * now.film_scale
        ref.vectors[item, 14:15, :] = now.grad_dot2 * ref.gain2[...] + now.grad_sum2 * ref.shift2[...]
        ref.vectors[item, 15:16, :] = now.grad_sum2
        ref.vectors[item, 16:17, :] = ref.embedding[:, 0:channels].astype(F32)
        ref.vectors[item, 17:18, :] = ref.embedding[:, channels : 2 * channels].astype(F32)
        ref.vectors[item, 18:19, :] = now.stats1[0:1]
        ref.vectors[item, 19:20, :] = now.stats1[3:4]
        mine = ref.vectors.at[item]
        now.wait_vectors = link.send_all(
            [(mine, mine, device) for _, device in link.others_in_item()], ref.vectors.at[pl.ds(0, n_item - 1)]
        )

    def image_grad():
        stats = now.stats4
        gain, inv = ref.gain1[...], now.inv1
        grad_sum, grad_dot = stats[11:12, c_in:channels], stats[11:12, 0:c_in]
        grouped = group_total(jnp.concatenate([grad_sum * gain, grad_dot * gain], axis=0), width1)
        first, second = grouped[0:1] / now.size1, grouped[1:2] / now.size1

        def body(i, carry):
            skip = mm_t(ref.gpre[i], ref.skip_w[...])
            skip = jnp.concatenate([skip, skip], axis=0)
            for u in range(2):
                y = 2 * i + u
                value = ref.slope1[y] * gain - ref.mask[y + 1] * (first + ref.normed1[y + 2] * second)
                value = value * inv + skip
                ref.line[pl.ds(0, half, stride=2), :] = value[0:half]
                ref.line[pl.ds(1, half, stride=2), :] = value[half:span]
                ref.image_grad[y] = ref.line[...].astype(BF16)
            return carry

        lax.fori_loop(0, low, body, 0)
        store("image_grad")

    def features_grad():
        last = n_row - 1
        link.arrived(ref.pair_grad.at[row], now.pair_sem + row)
        ref.grad_own[...] += ref.pair_grad[row].astype(F32) + ref.grad_tokens[slot].astype(F32)
        for index, there in ((last - row, row > 0), (last + row, row < last)):

            @pl.when(there)
            def _(index=index):
                link.arrived(ref.chain_grad.at[index], now.chain_sem + index)
                ref.grad_own[...] += ref.chain_grad[index].astype(F32)

        stats, gain = now.stats4, ref.gain3[...]
        grouped = group_total(jnp.concatenate([stats[0:1] * gain, stats[1:2] * gain], axis=0), width2)
        first, second = grouped[0:1] / now.size3, grouped[1:2] / now.size3
        normed = (ref.features[...].astype(F32) - now.mean3) * now.inv3
        value = ref.grad_own[...] * gain - lanes(ref.token_mask[...], channels) * (first + normed * second)
        ref.features_grad[...] = (ref.gres[...].astype(F32) + value * now.inv3).astype(BF16)
        store("features_grad")

    def step(name):
        stage = getattr(now, name)
        setattr(now, name, stage() if stage is not None else None)

    def step_a():
        step("sum_a")

    def step_b():
        step("sum_b")

    def step_c():
        step("sum_c")

    met = link.greet()
    local()
    met()
    first_sends()
    coarse_taps()
    back2()
    norm1()
    conv1()
    raw_step(1)
    queries()
    film()
    attend(0)
    mid()
    for k in range(2, min(3, n_row)): raw_step(k)
    kernel2_grad()
    taps1()
    step_a()
    hidden()
    attend(1)
    image_boxes()
    kernel1_grad()
    for k in range(3, n_row): raw_step(k)
    for k in range(2, min(3, n_row)): attend(k)
    step_c()
    for k in range(3, n_row): attend(k)
    step_a()
    attended()
    back(0)
    back(1)
    chain_send(0, True)
    step_a()
    for k in range(2, n_row - 1): (back(k), chain_send(k - 1, True))
    back(n_row - 1)
    step_c()
    mix_grads()
    chain_send(n_row - 2, True)
    result()
    step_b()
    chain_send(0, False)
    conv2()
    step_a()
    step_b()
    back1()
    for k in range(1, min(2, n_row - 1)): chain_send(k, False)
    step_c()
    last_share()
    step_a()
    step_b()
    for k in range(2, n_row - 1): chain_send(k, False)
    step_c()
    last_sums()
    step_b()
    image_grad()
    step_c()
    step_b()
    features_grad()
    steps = [now.sum_a, now.sum_c, now.sum_b, now.wait_vectors]
    while steps:
        steps = [stage() for stage in steps if stage is not None]
    for name in ("sum_a", "sum_b", "sum_c", "vectors"):
        store(name)
    link.finish()
    for copy in stores:
        copy.wait()
    assert link.sends <= ref.send_sem.shape[0] and link.recvs <= ref.recv_sem.shape[0], (link.sends, link.recvs)


class Scratch(NamedTuple):
    send_sem: Any
    recv_sem: Any
    flags: Any
    raw: Any
    image_up: Any
    image_down: Any
    land_up: Any
    land_down: Any
    pool_up: Any
    pool_down: Any
    mask: Any
    token_mask: Any
    line: Any
    normed1: Any
    image_low: Any
    column1: Any
    columns1: Any
    stats1: Any
    gpre: Any
    gpre_t: Any
    column2: Any
    columns2: Any
    coarse: Any
    padded_g: Any
    grad2: Any
    slope1: Any
    padded1: Any
    hidden: Any
    stats2: Any
    tokens: Any
    tokens_t: Any
    query: Any
    query_t: Any
    query_k: Any
    grad_att: Any
    grad_t: Any
    column3: Any
    edge3: Any
    stats3: Any
    kernel1_t: Any
    grad_hidden_t: Any
    column4: Any
    edge4: Any
    padded2: Any
    image_box: Any
    part_a: Any
    recv1_a: Any
    recv2_a: Any
    recv3_a: Any
    part_b: Any
    recv1_b: Any
    recv2_b: Any
    recv3_b: Any
    part_c: Any
    recv1_c: Any
    recv2_c: Any
    recv3_c: Any
    padded3: Any
    stats4: Any
    top: Any
    tops: Any
    norm: Any
    probs: Any
    mixed_t: Any
    grad_low_t: Any
    grad_low: Any
    grad_query_t: Any
    grad_tokens: Any
    pair_grad: Any
    chip_grad: Any
    chain_grad: Any
    grad_own: Any
    local_sem: Any


SCRATCH = Scratch._fields + tuple(name + "_in" for name in FETCHED) + tuple(name + "_out" for name in RESULTS)


class LastOut(NamedTuple):
    gain1: Any
    shift1: Any
    kernel1: Any
    bias1: Any
    film_w: Any
    film_b: Any
    gain2: Any
    shift2: Any
    kernel2: Any
    bias2: Any
    skip_w: Any
    skip_b: Any
    gain3: Any
    shift3: Any
    mix_w: Any
    mix_b: Any
    out_w: Any
    out_b: Any
    rms: Any


LAST_OUT = LastOut._fields
LAST_BIG = ("kernel1", "film_w", "kernel2", "skip_w", "mix_w", "out_w")


def last_kernel(n_item, *refs):
    count = len(RESULTS)
    source = dict(zip(RESULTS, refs))
    target = dict(zip(RESULTS[:4] + LAST_OUT, refs[count:]))
    rest = refs[count + 4 + len(LAST_OUT) :]
    held = dict(zip(RESULTS + LAST_BIG, rest))
    in_sem, out_sem = rest[count + len(LAST_BIG) :]
    arrivals = {}
    for index, name in enumerate(("vectors", "sum_c", "sum_b", "sum_a") + RESULTS[:4]):
        arrivals[name] = pltpu.make_async_copy(source[name], held[name], in_sem.at[index])
        arrivals[name].start()
    leaving = []

    def leave(name):
        copy = pltpu.make_async_copy(held[name], target[name], out_sem.at[len(leaving)])
        copy.start()
        leaving.append(copy)

    o = SimpleNamespace(**target)
    channels, c_in = o.bias1.shape[-1], o.gain1.shape[-1]

    arrivals["vectors"].wait()
    vectors = held["vectors"]
    value = vectors[0]
    for item in range(1, n_item):
        value = value + vectors[item]
    o.shift3[...] = value[0:1]
    o.gain3[...] = value[1:2]
    o.bias1[...] = value[2:3]
    o.bias2[...] = value[3:4]
    o.skip_b[...] = value[3:4]
    o.out_b[...] = value[4:5]
    o.mix_b[:, 0:channels] = value[5:6]
    o.mix_b[:, channels:] = value[6:7]
    o.gain1[...] = value[11:12, 0:c_in]
    o.shift1[...] = value[11:12, c_in:channels]
    o.gain2[...] = value[12:13]
    o.shift2[...] = value[13:14]
    o.film_b[:, 0:channels] = value[14:15]
    o.film_b[:, channels:] = value[15:16]
    pad = jnp.zeros((8 - n_item, 2 * channels), F32)

    def stacked(first):
        rows = [
            jnp.concatenate([vectors[i, first : first + 1, :], vectors[i, first + 1 : first + 2, :]], axis=1)
            for i in range(n_item)
        ]
        return jnp.concatenate(rows + [pad], axis=0)

    held["film_w"][...] = lax.dot_general(
        stacked(16), stacked(14), (((0,), (0,)), ((), ())), precision=HIGHEST, preferred_element_type=F32
    )
    leave("film_w")

    def lane_sum(row):
        return jnp.sum(row, axis=1, keepdims=True)

    land = jnp.maximum(value[19:20, 0:1], 1.0)
    token = jnp.maximum(value[19:20, 128:129], 1.0)
    place = iota((1, 5), 1)
    rms = jnp.zeros((1, 5), F32)
    for index, (square, size) in enumerate((
        (lane_sum(value[18:19, c_in:channels]), land * c_in),
        (lane_sum(value[7:8]), land * channels),
        (lane_sum(value[8:9]), land * channels),
        (lane_sum(value[9:10]), token * channels),
        (lane_sum(value[10:11]), token * channels),
    )):
        rms = jnp.where(place == index, jnp.sqrt(square / size), rms)
    o.rms[...] = rms

    def widen(name, blocks, start, stride):
        rows, width = held[name].shape
        for lane in range(width // 128):
            first = start + lane * stride
            piece = held[blocks][first : first + rows // 16].reshape(rows, 128)
            held[name][:, lane * 128 : (lane + 1) * 128] = piece.astype(F32)
        leave(name)

    rows_a, rows_b, rows_c, rows_k = 9 * channels // 16, channels // 16, 10 * c_in // 16, 9 * c_in // 16
    arrivals["sum_c"].wait()
    widen("kernel1", "sum_c", 0, rows_c)
    widen("skip_w", "sum_c", rows_k, rows_c)
    arrivals["sum_b"].wait()
    widen("mix_w", "sum_b", 0, rows_b)
    widen("out_w", "sum_b", 3 * (channels // 128) * rows_b, rows_b)
    arrivals["sum_a"].wait()
    widen("kernel2", "sum_a", 0, rows_a)
    for name in RESULTS[:4]:
        arrivals[name].wait()
        leave(name)
    for copy in leaving:
        copy.wait()


def on_device(mesh_shape, *args):
    names = INPUTS
    arg = SimpleNamespace(**dict(zip(names, args)))
    n_item, n_row = mesh_shape["item"], mesh_shape["row"]
    n_group = 2 * n_row
    _, height, span, c_in = arg.image.shape
    channels = arg.bias1.shape[-1]
    _, rows_t, cols_t, _ = arg.features.shape
    tokens = rows_t * cols_t
    low, half = height // 2, span // 2
    inputs = [
        arg.image.reshape(height, span, c_in),
        arg.land_mask.reshape(height, span) if hasattr(arg, "land_mask") else arg.land.reshape(height, span),
        arg.embedding,
        arg.gain1.reshape(1, c_in),
        arg.shift1.reshape(1, c_in),
        arg.kernel1.reshape(3, 3 * c_in, channels),
        arg.bias1.reshape(1, channels),
        arg.film_w,
        arg.film_b.reshape(1, 2 * channels),
        arg.gain2.reshape(1, channels),
        arg.shift2.reshape(1, channels),
        arg.kernel2.reshape(3, 3 * channels, channels),
        arg.bias2.reshape(1, channels),
        arg.skip_w,
        arg.skip_b.reshape(1, channels),
        arg.features.reshape(tokens, channels),
        arg.token.reshape(rows_t, cols_t),
        arg.gain3.reshape(1, channels),
        arg.shift3.reshape(1, channels),
        arg.mix_w,
        arg.mix_b.reshape(1, 2 * channels),
        arg.out_w,
        arg.out_b.reshape(1, channels),
        arg.gpool.reshape(low, half, channels),
        arg.gres.reshape(tokens, channels),
    ]
    share = 2 * n_item * n_row
    blocks_a = -(-9 * channels * channels // 2048 // share) * share
    blocks_b = -(-4 * channels * channels // 2048 // share) * share
    blocks_c = -(-10 * c_in * channels // 2048 // share) * share
    vmem = pltpu.VMEM

    def sums(blocks):
        unit = blocks // 2 // n_item
        return [
            vmem((blocks, 16, 128), BF16),
            vmem((blocks // 2, 16, 128), BF16),
            vmem((n_item - 1, unit, 16, 128), BF16),
            vmem((n_row - 1, unit // n_row, 16, 128), BF16),
        ]

    scratch = [
        pltpu.SemaphoreType.DMA((52 + 6 * n_row,)),
        pltpu.SemaphoreType.DMA((44 + 5 * n_row,)),
        vmem((n_group, -(-rows_t // 16) * 16, cols_t), BF16),
        vmem((n_group, tokens, channels), BF16),
        vmem((2, span, c_in), BF16),
        vmem((2, span, c_in), BF16),
        vmem((height, span), jnp.int32),
        vmem((height, span), jnp.int32),
        vmem((half, channels), BF16),
        vmem((half, channels), BF16),
        vmem((height + 2, span, 128), F32),
        vmem((tokens, 128), F32),
        vmem((span, c_in), F32),
        vmem((height + 4, span, c_in), F32),
        vmem((height, span, c_in), BF16),
        vmem((8, c_in), F32),
        vmem((3, 8, c_in), F32),
        vmem((n_group, 4, channels), F32),
        vmem((low, half, channels), BF16),
        vmem((channels, low * half), BF16),
        vmem((8, channels), F32),
        vmem((3, 8, channels), F32),
        vmem((8, channels, 2 * channels) if n_group < 8 or tokens < 2 * channels else (8, 16, 128), BF16),
        vmem((low + 2, half, 3 * channels), BF16),
        vmem((height + 2, span, channels), F32),
        vmem((height, span, c_in), F32),
        vmem((height + 4, span, 3 * c_in), BF16),
        vmem((height + 2, span, channels), F32),
        vmem((n_group, 2, channels), F32),
        vmem((n_group, tokens, channels), BF16),
        vmem((n_group, channels, tokens), BF16),
        vmem((tokens, channels), BF16),
        vmem((channels, tokens), BF16),
        vmem((tokens, channels), BF16),
        vmem((tokens, channels), BF16),
        vmem((channels, tokens), F32),
        vmem((16, channels), F32),
        vmem((16, channels), F32),
        vmem((n_group, 2, channels), F32),
        vmem((3, c_in, 3 * channels), BF16),
        vmem((height, channels, span), BF16),
        vmem((16, channels), F32),
        vmem((16, channels), F32),
        vmem((height + 2, span, 3 * channels), BF16),
        vmem((low, half, c_in), BF16),
        *sums(blocks_a),
        *sums(blocks_b),
        *sums(blocks_c),
        vmem((height + 2, span, 3 * channels), BF16),
        vmem((n_group, 12, channels), F32),
        vmem((8, tokens), F32),
        vmem((n_group, 8, tokens), F32),
        vmem((8, tokens), F32),
        vmem((n_group, tokens, tokens), BF16),
        vmem((channels, tokens), F32),
        vmem((channels, tokens), BF16),
        vmem((tokens, channels), BF16),
        vmem((channels, tokens), F32),
        vmem((n_group, tokens, channels), BF16),
        vmem((n_row, tokens, channels), BF16),
        vmem((n_row - 1, tokens, channels), BF16),
        vmem((2 * (n_row - 1), tokens, channels), BF16),
        vmem((tokens, channels), F32),
        pltpu.SemaphoreType.DMA((len(FETCHED) + len(RESULTS),)),
        *[vmem(inputs[INPUTS.index(name)].shape, BF16) for name in FETCHED],
    ]
    shape = jax.ShapeDtypeStruct
    mid = [
        shape((low, half, channels), BF16),
        shape((tokens, channels), BF16),
        shape((height, span, c_in), BF16),
        shape((tokens, channels), BF16),
        shape((blocks_a, 16, 128), BF16),
        shape((blocks_b, 16, 128), BF16),
        shape((blocks_c, 16, 128), BF16),
        shape((n_item, 20, channels), F32),
    ]
    scratch += [vmem(out.shape, out.dtype) for out in mid]
    in_vmem, anywhere = pl.BlockSpec(memory_space=vmem), pl.BlockSpec(memory_space=pl.ANY)
    parts = pl.pallas_call(
        functools.partial(main_kernel, n_item, n_row),
        out_shape=mid,
        in_specs=[anywhere if name in FETCHED else in_vmem for name in INPUTS],
        out_specs=[anywhere] * len(mid),
        scratch_shapes=scratch,
        compiler_params=pltpu.CompilerParams(
            collective_id=0, has_side_effects=True, vmem_limit_bytes=int(63.9 * 1024 * 1024)
        ),
    )(*inputs)
    emb = arg.embedding.shape[-1]
    final = [
        *mid[:4],
        shape((1, c_in), F32),
        shape((1, c_in), F32),
        shape((9 * c_in, channels), F32),
        shape((1, channels), F32),
        shape((emb, 2 * channels), F32),
        shape((1, 2 * channels), F32),
        shape((1, channels), F32),
        shape((1, channels), F32),
        shape((9 * channels, channels), F32),
        shape((1, channels), F32),
        shape((c_in, channels), F32),
        shape((1, channels), F32),
        shape((1, channels), F32),
        shape((1, channels), F32),
        shape((channels, 3 * channels), F32),
        shape((1, 2 * channels), F32),
        shape((channels, channels), F32),
        shape((1, channels), F32),
        shape((1, 5), F32),
    ]
    outs = pl.pallas_call(
        functools.partial(last_kernel, n_item),
        out_shape=final,
        in_specs=[anywhere] * len(mid),
        out_specs=[anywhere] * 4 + [anywhere if name in LAST_BIG else in_vmem for name in LAST_OUT],
        scratch_shapes=[
            *[vmem(out.shape, out.dtype) for out in mid],
            *[vmem(final[4 + LAST_OUT.index(name)].shape, F32) for name in LAST_BIG],
            pltpu.SemaphoreType.DMA((len(mid),)),
            pltpu.SemaphoreType.DMA((4 + len(LAST_BIG),)),
        ],
        compiler_params=pltpu.CompilerParams(vmem_limit_bytes=int(63.9 * 1024 * 1024)),
    )(*parts)
    shapes = (
        (1, low, half, channels),
        (1, rows_t, cols_t, channels),
        (1, height, span, c_in),
        (1, rows_t, cols_t, channels),
        (c_in,),
        (c_in,),
        (3, 3, c_in, channels),
        (channels,),
        (emb, 2 * channels),
        (2 * channels,),
        (channels,),
        (channels,),
        (3, 3, channels, channels),
        (channels,),
        (c_in, channels),
        (channels,),
        (channels,),
        (channels,),
        (channels, 3 * channels),
        (2 * channels,),
        (channels, channels),
        (channels,),
        (5,),
    )
    return tuple(out.reshape(to) for out, to in zip(outs, shapes))


def solution(mesh):
    tiled = P("item", "row", "pair", None)
    mask = P("item", "row", "pair")
    in_specs = [P()] * len(INPUTS)
    for name in ("image", "features", "gpool", "gres"):
        in_specs[INPUTS.index(name)] = tiled
    for name in ("land", "token"):
        in_specs[INPUTS.index(name)] = mask
    in_specs[INPUTS.index("embedding")] = P("item", None)
    return jax.shard_map(
        functools.partial(on_device, dict(mesh.shape)),
        mesh=mesh,
        in_specs=tuple(in_specs),
        out_specs=(tiled,) * 4 + (P(),) * 19,
        check_vma=False,
    )
```

```python
import functools
import math
from types import SimpleNamespace
from typing import Any, NamedTuple

import jax
import jax.numpy as jnp
from jax import lax
from jax.experimental import pallas as pl
from jax.experimental.pallas import tpu as pltpu
from jax.sharding import PartitionSpec as P

GROUPS = 32
EPS = 1e-05
MASKED = -1000000000.0
LOG2E = 1.4426950408889634
F32 = jnp.float32
BF16 = jnp.bfloat16
MESH = pl.DeviceIdType.MESH
HIGHEST = lax.Precision.HIGHEST


def mm(left, right):
    return jnp.dot(left, right, preferred_element_type=F32)


def mm_t(left, right):
    return lax.dot_general(left, right, (((1,), (1,)), ((), ())), preferred_element_type=F32)


def iota(shape, dim):
    return lax.broadcasted_iota(jnp.int32, shape, dim)


def fold(value):
    rows, width = value.shape
    return jnp.sum(value.reshape(rows // 8, 8, width), axis=0)


def total(value):
    return jnp.sum(value, axis=0, keepdims=True)


def group_total(rows, width):
    channels = rows.shape[-1]
    left = jnp.floor(iota((channels, channels), 0).astype(F32) * (1.0 / width))
    right = jnp.floor(iota((channels, channels), 1).astype(F32) * (1.0 / width))
    same = (left == right).astype(F32)
    padded = jnp.concatenate([rows, jnp.zeros((8 - rows.shape[0], channels), F32)], axis=0)
    return jnp.dot(padded, same, precision=HIGHEST, preferred_element_type=F32)


def sigmoid(value):
    return 0.5 * jnp.tanh(0.5 * value) + 0.5


class Inputs(NamedTuple):
    image: Any
    land: Any
    embedding: Any
    gain1: Any
    shift1: Any
    kernel1: Any
    bias1: Any
    film_w: Any
    film_b: Any
    gain2: Any
    shift2: Any
    kernel2: Any
    bias2: Any
    skip_w: Any
    skip_b: Any
    features: Any
    token: Any
    gain3: Any
    shift3: Any
    mix_w: Any
    mix_b: Any
    out_w: Any
    out_b: Any
    gpool: Any
    gres: Any


class Results(NamedTuple):
    pooled: Any
    result: Any
    image_grad: Any
    features_grad: Any
    sum_a: Any
    sum_b: Any
    sum_c: Any
    vectors: Any


INPUTS, RESULTS = Inputs._fields, Results._fields
FETCHED = ("kernel2", "kernel1", "film_w", "mix_w", "out_w", "skip_w", "gres")


class Links:
    def __init__(self, ref, n_item, n_row):
        self.ref = ref
        self.n_item, self.n_row, self.n_group = n_item, n_row, n_row * 2
        self.item, self.row, self.pair = (lax.axis_index(a) for a in ("item", "row", "pair"))
        self.sibling = 1 - self.pair
        self.slot = self.row * 2 + self.pair
        self.sends = 0
        self.recvs = 0
        self.pending = []

    def at(self, row=None, pair=None, item=None):
        return (
            self.item if item is None else item,
            self.row if row is None else row,
            self.pair if pair is None else pair,
        )

    def others_in_group(self):
        for step in range(1, self.n_group):
            other = lax.rem(self.slot + step, self.n_group)
            yield other, self.at(lax.div(other, 2), lax.rem(other, 2))

    def others_in_row(self):
        for step in range(1, self.n_row):
            other = lax.rem(self.row + step, self.n_row)
            yield other, self.at(row=other)

    def others_in_item(self):
        for step in range(1, self.n_item):
            other = lax.rem(self.item + step, self.n_item)
            yield other, self.at(item=other)

    def new_recv(self, count=1):
        self.recvs += count
        return self.recvs - count

    def copy(self, source, target, device, send, recv):
        return pltpu.make_async_remote_copy(
            src_ref=source,
            dst_ref=target,
            send_sem=self.ref.send_sem.at[send],
            recv_sem=self.ref.recv_sem.at[recv],
            device_id=device,
            device_id_type=MESH,
        )

    def send(self, source, target, device, recv, when=None):
        index = self.sends
        self.sends += 1

        def make():
            return self.copy(source, target, device, index, recv)

        if when is None:
            make().start()
        else:
            pl.when(when)(lambda: make().start())
        self.pending.append((make, when))

    def send_all(self, copies, size):
        index, recv = self.sends, self.new_recv()
        self.sends += 1
        for source, target, device in copies:
            self.copy(source, target, device, index, recv).start()
        whole = self.copy(size, size, self.at(pair=self.sibling), index, recv)
        self.pending.append((lambda: whole, None))
        return whole.wait_recv

    def arrived(self, target, recv, when=None):
        def wait():
            self.copy(target, target, self.at(pair=self.sibling), 0, recv).wait_recv()

        if when is None:
            wait()
        else:
            pl.when(when)(wait)

    def finish(self):
        for make, when in self.pending:
            if when is None:
                make().wait_send()
            else:
                pl.when(when)(lambda make=make: make().wait_send())

    def greet(self):
        barrier = pltpu.get_barrier_semaphore()
        devices = [d for _, d in self.others_in_group()] + [d for _, d in self.others_in_item()]
        for device in devices:
            pl.semaphore_signal(barrier, inc=1, device_id=device, device_id_type=MESH)
        return lambda: pl.semaphore_wait(barrier, len(devices))

    def share(self, slots):
        mine = slots.at[self.slot]
        copies = [(mine, mine, device) for _, device in self.others_in_group()]
        return self.send_all(copies, slots.at[pl.ds(0, self.n_group - 1)])

    def edge_rows(self, first, last, above, below):
        has_above, has_below = self.row > 0, self.row < self.n_row - 1
        from_above, from_below = self.new_recv(), self.new_recv()
        self.send(first, below, self.at(row=self.row - 1), from_below, has_above)
        self.send(last, above, self.at(row=self.row + 1), from_above, has_below)

        def wait():
            self.arrived(above, from_above, has_above)
            self.arrived(below, from_below, has_below)

            @pl.when(self.row == 0)
            def _():
                above[...] = jnp.zeros(above.shape, above.dtype)

            @pl.when(self.row == self.n_row - 1)
            def _():
                below[...] = jnp.zeros(below.shape, below.dtype)

        return wait

    def edge_columns(self, column, columns):
        has_above, has_below = self.row > 0, self.row < self.n_row - 1
        base = self.new_recv(3)
        self.send(column, columns.at[2], self.at(self.row - 1, self.sibling), base + 2, has_above)
        self.send(column, columns.at[0], self.at(self.row + 1, self.sibling), base, has_below)
        self.send(column, columns.at[1], self.at(pair=self.sibling), base + 1)

        def wait():
            self.arrived(columns.at[1], base + 1)
            self.arrived(columns.at[0], base, has_above)
            self.arrived(columns.at[2], base + 2, has_below)

            @pl.when(self.row == 0)
            def _():
                columns[0] = jnp.zeros(columns.shape[1:], columns.dtype)

            @pl.when(self.row == self.n_row - 1)
            def _():
                columns[2] = jnp.zeros(columns.shape[1:], columns.dtype)

        return wait

    def all_sum(self, part, recv1, recv2, recv3, out):
        half = part.shape[0] // 2
        quarter = half // self.n_item
        chunk = quarter // self.n_row
        mine = self.pair * half
        item_at = mine + self.item * quarter
        own = item_at + self.row * chunk

        def span(ref, start, size):
            return ref.at[pl.ds(start, size)]

        def grow(start, size, arrivals):
            value = part[pl.ds(start, size)].astype(F32)
            for arrival in arrivals:
                value = value + arrival.astype(F32)
            return value.astype(BF16)

        def stage2():
            wait1()
            part[pl.ds(mine, half)] = grow(mine, half, [recv1[...]])
            copies = [
                (span(part, mine + other * quarter, quarter), recv2.at[step], device)
                for step, (other, device) in enumerate(self.others_in_item())
            ]
            wait2 = self.send_all(copies, recv2)

            def stage3():
                wait2()
                part[pl.ds(item_at, quarter)] = grow(item_at, quarter, [recv2[k] for k in range(self.n_item - 1)])
                copies = [
                    (span(part, item_at + other * chunk, chunk), recv3.at[step], device)
                    for step, (other, device) in enumerate(self.others_in_row())
                ]
                wait3 = self.send_all(copies, recv3)

                def stage4():
                    wait3()
                    out[pl.ds(own, chunk)] = grow(own, chunk, [recv3[k] for k in range(self.n_row - 1)])
                    source = span(out, own, chunk)
                    copies = [(source, source, device) for _, device in self.others_in_row()]
                    wait4 = self.send_all(copies, span(out, 0, (self.n_row - 1) * chunk))

                    def stage5():
                        wait4()
                        source = span(out, item_at, quarter)
                        copies = [(source, source, device) for _, device in self.others_in_item()]
                        wait5 = self.send_all(copies, span(out, 0, (self.n_item - 1) * quarter))

                        def stage6():
                            wait5()
                            source = span(out, mine, half)
                            return self.send_all([(source, source, self.at(pair=self.sibling))], span(out, 0, half))

                        return stage6

                    return stage5

                return stage4

            return stage3

        wait1 = self.send_all([(span(part, self.sibling * half, half), recv1, self.at(pair=self.sibling))], recv1)
        return stage2


def norm_terms(sums, squares, count, width):
    size = jnp.maximum(count, 1.0) * width
    grouped = group_total(jnp.concatenate([sums, squares], axis=0), width)
    mean = grouped[0:1] / size
    return mean, lax.rsqrt(grouped[1:2] / size - mean * mean + EPS), size


def arrival_order(n_row):
    orders = []
    for row in range(n_row):
        found = [row]
        for step in range(1, n_row):
            found += [r for r in (row - step, row + step) if 0 <= r < n_row]
        orders.append(found)
    return orders


def pick(values, index):
    chosen = jnp.int32(0)
    for k, value in enumerate(values):
        chosen = chosen + jnp.where(index == k, jnp.int32(value), jnp.int32(0))
    return chosen


def main_kernel(n_item, n_row, *refs):
    names = INPUTS + RESULTS + SCRATCH
    ref = SimpleNamespace(**dict(zip(names, refs)))
    fetches = []
    for index, name in enumerate(FETCHED):
        fetches.append(pltpu.make_async_copy(getattr(ref, name), getattr(ref, name + "_in"), ref.local_sem.at[index]))
        fetches[-1].start()
        setattr(ref, name, getattr(ref, name + "_in"))
    stores = []
    homes = {name: getattr(ref, name) for name in RESULTS}
    for name in RESULTS:
        setattr(ref, name, getattr(ref, name + "_out"))

    def store(name):
        copy = pltpu.make_async_copy(getattr(ref, name), homes[name], ref.local_sem.at[len(FETCHED) + len(stores)])
        copy.start()
        stores.append(copy)

    link = Links(ref, n_item, n_row)
    height, span, c_in = ref.image.shape
    channels = ref.bias1.shape[-1]
    half = span // 2
    tokens = ref.features.shape[0]
    n_group = link.n_group
    low = height // 2
    side = link.pair.astype(F32)
    width1, width2 = c_in // GROUPS, channels // GROUPS
    slot, item, row, pair, sibling = link.slot, link.item, link.row, link.pair, link.sibling
    has_up = (row > 0).astype(F32)
    has_down = (row < n_row - 1).astype(F32)
    factor = channels ** (-0.5)
    zero1 = jnp.zeros((8, c_in), F32)
    zero2 = jnp.zeros((8, channels), F32)
    rows_t, cols_t = ref.token.shape
    now = SimpleNamespace()

    def lanes(mask, width):
        if width <= mask.shape[1]:
            return mask[:, 0:width]
        return jnp.concatenate([mask] * (width // mask.shape[1]), axis=1)

    def wide_mask(y):
        return lanes(ref.mask[y], channels)

    def inner(y):
        return ((y > 0) & (y < height + 1)).astype(F32)

    def exists(y):
        return jnp.where(y == 0, has_up, jnp.where(y == height + 1, has_down, 1.0))

    def slot_sum(slots):
        value = slots[0]
        for other in range(1, n_group):
            value = value + slots[other]
        return value

    def land_line(line):
        place = iota((span, span), 0)
        place = jnp.where(place < half, 2 * place, 2 * (place - half) + 1)
        line = jnp.broadcast_to(line.astype(F32), (span, span))
        line = jnp.where(place == iota((span, span), 1), line, 0.0).astype(BF16)
        return mm(line, jnp.ones((span, 128), BF16))

    def token_mask(flags):
        chosen = iota((rows_t, cols_t, rows_t), 0) == iota((rows_t, cols_t, rows_t), 2)
        lines = mm(chosen.reshape(tokens, rows_t).astype(BF16), flags)
        keep = (iota((rows_t, cols_t, cols_t), 1) == iota((rows_t, cols_t, cols_t), 2)).reshape(tokens, cols_t)
        return mm(jnp.where(keep, lines, 0.0).astype(BF16), jnp.ones((cols_t, 128), BF16))

    def split_row(y, line):
        ref.line[...] = line.astype(F32)
        even = ref.line[pl.ds(0, half, stride=2), :]
        odd = ref.line[pl.ds(1, half, stride=2), :]
        ref.normed1[y, 0:half] = even
        ref.normed1[y, half:span] = odd
        return even, odd

    def write_shifted(target, y, even, odd, edge, size):
        top = iota((half, size), 0) == 0
        end = iota((half, size), 0) == half - 1
        before = jnp.where(top, edge * side, pltpu.roll(odd, 1, 0)).astype(BF16)
        after = jnp.where(end, edge * (1.0 - side), pltpu.roll(even, half - 1, 0)).astype(BF16)
        even, odd = even.astype(BF16), odd.astype(BF16)
        target[y, 0:half, 0:size] = before
        target[y, 0:half, size : 2 * size] = even
        target[y, 0:half, 2 * size : 3 * size] = odd
        target[y, half:span, 0:size] = even
        target[y, half:span, size : 2 * size] = odd
        target[y, half:span, 2 * size : 3 * size] = after

    def set_edges(target, edges):
        size = channels

        def body(y, carry):
            edge = edges[pl.ds(y, 1), :]

            @pl.when(pair == 1)
            def _():
                tile = target[y, 0:16, 0:size].astype(F32)
                target[y, 0:16, 0:size] = jnp.where(iota((16, size), 0) == 0, edge, tile).astype(BF16)

            @pl.when(pair == 0)
            def _():
                tile = target[y, span - 16 : span, 2 * size : 3 * size].astype(F32)
                tile = jnp.where(iota((16, size), 0) == 15, edge, tile).astype(BF16)
                target[y, span - 16 : span, 2 * size : 3 * size] = tile

            return carry

        lax.fori_loop(0, height + 2, body, 0)

    def put(target, start, stride, value):
        count = value.shape[0] // 16
        for lane in range(value.shape[1] // 128):
            piece = value[:, lane * 128 : (lane + 1) * 128].astype(BF16)
            target[pl.ds(start + lane * stride, count)] = piece.reshape(count, 16, 128)

    rows_a, rows_b, rows_c = 9 * channels // 16, channels // 16, 10 * c_in // 16

    def local():
        def land_row(y, carry):
            ref.mask[y + 1] = land_line(ref.land[pl.ds(y, 1), :])
            return carry

        lax.fori_loop(0, height, land_row, 0)
        ref.token_mask[...] = token_mask(ref.token[...].astype(F32).astype(BF16))

        def image_row(y, carry):
            sums, squares, count = carry
            even, odd = split_row(y + 2, ref.image[y])
            value = jnp.concatenate([even, odd], axis=0)
            ref.image_low[y] = value.astype(BF16)
            ref.column1[pl.ds(y, 1), :] = jnp.where(side > 0.5, even[0:1], odd[half - 1 : half])
            mask = ref.mask[y + 1]
            masked = value * mask
            return sums + fold(masked), squares + fold(masked * value), count + fold(mask)

        sums, squares, count = lax.fori_loop(0, height, image_row, (zero1, zero1, jnp.zeros((8, 128), F32)))
        raw = ref.features[...].astype(F32)
        tmask = ref.token_mask[...]
        masked = raw * lanes(tmask, channels)
        ref.stats1[slot, 0:1, 0:c_in] = total(sums)
        ref.stats1[slot, 0:1, c_in:channels] = total(squares)
        ref.stats1[slot, 1:2, :] = total(masked)
        ref.stats1[slot, 2:3, :] = total(masked * raw)
        ref.stats1[slot, 3:4, 0:128] = total(count)
        ref.stats1[slot, 3:4, 128:256] = total(tmask)
        now.gpre_sum = zero2
        for i in range(low):
            value = (ref.gpool[i].astype(F32) * 0.25 * math.sqrt(0.5)).astype(BF16)
            ref.gpre[i] = value
            ref.gpre_t[:, i * half : (i + 1) * half] = value.T
            wide = value.astype(F32)
            ref.column2[i : i + 1, :] = jnp.where(side > 0.5, wide[0:1], wide[half - 1 : half])
            now.gpre_sum = now.gpre_sum + fold(wide)
        ref.flags[slot, 0:rows_t] = ref.token[...].astype(F32).astype(BF16)
        ref.raw[slot] = ref.features[...]

    class Gather:
        def __init__(self, slots):
            self.slots, self.base = slots, link.new_recv(n_group)
            self.pass_on(row, True, row < n_row - 1, row > 0)
            self.across(row)

        def send(self, block, device, when=None):
            index = block * 2 + pair
            link.send(self.slots.at[index], self.slots.at[index], device, self.base + index, when)

        def pass_on(self, block, there, up, down):
            if up is not None:
                self.send(block, link.at(row=row + 1), there & up)
            if down is not None:
                self.send(block, link.at(row=row - 1), there & down)

        def across(self, block, there=None):
            self.send(block, link.at(pair=sibling), there)

        def step(self, step):
            below, above = row - step, row + step
            for block, there in ((below, below >= 0), (above, above < n_row)):
                index = block * 2 + pair
                link.arrived(self.slots.at[index], self.base + index, there)
            if step < n_row - 1:
                self.pass_on(below, below >= 0, row < n_row - 1, None)
                self.pass_on(above, above < n_row, None, row > 0)
            self.across(below, below >= 0)
            self.across(above, above < n_row)

        def from_sibling(self, index):
            link.arrived(self.slots.at[index], self.base + index)

    def first_sends():
        now.wait_stats1 = link.share(ref.stats1)
        now.wait_pool_columns = link.edge_columns(ref.column2, ref.columns2)
        now.wait_image_columns = link.edge_columns(ref.column1, ref.columns1)
        now.wait_pool_rows = link.edge_rows(ref.gpool.at[0], ref.gpool.at[low - 1], ref.pool_up, ref.pool_down)
        now.wait_image_rows = link.edge_rows(
            ref.image.at[pl.ds(0, 2)], ref.image.at[pl.ds(height - 2, 2)], ref.image_up, ref.image_down
        )
        now.wait_land_rows = link.edge_rows(ref.land, ref.land, ref.land_up, ref.land_down)
        now.wait_token = link.share(ref.flags)
        now.raw = Gather(ref.raw)

    def raw_step(step):
        now.raw.step(step)

    def gres_first():
        ref.gres_all[slot] = ref.gres[...]
        now.gres = Gather(ref.gres_all)

    def gres_step(step):
        now.gres.step(step)

    coarse = ref.probs if n_group >= 8 and tokens >= 2 * channels else ref.coarse

    def coarse_taps():
        for copy in fetches:
            copy.wait()
        upper, lower = {0: (2,), 1: (1, 2)}, {0: (0, 1), 1: (0,)}
        for u in range(2):
            for line, row_taps in enumerate((upper[u], lower[u])):
                tall = []
                for b in range(3):
                    at = slice(b * channels, (b + 1) * channels)
                    tall.append(sum(ref.kernel2[a, at, :].astype(F32) for a in row_taps))
                for v in range(2):
                    for place_x, column_taps in enumerate((upper[v], lower[v])):
                        tile = sum(tall[b] for b in column_taps)
                        at = slice(place_x * channels, (place_x + 1) * channels)
                        coarse[u * 4 + v * 2 + line, 0:channels, at] = tile.astype(BF16)

    def back2():
        now.wait_pool_rows()
        now.wait_pool_columns()
        first_row = iota((half, channels), 0) == 0
        last_row = iota((half, channels), 0) == half - 1
        for i in range(low + 2):
            if i == 0:
                value, edge = ref.pool_up[...], ref.columns2[0, low - 1 : low, :]
            elif i == low + 1:
                value, edge = ref.pool_down[...], ref.columns2[2, 0:1, :]
            else:
                value, edge = ref.gpre[i - 1], ref.columns2[1, i - 1 : i, :]
            if i in (0, low + 1):
                value = (value.astype(F32) * 0.25 * math.sqrt(0.5)).astype(BF16)
            wide = value.astype(F32)
            left = jnp.where(first_row, edge * side, pltpu.roll(wide, 1, 0))
            right = jnp.where(last_row, edge * (1.0 - side), pltpu.roll(wide, half - 1, 0))
            ref.padded_g[i, :, 0:channels] = left.astype(BF16)
            ref.padded_g[i, :, channels : 2 * channels] = value
            ref.padded_g[i, :, 2 * channels : 3 * channels] = right.astype(BF16)
        for u in range(2):
            for v in range(2):
                value = 0.0
                for line in range(2):
                    rows = ref.padded_g[line : line + low + 1, :, v * channels : (v + 2) * channels]
                    taps = coarse[u * 4 + v * 2 + line, 0:channels, 0 : 2 * channels]
                    value = value + mm_t(rows.reshape((low + 1) * half, 2 * channels), taps)
                for i in range(low + 1):
                    ref.grad2[2 * i + 1 - u, v * half : (v + 1) * half, :] = value[i * half : (i + 1) * half]

    def norm1():
        now.wait_stats1()
        stats = slot_sum(ref.stats1)
        now.stats1 = stats
        now.count_land = lanes(stats[3:4, 0:128], channels)
        now.count_token = lanes(stats[3:4, 128:256], channels)
        mean, inv, now.size1 = norm_terms(
            stats[0:1, 0:c_in], stats[0:1, c_in:channels], now.count_land[:, 0:c_in], width1
        )
        now.inv1 = inv
        now.mean3, now.inv3, now.size3 = norm_terms(stats[1:2], stats[2:3], now.count_token, width2)
        gain, shift = ref.gain1[...], ref.shift1[...]

        def act1(value):
            normed = (value - mean) * inv
            affine = normed * gain + shift
            return normed, affine, sigmoid(affine)

        def edge_act(rows):
            _, affine, gate = act1(rows)
            return affine * gate

        now.wait_image_columns()
        ref.columns1[0] = edge_act(ref.columns1[0]) * has_up
        ref.columns1[1] = edge_act(ref.columns1[1])
        ref.columns1[2] = edge_act(ref.columns1[2]) * has_down

        def edge_row(y, edge, there):
            _, affine, gate = act1(ref.normed1[y])
            act = affine * gate * there
            write_shifted(ref.padded1, y, act[0:half], act[half:span], edge, c_in)

        def act1_row(y, carry):
            normed, affine, gate = act1(ref.normed1[y + 2])
            act = affine * gate
            ref.normed1[y + 2] = normed
            ref.slope1[y] = gate * (1.0 + affine * (1.0 - gate))
            write_shifted(ref.padded1, y + 2, act[0:half], act[half:span], ref.columns1[1, pl.ds(y, 1), :], c_in)
            return carry

        lax.fori_loop(0, height, act1_row, 0)
        now.wait_image_rows()
        for k in range(2):
            split_row(k, ref.image_up[k])
            split_row(height + 2 + k, ref.image_down[k])
        for k in range(2):
            edge_row(k, ref.columns1[0, height - 2 + k : height - 1 + k, :], has_up)
            edge_row(height + 2 + k, ref.columns1[2, k : k + 1, :], has_down)

    def conv1():
        now.wait_land_rows()
        ref.mask[0] = land_line(ref.land_up[height - 1 : height, :])
        ref.mask[height + 1] = land_line(ref.land_down[0:1, :])

        def conv1_row(y, carry):
            sums, squares = carry
            value = mm(ref.padded1[y], ref.kernel1[0])
            value = value + mm(ref.padded1[y + 1], ref.kernel1[1])
            value = value + mm(ref.padded1[y + 2], ref.kernel1[2])
            value = value + ref.bias1[...]
            ref.hidden[y] = value
            masked = value * wide_mask(y)
            keep = inner(y)
            return sums + fold(masked) * keep, squares + fold(masked * value) * keep

        sums, squares = lax.fori_loop(0, height + 2, conv1_row, (zero2, zero2))
        ref.stats2[slot, 0:1, :] = total(sums)
        ref.stats2[slot, 1:2, :] = total(squares)
        now.wait_stats2 = link.share(ref.stats2)

    def normalize(index):
        scale = now.inv3 * ref.gain3[...]
        value = ((ref.raw[index].astype(F32) - now.mean3) * scale + ref.shift3[...]).astype(BF16)
        ref.tokens[index] = value
        ref.tokens_t[index] = value.T

    def weights(k):
        return ref.mix_w[:, k * channels : (k + 1) * channels]

    def queries():
        now.wait_token()
        normalize(slot)
        mine = ref.tokens[slot]
        now.alive = (now.count_token > 0.0).astype(F32) * factor
        query_of(slot, ref.query)
        ref.query_t[...] = (mm_t(weights(1), ref.query[...]) * (factor * LOG2E)).astype(BF16)
        ref.mix_vo[...] = mm(weights(2), ref.out_w[...]).astype(BF16)
        ref.key[...] = (mm(mine, weights(1)) * (factor * LOG2E)).astype(BF16)
        ref.value[...] = mm(mine, ref.mix_vo[...]).astype(BF16)
        ref.grad_att[...] = mm_t(ref.gres[...], ref.out_w[...]).astype(BF16)
        ref.grad_low_t[...] = mm_t(ref.mix_vo[...], ref.gres[...]).astype(BF16)
        ref.mixed_t[...] = jnp.zeros((channels, tokens), F32)
        ref.top[...] = jnp.full((8, tokens), -3e38, F32)
        ref.norm[...] = jnp.zeros((8, tokens), F32)

    def query_of(index, target):
        target[...] = (mm(ref.tokens[index], weights(0)) + ref.mix_b[:, 0:channels]).astype(BF16)

    arrivals = arrival_order(n_row)

    def blocks_at(position):
        block = pick([order[position] for order in arrivals], row)
        return block * 2 + pair, block * 2 + sibling

    def attend(position):
        blocks = blocks_at(position)
        if position > 0:
            normalize(blocks[0])
        now.raw.from_sibling(blocks[1])
        normalize(blocks[1])
        old = new = ref.top[0:1]
        scores = []
        for index in blocks:
            mask = lanes(token_mask(ref.flags[index, 0:rows_t]), tokens)
            score = mm(ref.tokens[index], ref.query_t[...])
            score = jnp.where(mask > 0.5, score, MASKED * LOG2E)
            best = jnp.max(score.reshape(tokens // 8, 8, tokens), axis=0)
            new = jnp.maximum(new, jnp.max(best, axis=0, keepdims=True))
            scores.append(score)
        shrink = jnp.exp2(old - new)
        norm = ref.norm[0:1] * shrink
        mixed = ref.mixed_t[...] * shrink
        for index, score in zip(blocks, scores):
            probs = jnp.exp2(score - new)
            low_probs = probs.astype(BF16)
            ref.probs[index] = low_probs
            ref.tops[index, 0:1] = new
            norm = norm + total(fold(probs))
            mixed = mixed + mm(ref.tokens_t[index], low_probs)
        ref.top[0:1] = new
        ref.norm[0:1] = norm
        ref.mixed_t[...] = mixed

    def film():
        lines = jnp.broadcast_to(ref.embedding[...], (8, ref.embedding.shape[-1]))
        value = mm(lines, ref.film_w[...])[0:1] + ref.film_b[...]
        now.film_scale = 1.0 + value[:, 0:channels]
        now.slope_m = ref.gain2[...] * now.film_scale
        now.shift_m = ref.shift2[...] * now.film_scale + value[:, channels:]

    def mid():
        now.wait_stats2()
        stats = slot_sum(ref.stats2)
        mean, inv, now.size2 = norm_terms(stats[0:1], stats[1:2], now.count_land, width2)
        now.inv2 = inv
        slope_m, shift_m = now.slope_m, now.shift_m

        def mid_row(y, carry):
            grad_sum, grad_dot = carry
            normed = (ref.hidden[y] - mean) * inv
            affine = normed * slope_m + shift_m
            gate = sigmoid(affine)
            act = affine * gate
            grad = ref.grad2[y] * (gate * (1.0 + affine * (1.0 - gate)))
            ref.hidden[y] = normed
            ref.grad2[y] = grad
            act = act * exists(y)
            write_shifted(ref.padded2, y, act[0:half], act[half:span], 0.0, channels)
            ref.column3[pl.ds(y, 1), :] = jnp.where(side > 0.5, act[0:1], act[span - 1 : span])
            keep = inner(y)
            return grad_sum + fold(grad) * keep, grad_dot + fold(grad * normed) * keep

        grad_sum, grad_dot = lax.fori_loop(0, height + 2, mid_row, (zero2, zero2))
        ref.stats3[slot, 0:1, :] = total(grad_sum)
        ref.stats3[slot, 1:2, :] = total(grad_dot)
        now.wait_stats3 = link.share(ref.stats3)
        now.wait_act_column = link.send_all([(ref.column3, ref.edge3, link.at(pair=sibling))], ref.edge3)

    def kernel2_grad():
        now.wait_act_column()
        set_edges(ref.padded2, ref.edge3)

        def box_row(i, carry):
            for a in range(3):
                value = 0.0
                for dy in range(2):
                    for side_x in range(2):
                        line = ref.padded2[2 * i + a + dy, side_x * half : (side_x + 1) * half, :]
                        value = value + line.astype(F32)
                at = a * (low // 2) + lax.div(i, 2)
                ref.padded3[at, pl.ds(lax.rem(i, 2) * half, half), :] = value.astype(BF16)
            return carry

        lax.fori_loop(0, low, box_row, 0)

        def body(a, carry):
            boxes = ref.padded3[pl.ds(a * (low // 2), low // 2)].reshape(low * half, 3 * channels)
            value = mm(ref.gpre_t[...], boxes).T
            put(ref.part_a, a * (rows_a // 3), rows_a, value)
            return carry

        lax.fori_loop(0, 3, body, 0)
        now.sum_a = link.all_sum(ref.part_a, ref.recv1_a, ref.recv2_a, ref.recv3_a, ref.sum_a)

    def hidden():
        now.wait_stats3()
        stats = slot_sum(ref.stats3)
        now.grad_sum2, now.grad_dot2 = stats[0:1], stats[1:2]
        slope_m, inv = now.slope_m, now.inv2
        grouped = group_total(jnp.concatenate([now.grad_sum2 * slope_m, now.grad_dot2 * slope_m], axis=0), width2)
        first, second = grouped[0:1] / now.size2, grouped[1:2] / now.size2

        def hidden_row(y, carry):
            normed = ref.hidden[y]
            grad = ref.grad2[y] * slope_m - wide_mask(y) * (first + normed * second)
            grad = (grad * (inv * exists(y))).astype(BF16)
            wide = grad.astype(F32)
            write_shifted(ref.padded3, y, wide[0:half], wide[half:span], 0.0, channels)
            ref.column4[pl.ds(y, 1), :] = jnp.where(side > 0.5, wide[0:1], wide[span - 1 : span])

            @pl.when((y > 0) & (y < height + 1))
            def _():
                ref.grad_hidden_t[y - 1] = grad.T

            return carry + fold(wide) * inner(y)

        now.bias1_sum = lax.fori_loop(0, height + 2, hidden_row, zero2)
        now.wait_hidden_column = link.send_all([(ref.column4, ref.edge4, link.at(pair=sibling))], ref.edge4)

    def image_boxes():
        for i in range(low):
            value = 0.0
            for dy in range(2):
                for side_x in range(2):
                    at = slice(side_x * half, (side_x + 1) * half)
                    value = value + ref.image_low[2 * i + dy, at, :].astype(F32)
            ref.image_box[i] = value.astype(BF16)
        value = mm(ref.gpre_t[...], ref.image_box[...].reshape(low * half, c_in)).T
        put(ref.part_c, 9 * c_in // 16, rows_c, value)

    def kernel1_grad():
        def body(a, carry):
            value = 0.0
            for y in range(height):
                value = value + mm(ref.grad_hidden_t[y], ref.padded1[a + y + 1])
            put(ref.part_c, a * (3 * c_in // 16), rows_c, value.T)
            return carry

        lax.fori_loop(0, 3, body, 0)
        now.sum_c = link.all_sum(ref.part_c, ref.recv1_c, ref.recv2_c, ref.recv3_c, ref.sum_c)

    def attended():
        norm = 1.0 / ref.norm[0:1]
        mixed_t = ref.mixed_t[...] * norm
        ref.mixed_t[...] = mixed_t
        ref.query_stats[slot, 0:1] = ref.top[0:1]
        ref.query_stats[slot, 1:2] = norm
        ref.query_stats[slot, 2:3] = total(ref.grad_low_t[...].astype(F32) * mixed_t)
        ref.grad_query_t[...] = jnp.zeros((channels, tokens), F32)
        ref.key_grad[...] = jnp.zeros((tokens, channels), F32)
        ref.value_grad[...] = jnp.zeros((tokens, channels), F32)
        now.wait_query_stats = link.share(ref.query_stats)

    def query_back(first, last):
        top, norm, delta = (ref.query_stats[slot, k : k + 1] for k in range(3))

        def body(step, carry):
            value = ref.grad_query_t[...]
            for index in (2 * step, 2 * step + 1):
                probs = ref.probs[index].astype(F32) * (jnp.exp2(ref.tops[index, 0:1] - top) * norm)
                grad = mm(ref.tokens[index], ref.grad_low_t[...])
                grad = (probs * (grad - delta)).astype(BF16)
                value = value + mm(ref.tokens_t[index], grad)
            ref.grad_query_t[...] = value
            return carry

        lax.fori_loop(first, last, body, 0)

    def key_back(position):
        blocks = blocks_at(position)
        if position == 0:
            now.wait_query_stats()
        now.gres.from_sibling(blocks[1])
        key_sum, value_sum = ref.key_grad[...], ref.value_grad[...]
        for lane, index in enumerate(blocks):
            top, norm, delta = (ref.query_stats[index, k : k + 1] for k in range(3))
            query = ref.query_all.at[lane]
            query_of(index, query)
            scores = mm_t(ref.key[...], query[...])
            scores = jnp.where(lanes(ref.token_mask[...], tokens) > 0.5, scores, MASKED * LOG2E)
            probs = jnp.exp2(scores - top) * norm
            grad = mm_t(ref.value[...], ref.gres_all[index])
            grad = (probs * (grad - delta)).astype(BF16)
            key_sum = key_sum + mm(grad, query[...])
            value_sum = value_sum + mm(probs.astype(BF16), ref.gres_all[index])
        ref.key_grad[...] = key_sum
        ref.value_grad[...] = value_sum

    def mix_grads():
        grad_query_t = (ref.grad_query_t[...] * now.alive[0:1, 0:1]).astype(BF16)
        now.grad_query = mm(grad_query_t.T, weights(1)).astype(BF16)
        mixed_t = ref.mixed_t[...]
        now.attended = (mm(mixed_t.T.astype(BF16), weights(2)) + ref.mix_b[:, channels:]).astype(BF16)
        put(ref.part_b, 6 * rows_b, rows_b, mm(now.attended.T, ref.gres[...]))
        put(ref.part_b, 4 * rows_b, rows_b, mm(mixed_t.astype(BF16), ref.grad_att[...]))
        put(ref.part_b, 0, rows_b, mm(ref.tokens_t[slot], now.grad_query))
        put(ref.part_b, 2 * rows_b, rows_b, mm(grad_query_t, ref.query[...]))
        now.sum_b = link.all_sum(ref.part_b, ref.recv1_b, ref.recv2_b, ref.recv3_b, ref.sum_b)

    def result():
        update = mm(now.attended, ref.out_w[...]) + ref.out_b[...]
        raw = ref.features[...].astype(F32)
        value = raw + update
        ref.result[...] = value.astype(BF16)
        store("result")
        tmask2 = lanes(ref.token_mask[...], channels)
        now.update_sum = fold(update * update * tmask2)
        now.result_sum = fold(value * value * tmask2)

    def own_grad():
        value = mm_t(now.grad_query, weights(0))
        value = value + mm_t((ref.key_grad[...] * now.alive).astype(BF16), weights(1))
        value = value + mm_t(ref.value_grad[...].astype(BF16), ref.mix_vo[...])
        ref.grad_own[...] = value
        now.grad_sum3 = total(fold(value))
        now.grad_dot3 = total(fold(value * ref.features[...].astype(F32)))

    def conv2():
        def conv2_rows(i, carry):
            branch_sum, stream_sum = carry
            pooled = 0.0
            for u in range(2):
                y = 2 * i + u
                branch = mm(ref.padded2[y], ref.kernel2[0])
                branch = branch + mm(ref.padded2[y + 1], ref.kernel2[1])
                branch = branch + mm(ref.padded2[y + 2], ref.kernel2[2])
                branch = branch + ref.bias2[...]
                stream = (branch + mm(ref.image_low[y], ref.skip_w[...]) + ref.skip_b[...]) * math.sqrt(0.5)
                mask = wide_mask(y + 1)
                branch_sum = branch_sum + fold(branch * branch * mask)
                stream_sum = stream_sum + fold(stream * stream * mask)
                pooled = pooled + stream[0:half] + stream[half:span]
            ref.pooled[i] = (pooled * 0.25).astype(BF16)
            return branch_sum, stream_sum

        now.branch_sum, now.stream_sum = lax.fori_loop(0, low, conv2_rows, (zero2, zero2))
        store("pooled")

    def taps1():
        for a in range(3):
            for b in range(3):
                at = slice((2 - b) * channels, (3 - b) * channels)
                ref.kernel1_t[2 - a, :, at] = ref.kernel1[a, b * c_in : (b + 1) * c_in, :]

    def back1():
        now.wait_hidden_column()
        set_edges(ref.padded3, ref.edge4)

        def back1_row(y, carry):
            grad_sum, grad_dot = carry
            value = mm_t(ref.padded3[y], ref.kernel1_t[0])
            value = value + mm_t(ref.padded3[y + 1], ref.kernel1_t[1])
            value = value + mm_t(ref.padded3[y + 2], ref.kernel1_t[2])
            value = value * ref.slope1[y]
            ref.slope1[y] = value
            return grad_sum + fold(value), grad_dot + fold(value * ref.normed1[y + 2])

        now.grad_sum1, now.grad_dot1 = lax.fori_loop(0, height, back1_row, (zero1, zero1))

    def last_share():
        ref.stats4[slot, 11:12, 0:c_in] = total(now.grad_dot1)
        ref.stats4[slot, 11:12, c_in:channels] = total(now.grad_sum1)
        for index, value in enumerate((
            now.grad_sum3,
            (now.grad_dot3 - now.mean3 * now.grad_sum3) * now.inv3,
            total(now.bias1_sum),
            4.0 * total(now.gpre_sum),
            total(fold(ref.gres[...].astype(F32))),
            total(fold(now.grad_query.astype(F32))),
            total(fold(ref.grad_att[...].astype(F32))),
            total(now.branch_sum),
            total(now.stream_sum),
            total(now.update_sum),
            total(now.result_sum),
        )):
            ref.stats4[slot, index : index + 1, :] = value
        now.wait_stats4 = link.share(ref.stats4)

    def last_sums():
        now.wait_stats4()
        stats = slot_sum(ref.stats4)
        now.stats4 = stats
        ref.vectors[item, 0:12, :] = stats
        ref.vectors[item, 12:13, :] = now.grad_dot2 * now.film_scale
        ref.vectors[item, 13:14, :] = now.grad_sum2 * now.film_scale
        ref.vectors[item, 14:15, :] = now.grad_dot2 * ref.gain2[...] + now.grad_sum2 * ref.shift2[...]
        ref.vectors[item, 15:16, :] = now.grad_sum2
        ref.vectors[item, 16:17, :] = ref.embedding[:, 0:channels].astype(F32)
        ref.vectors[item, 17:18, :] = ref.embedding[:, channels : 2 * channels].astype(F32)
        ref.vectors[item, 18:19, :] = now.stats1[0:1]
        ref.vectors[item, 19:20, :] = now.stats1[3:4]
        mine = ref.vectors.at[item]
        now.wait_vectors = link.send_all(
            [(mine, mine, device) for _, device in link.others_in_item()], ref.vectors.at[pl.ds(0, n_item - 1)]
        )

    def image_grad():
        stats = now.stats4
        gain, inv = ref.gain1[...], now.inv1
        grad_sum, grad_dot = stats[11:12, c_in:channels], stats[11:12, 0:c_in]
        grouped = group_total(jnp.concatenate([grad_sum * gain, grad_dot * gain], axis=0), width1)
        first, second = grouped[0:1] / now.size1, grouped[1:2] / now.size1

        def body(i, carry):
            skip = mm_t(ref.gpre[i], ref.skip_w[...])
            skip = jnp.concatenate([skip, skip], axis=0)
            for u in range(2):
                y = 2 * i + u
                value = ref.slope1[y] * gain - ref.mask[y + 1] * (first + ref.normed1[y + 2] * second)
                value = value * inv + skip
                ref.line[pl.ds(0, half, stride=2), :] = value[0:half]
                ref.line[pl.ds(1, half, stride=2), :] = value[half:span]
                ref.image_grad[y] = ref.line[...].astype(BF16)
            return carry

        lax.fori_loop(0, low, body, 0)
        store("image_grad")

    def features_grad():
        stats, gain = now.stats4, ref.gain3[...]
        grouped = group_total(jnp.concatenate([stats[0:1] * gain, stats[1:2] * gain], axis=0), width2)
        first, second = grouped[0:1] / now.size3, grouped[1:2] / now.size3
        normed = (ref.features[...].astype(F32) - now.mean3) * now.inv3
        value = ref.grad_own[...] * gain - lanes(ref.token_mask[...], channels) * (first + normed * second)
        ref.features_grad[...] = (ref.gres[...].astype(F32) + value * now.inv3).astype(BF16)
        store("features_grad")

    def step(name):
        stage = getattr(now, name)
        setattr(now, name, stage() if stage is not None else None)

    def step_a():
        step("sum_a")

    def step_b():
        step("sum_b")

    def step_c():
        step("sum_c")

    met = link.greet()
    local()
    met()
    first_sends()
    coarse_taps()
    back2()
    norm1()
    conv1()
    raw_step(1)
    gres_first()
    queries()
    film()
    attend(0)
    mid()
    for k in range(2, min(3, n_row)): raw_step(k)
    kernel2_grad()
    taps1()
    step_a()
    hidden()
    gres_step(1)
    attend(1)
    image_boxes()
    kernel1_grad()
    for k in range(3, n_row): raw_step(k)
    for k in range(2, min(3, n_row)): attend(k)
    step_c()
    for k in range(3, n_row): attend(k)
    step_a()
    attended()
    for k in range(2, min(3, n_row)): gres_step(k)
    query_back(0, n_row)
    mix_grads()
    step_a()
    step_c()
    key_back(0)
    step_b()
    key_back(1)
    for k in range(3, n_row): gres_step(k)
    for k in range(2, min(3, n_row)): key_back(k)
    step_a()
    step_b()
    for k in range(3, n_row): key_back(k)
    step_c()
    result()
    conv2()
    step_b()
    step_c()
    back1()
    own_grad()
    last_share()
    step_a()
    step_b()
    step_c()
    last_sums()
    step_b()
    image_grad()
    features_grad()
    steps = [now.sum_a, now.sum_c, now.sum_b, now.wait_vectors]
    while steps:
        steps = [stage() for stage in steps if stage is not None]
    for name in ("sum_a", "sum_b", "sum_c", "vectors"):
        store(name)
    link.finish()
    for copy in stores:
        copy.wait()
    assert link.sends <= ref.send_sem.shape[0] and link.recvs <= ref.recv_sem.shape[0], (link.sends, link.recvs)


class Scratch(NamedTuple):
    send_sem: Any
    recv_sem: Any
    flags: Any
    raw: Any
    image_up: Any
    image_down: Any
    land_up: Any
    land_down: Any
    pool_up: Any
    pool_down: Any
    mask: Any
    token_mask: Any
    line: Any
    normed1: Any
    image_low: Any
    column1: Any
    columns1: Any
    stats1: Any
    gpre: Any
    gpre_t: Any
    column2: Any
    columns2: Any
    coarse: Any
    padded_g: Any
    grad2: Any
    slope1: Any
    padded1: Any
    hidden: Any
    stats2: Any
    tokens: Any
    tokens_t: Any
    query: Any
    query_t: Any
    grad_att: Any
    column3: Any
    edge3: Any
    stats3: Any
    kernel1_t: Any
    grad_hidden_t: Any
    column4: Any
    edge4: Any
    padded2: Any
    image_box: Any
    part_a: Any
    recv1_a: Any
    recv2_a: Any
    recv3_a: Any
    part_b: Any
    recv1_b: Any
    recv2_b: Any
    recv3_b: Any
    part_c: Any
    recv1_c: Any
    recv2_c: Any
    recv3_c: Any
    padded3: Any
    stats4: Any
    top: Any
    tops: Any
    norm: Any
    probs: Any
    mixed_t: Any
    grad_low_t: Any
    grad_query_t: Any
    grad_own: Any
    gres_all: Any
    query_stats: Any
    mix_vo: Any
    key: Any
    value: Any
    key_grad: Any
    value_grad: Any
    query_all: Any
    local_sem: Any


SCRATCH = Scratch._fields + tuple(name + "_in" for name in FETCHED) + tuple(name + "_out" for name in RESULTS)


class LastOut(NamedTuple):
    gain1: Any
    shift1: Any
    kernel1: Any
    bias1: Any
    film_w: Any
    film_b: Any
    gain2: Any
    shift2: Any
    kernel2: Any
    bias2: Any
    skip_w: Any
    skip_b: Any
    gain3: Any
    shift3: Any
    mix_w: Any
    mix_b: Any
    out_w: Any
    out_b: Any
    rms: Any


LAST_OUT = LastOut._fields
LAST_BIG = ("kernel1", "film_w", "kernel2", "skip_w", "mix_w", "out_w")


def last_kernel(n_item, *refs):
    count = len(RESULTS)
    source = dict(zip(RESULTS, refs))
    target = dict(zip(RESULTS[:4] + LAST_OUT, refs[count:]))
    rest = refs[count + 4 + len(LAST_OUT) :]
    held = dict(zip(RESULTS + LAST_BIG, rest))
    in_sem, out_sem = rest[count + len(LAST_BIG) :]
    arrivals = {}
    for index, name in enumerate(("vectors", "sum_c", "sum_b", "sum_a") + RESULTS[:4]):
        arrivals[name] = pltpu.make_async_copy(source[name], held[name], in_sem.at[index])
        arrivals[name].start()
    leaving = []

    def leave(name):
        copy = pltpu.make_async_copy(held[name], target[name], out_sem.at[len(leaving)])
        copy.start()
        leaving.append(copy)

    o = SimpleNamespace(**target)
    channels, c_in = o.bias1.shape[-1], o.gain1.shape[-1]

    arrivals["vectors"].wait()
    vectors = held["vectors"]
    value = vectors[0]
    for item in range(1, n_item):
        value = value + vectors[item]
    o.shift3[...] = value[0:1]
    o.gain3[...] = value[1:2]
    o.bias1[...] = value[2:3]
    o.bias2[...] = value[3:4]
    o.skip_b[...] = value[3:4]
    o.out_b[...] = value[4:5]
    o.mix_b[:, 0:channels] = value[5:6]
    o.mix_b[:, channels:] = value[6:7]
    o.gain1[...] = value[11:12, 0:c_in]
    o.shift1[...] = value[11:12, c_in:channels]
    o.gain2[...] = value[12:13]
    o.shift2[...] = value[13:14]
    o.film_b[:, 0:channels] = value[14:15]
    o.film_b[:, channels:] = value[15:16]
    pad = jnp.zeros((8 - n_item, 2 * channels), F32)

    def stacked(first):
        rows = [
            jnp.concatenate([vectors[i, first : first + 1, :], vectors[i, first + 1 : first + 2, :]], axis=1)
            for i in range(n_item)
        ]
        return jnp.concatenate(rows + [pad], axis=0)

    held["film_w"][...] = lax.dot_general(
        stacked(16), stacked(14), (((0,), (0,)), ((), ())), precision=HIGHEST, preferred_element_type=F32
    )
    leave("film_w")

    def lane_sum(row):
        return jnp.sum(row, axis=1, keepdims=True)

    land = jnp.maximum(value[19:20, 0:1], 1.0)
    token = jnp.maximum(value[19:20, 128:129], 1.0)
    place = iota((1, 5), 1)
    rms = jnp.zeros((1, 5), F32)
    for index, (square, size) in enumerate((
        (lane_sum(value[18:19, c_in:channels]), land * c_in),
        (lane_sum(value[7:8]), land * channels),
        (lane_sum(value[8:9]), land * channels),
        (lane_sum(value[9:10]), token * channels),
        (lane_sum(value[10:11]), token * channels),
    )):
        rms = jnp.where(place == index, jnp.sqrt(square / size), rms)
    o.rms[...] = rms

    def widen(name, blocks, start, stride):
        rows, width = held[name].shape
        for lane in range(width // 128):
            first = start + lane * stride
            piece = held[blocks][first : first + rows // 16].reshape(rows, 128)
            held[name][:, lane * 128 : (lane + 1) * 128] = piece.astype(F32)
        leave(name)

    rows_a, rows_b, rows_c, rows_k = 9 * channels // 16, channels // 16, 10 * c_in // 16, 9 * c_in // 16
    arrivals["sum_c"].wait()
    widen("kernel1", "sum_c", 0, rows_c)
    widen("skip_w", "sum_c", rows_k, rows_c)
    arrivals["sum_b"].wait()
    widen("mix_w", "sum_b", 0, rows_b)
    widen("out_w", "sum_b", 3 * (channels // 128) * rows_b, rows_b)
    arrivals["sum_a"].wait()
    widen("kernel2", "sum_a", 0, rows_a)
    for name in RESULTS[:4]:
        arrivals[name].wait()
        leave(name)
    for copy in leaving:
        copy.wait()


def on_device(mesh_shape, *args):
    names = INPUTS
    arg = SimpleNamespace(**dict(zip(names, args)))
    n_item, n_row = mesh_shape["item"], mesh_shape["row"]
    n_group = 2 * n_row
    _, height, span, c_in = arg.image.shape
    channels = arg.bias1.shape[-1]
    _, rows_t, cols_t, _ = arg.features.shape
    tokens = rows_t * cols_t
    low, half = height // 2, span // 2
    inputs = [
        arg.image.reshape(height, span, c_in),
        arg.land_mask.reshape(height, span) if hasattr(arg, "land_mask") else arg.land.reshape(height, span),
        arg.embedding,
        arg.gain1.reshape(1, c_in),
        arg.shift1.reshape(1, c_in),
        arg.kernel1.reshape(3, 3 * c_in, channels),
        arg.bias1.reshape(1, channels),
        arg.film_w,
        arg.film_b.reshape(1, 2 * channels),
        arg.gain2.reshape(1, channels),
        arg.shift2.reshape(1, channels),
        arg.kernel2.reshape(3, 3 * channels, channels),
        arg.bias2.reshape(1, channels),
        arg.skip_w,
        arg.skip_b.reshape(1, channels),
        arg.features.reshape(tokens, channels),
        arg.token.reshape(rows_t, cols_t),
        arg.gain3.reshape(1, channels),
        arg.shift3.reshape(1, channels),
        arg.mix_w,
        arg.mix_b.reshape(1, 2 * channels),
        arg.out_w,
        arg.out_b.reshape(1, channels),
        arg.gpool.reshape(low, half, channels),
        arg.gres.reshape(tokens, channels),
    ]
    share = 2 * n_item * n_row
    blocks_a = -(-9 * channels * channels // 2048 // share) * share
    blocks_b = -(-4 * channels * channels // 2048 // share) * share
    blocks_c = -(-10 * c_in * channels // 2048 // share) * share
    vmem = pltpu.VMEM

    def sums(blocks):
        unit = blocks // 2 // n_item
        return [
            vmem((blocks, 16, 128), BF16),
            vmem((blocks // 2, 16, 128), BF16),
            vmem((n_item - 1, unit, 16, 128), BF16),
            vmem((n_row - 1, unit // n_row, 16, 128), BF16),
        ]

    scratch = [
        pltpu.SemaphoreType.DMA((8 * n_row + 33,)),
        pltpu.SemaphoreType.DMA((4 * n_row + 39,)),
        vmem((n_group, -(-rows_t // 16) * 16, cols_t), BF16),
        vmem((n_group, tokens, channels), BF16),
        vmem((2, span, c_in), BF16),
        vmem((2, span, c_in), BF16),
        vmem((height, span), jnp.int32),
        vmem((height, span), jnp.int32),
        vmem((half, channels), BF16),
        vmem((half, channels), BF16),
        vmem((height + 2, span, 128), F32),
        vmem((tokens, 128), F32),
        vmem((span, c_in), F32),
        vmem((height + 4, span, c_in), F32),
        vmem((height, span, c_in), BF16),
        vmem((8, c_in), F32),
        vmem((3, 8, c_in), F32),
        vmem((n_group, 4, channels), F32),
        vmem((low, half, channels), BF16),
        vmem((channels, low * half), BF16),
        vmem((8, channels), F32),
        vmem((3, 8, channels), F32),
        vmem((8, channels, 2 * channels) if n_group < 8 or tokens < 2 * channels else (8, 16, 128), BF16),
        vmem((low + 2, half, 3 * channels), BF16),
        vmem((height + 2, span, channels), F32),
        vmem((height, span, c_in), F32),
        vmem((height + 4, span, 3 * c_in), BF16),
        vmem((height + 2, span, channels), F32),
        vmem((n_group, 2, channels), F32),
        vmem((n_group, tokens, channels), BF16),
        vmem((n_group, channels, tokens), BF16),
        vmem((tokens, channels), BF16),
        vmem((channels, tokens), BF16),
        vmem((tokens, channels), BF16),
        vmem((16, channels), F32),
        vmem((16, channels), F32),
        vmem((n_group, 2, channels), F32),
        vmem((3, c_in, 3 * channels), BF16),
        vmem((height, channels, span), BF16),
        vmem((16, channels), F32),
        vmem((16, channels), F32),
        vmem((height + 2, span, 3 * channels), BF16),
        vmem((low, half, c_in), BF16),
        *sums(blocks_a),
        *sums(blocks_b),
        *sums(blocks_c),
        vmem((height + 2, span, 3 * channels), BF16),
        vmem((n_group, 12, channels), F32),
        vmem((8, tokens), F32),
        vmem((n_group, 8, tokens), F32),
        vmem((8, tokens), F32),
        vmem((n_group, tokens, tokens), BF16),
        vmem((channels, tokens), F32),
        vmem((channels, tokens), BF16),
        vmem((channels, tokens), F32),
        vmem((tokens, channels), F32),
        vmem((n_group, tokens, channels), BF16),
        vmem((n_group, 4, tokens), F32),
        vmem((channels, channels), BF16),
        vmem((tokens, channels), BF16),
        vmem((tokens, channels), BF16),
        vmem((tokens, channels), F32),
        vmem((tokens, channels), F32),
        vmem((2, tokens, channels), BF16),
        pltpu.SemaphoreType.DMA((len(FETCHED) + len(RESULTS),)),
        *[vmem(inputs[INPUTS.index(name)].shape, BF16) for name in FETCHED],
    ]
    shape = jax.ShapeDtypeStruct
    mid = [
        shape((low, half, channels), BF16),
        shape((tokens, channels), BF16),
        shape((height, span, c_in), BF16),
        shape((tokens, channels), BF16),
        shape((blocks_a, 16, 128), BF16),
        shape((blocks_b, 16, 128), BF16),
        shape((blocks_c, 16, 128), BF16),
        shape((n_item, 20, channels), F32),
    ]
    scratch += [vmem(out.shape, out.dtype) for out in mid]
    in_vmem, anywhere = pl.BlockSpec(memory_space=vmem), pl.BlockSpec(memory_space=pl.ANY)
    parts = pl.pallas_call(
        functools.partial(main_kernel, n_item, n_row),
        out_shape=mid,
        in_specs=[anywhere if name in FETCHED else in_vmem for name in INPUTS],
        out_specs=[anywhere] * len(mid),
        scratch_shapes=scratch,
        compiler_params=pltpu.CompilerParams(
            collective_id=0, has_side_effects=True, vmem_limit_bytes=int(63.9 * 1024 * 1024)
        ),
    )(*inputs)
    emb = arg.embedding.shape[-1]
    final = [
        *mid[:4],
        shape((1, c_in), F32),
        shape((1, c_in), F32),
        shape((9 * c_in, channels), F32),
        shape((1, channels), F32),
        shape((emb, 2 * channels), F32),
        shape((1, 2 * channels), F32),
        shape((1, channels), F32),
        shape((1, channels), F32),
        shape((9 * channels, channels), F32),
        shape((1, channels), F32),
        shape((c_in, channels), F32),
        shape((1, channels), F32),
        shape((1, channels), F32),
        shape((1, channels), F32),
        shape((channels, 3 * channels), F32),
        shape((1, 2 * channels), F32),
        shape((channels, channels), F32),
        shape((1, channels), F32),
        shape((1, 5), F32),
    ]
    outs = pl.pallas_call(
        functools.partial(last_kernel, n_item),
        out_shape=final,
        in_specs=[anywhere] * len(mid),
        out_specs=[anywhere] * 4 + [anywhere if name in LAST_BIG else in_vmem for name in LAST_OUT],
        scratch_shapes=[
            *[vmem(out.shape, out.dtype) for out in mid],
            *[vmem(final[4 + LAST_OUT.index(name)].shape, F32) for name in LAST_BIG],
            pltpu.SemaphoreType.DMA((len(mid),)),
            pltpu.SemaphoreType.DMA((4 + len(LAST_BIG),)),
        ],
        compiler_params=pltpu.CompilerParams(vmem_limit_bytes=int(63.9 * 1024 * 1024)),
    )(*parts)
    shapes = (
        (1, low, half, channels),
        (1, rows_t, cols_t, channels),
        (1, height, span, c_in),
        (1, rows_t, cols_t, channels),
        (c_in,),
        (c_in,),
        (3, 3, c_in, channels),
        (channels,),
        (emb, 2 * channels),
        (2 * channels,),
        (channels,),
        (channels,),
        (3, 3, channels, channels),
        (channels,),
        (c_in, channels),
        (channels,),
        (channels,),
        (channels,),
        (channels, 3 * channels),
        (2 * channels,),
        (channels, channels),
        (channels,),
        (5,),
    )
    return tuple(out.reshape(to) for out, to in zip(outs, shapes))


def solution(mesh):
    tiled = P("item", "row", "pair", None)
    mask = P("item", "row", "pair")
    in_specs = [P()] * len(INPUTS)
    for name in ("image", "features", "gpool", "gres"):
        in_specs[INPUTS.index(name)] = tiled
    for name in ("land", "token"):
        in_specs[INPUTS.index(name)] = mask
    in_specs[INPUTS.index("embedding")] = P("item", None)
    return jax.shard_map(
        functools.partial(on_device, dict(mesh.shape)),
        mesh=mesh,
        in_specs=tuple(in_specs),
        out_specs=(tiled,) * 4 + (P(),) * 19,
        check_vma=False,
    )
```

```python
import functools
import math
from types import SimpleNamespace
from typing import Any, NamedTuple

import jax
import jax.numpy as jnp
from jax import lax
from jax.experimental import pallas as pl
from jax.experimental.pallas import tpu as pltpu
from jax.sharding import PartitionSpec as P

GROUPS = 32
EPS = 1e-05
MASKED = -1000000000.0
LOG2E = 1.4426950408889634
F32 = jnp.float32
BF16 = jnp.bfloat16
MESH = pl.DeviceIdType.MESH
HIGHEST = lax.Precision.HIGHEST


def mm(left, right):
    return jnp.dot(left, right, preferred_element_type=F32)


def mm_t(left, right):
    return lax.dot_general(left, right, (((1,), (1,)), ((), ())), preferred_element_type=F32)


def iota(shape, dim):
    return lax.broadcasted_iota(jnp.int32, shape, dim)


def fold(value):
    rows, width = value.shape
    return jnp.sum(value.reshape(rows // 8, 8, width), axis=0)


def total(value):
    return jnp.sum(value, axis=0, keepdims=True)


def group_total(rows, width):
    channels = rows.shape[-1]
    left = jnp.floor(iota((channels, channels), 0).astype(F32) * (1.0 / width))
    right = jnp.floor(iota((channels, channels), 1).astype(F32) * (1.0 / width))
    same = (left == right).astype(F32)
    padded = jnp.concatenate([rows, jnp.zeros((8 - rows.shape[0], channels), F32)], axis=0)
    return jnp.dot(padded, same, precision=HIGHEST, preferred_element_type=F32)


def sigmoid(value):
    return 0.5 * jnp.tanh(0.5 * value) + 0.5


class Inputs(NamedTuple):
    image: Any
    land: Any
    embedding: Any
    gain1: Any
    shift1: Any
    kernel1: Any
    bias1: Any
    film_w: Any
    film_b: Any
    gain2: Any
    shift2: Any
    kernel2: Any
    bias2: Any
    skip_w: Any
    skip_b: Any
    features: Any
    token: Any
    gain3: Any
    shift3: Any
    mix_w: Any
    mix_b: Any
    out_w: Any
    out_b: Any
    gpool: Any
    gres: Any


class Results(NamedTuple):
    pooled: Any
    result: Any
    image_grad: Any
    features_grad: Any
    sum_a: Any
    sum_b: Any
    sum_c: Any
    vectors: Any


INPUTS, RESULTS = Inputs._fields, Results._fields
FETCHED = ("kernel2", "kernel1", "film_w", "mix_w", "out_w", "skip_w", "gres")


class Links:
    def __init__(self, ref, n_item, n_row):
        self.ref = ref
        self.n_item, self.n_row, self.n_group = n_item, n_row, n_row * 2
        self.item, self.row, self.pair = (lax.axis_index(a) for a in ("item", "row", "pair"))
        self.sibling = 1 - self.pair
        self.slot = self.row * 2 + self.pair
        self.sends = 0
        self.recvs = 0
        self.pending = []

    def at(self, row=None, pair=None, item=None):
        return (
            self.item if item is None else item,
            self.row if row is None else row,
            self.pair if pair is None else pair,
        )

    def others_in_group(self):
        for step in range(1, self.n_group):
            other = lax.rem(self.slot + step, self.n_group)
            yield other, self.at(lax.div(other, 2), lax.rem(other, 2))

    def others_in_row(self):
        for step in range(1, self.n_row):
            other = lax.rem(self.row + step, self.n_row)
            yield other, self.at(row=other)

    def others_in_item(self):
        for step in range(1, self.n_item):
            other = lax.rem(self.item + step, self.n_item)
            yield other, self.at(item=other)

    def new_recv(self, count=1):
        self.recvs += count
        return self.recvs - count

    def copy(self, source, target, device, send, recv):
        return pltpu.make_async_remote_copy(
            src_ref=source,
            dst_ref=target,
            send_sem=self.ref.send_sem.at[send],
            recv_sem=self.ref.recv_sem.at[recv],
            device_id=device,
            device_id_type=MESH,
        )

    def send(self, source, target, device, recv, when=None):
        index = self.sends
        self.sends += 1

        def make():
            return self.copy(source, target, device, index, recv)

        if when is None:
            make().start()
        else:
            pl.when(when)(lambda: make().start())
        self.pending.append((make, when))

    def send_all(self, copies, size):
        index, recv = self.sends, self.new_recv()
        self.sends += 1
        for source, target, device in copies:
            self.copy(source, target, device, index, recv).start()
        whole = self.copy(size, size, self.at(pair=self.sibling), index, recv)
        self.pending.append((lambda: whole, None))
        return whole.wait_recv

    def arrived(self, target, recv, when=None):
        def wait():
            self.copy(target, target, self.at(pair=self.sibling), 0, recv).wait_recv()

        if when is None:
            wait()
        else:
            pl.when(when)(wait)

    def finish(self):
        for make, when in self.pending:
            if when is None:
                make().wait_send()
            else:
                pl.when(when)(lambda make=make: make().wait_send())

    def greet(self):
        barrier = pltpu.get_barrier_semaphore()
        devices = [d for _, d in self.others_in_group()] + [d for _, d in self.others_in_item()]
        for device in devices:
            pl.semaphore_signal(barrier, inc=1, device_id=device, device_id_type=MESH)
        return lambda: pl.semaphore_wait(barrier, len(devices))

    def share(self, slots):
        mine = slots.at[self.slot]
        copies = [(mine, mine, device) for _, device in self.others_in_group()]
        return self.send_all(copies, slots.at[pl.ds(0, self.n_group - 1)])

    def edge_rows(self, first, last, above, below):
        has_above, has_below = self.row > 0, self.row < self.n_row - 1
        from_above, from_below = self.new_recv(), self.new_recv()
        self.send(first, below, self.at(row=self.row - 1), from_below, has_above)
        self.send(last, above, self.at(row=self.row + 1), from_above, has_below)

        def wait():
            self.arrived(above, from_above, has_above)
            self.arrived(below, from_below, has_below)

            @pl.when(self.row == 0)
            def _():
                above[...] = jnp.zeros(above.shape, above.dtype)

            @pl.when(self.row == self.n_row - 1)
            def _():
                below[...] = jnp.zeros(below.shape, below.dtype)

        return wait

    def edge_columns(self, column, columns):
        has_above, has_below = self.row > 0, self.row < self.n_row - 1
        base = self.new_recv(3)
        self.send(column, columns.at[2], self.at(self.row - 1, self.sibling), base + 2, has_above)
        self.send(column, columns.at[0], self.at(self.row + 1, self.sibling), base, has_below)
        self.send(column, columns.at[1], self.at(pair=self.sibling), base + 1)

        def wait():
            self.arrived(columns.at[1], base + 1)
            self.arrived(columns.at[0], base, has_above)
            self.arrived(columns.at[2], base + 2, has_below)

            @pl.when(self.row == 0)
            def _():
                columns[0] = jnp.zeros(columns.shape[1:], columns.dtype)

            @pl.when(self.row == self.n_row - 1)
            def _():
                columns[2] = jnp.zeros(columns.shape[1:], columns.dtype)

        return wait

    def all_sum(self, part, recv1, recv2, recv3, out):
        half = part.shape[0] // 2
        quarter = half // self.n_item
        chunk = quarter // self.n_row
        mine = self.pair * half
        item_at = mine + self.item * quarter
        own = item_at + self.row * chunk

        def span(ref, start, size):
            return ref.at[pl.ds(start, size)]

        def grow(start, size, arrivals):
            value = part[pl.ds(start, size)].astype(F32)
            for arrival in arrivals:
                value = value + arrival.astype(F32)
            return value.astype(BF16)

        def stage2():
            wait1()
            part[pl.ds(mine, half)] = grow(mine, half, [recv1[...]])
            copies = [
                (span(part, mine + other * quarter, quarter), recv2.at[step], device)
                for step, (other, device) in enumerate(self.others_in_item())
            ]
            wait2 = self.send_all(copies, recv2)

            def stage3():
                wait2()
                part[pl.ds(item_at, quarter)] = grow(item_at, quarter, [recv2[k] for k in range(self.n_item - 1)])
                copies = [
                    (span(part, item_at + other * chunk, chunk), recv3.at[step], device)
                    for step, (other, device) in enumerate(self.others_in_row())
                ]
                wait3 = self.send_all(copies, recv3)

                def stage4():
                    wait3()
                    out[pl.ds(own, chunk)] = grow(own, chunk, [recv3[k] for k in range(self.n_row - 1)])
                    source = span(out, own, chunk)
                    copies = [(source, source, device) for _, device in self.others_in_row()]
                    wait4 = self.send_all(copies, span(out, 0, (self.n_row - 1) * chunk))

                    def stage5():
                        wait4()
                        source = span(out, item_at, quarter)
                        copies = [(source, source, device) for _, device in self.others_in_item()]
                        wait5 = self.send_all(copies, span(out, 0, (self.n_item - 1) * quarter))

                        def stage6():
                            wait5()
                            source = span(out, mine, half)
                            return self.send_all([(source, source, self.at(pair=self.sibling))], span(out, 0, half))

                        return stage6

                    return stage5

                return stage4

            return stage3

        wait1 = self.send_all([(span(part, self.sibling * half, half), recv1, self.at(pair=self.sibling))], recv1)
        return stage2


def norm_terms(sums, squares, count, width):
    size = jnp.maximum(count, 1.0) * width
    grouped = group_total(jnp.concatenate([sums, squares], axis=0), width)
    mean = grouped[0:1] / size
    return mean, lax.rsqrt(grouped[1:2] / size - mean * mean + EPS), size


def arrival_order(n_row):
    orders = []
    for row in range(n_row):
        found = [row]
        for step in range(1, n_row):
            found += [r for r in (row - step, row + step) if 0 <= r < n_row]
        orders.append(found)
    return orders


def pick(values, index):
    chosen = jnp.int32(0)
    for k, value in enumerate(values):
        chosen = chosen + jnp.where(index == k, jnp.int32(value), jnp.int32(0))
    return chosen


def main_kernel(n_item, n_row, *refs):
    names = INPUTS + RESULTS + SCRATCH
    ref = SimpleNamespace(**dict(zip(names, refs)))
    fetches = []
    for index, name in enumerate(FETCHED):
        fetches.append(pltpu.make_async_copy(getattr(ref, name), getattr(ref, name + "_in"), ref.local_sem.at[index]))
        fetches[-1].start()
        setattr(ref, name, getattr(ref, name + "_in"))
    stores = []
    homes = {name: getattr(ref, name) for name in RESULTS}
    for name in RESULTS:
        setattr(ref, name, getattr(ref, name + "_out"))

    def store(name):
        copy = pltpu.make_async_copy(getattr(ref, name), homes[name], ref.local_sem.at[len(FETCHED) + len(stores)])
        copy.start()
        stores.append(copy)

    link = Links(ref, n_item, n_row)
    height, span, c_in = ref.image.shape
    channels = ref.bias1.shape[-1]
    half = span // 2
    tokens = ref.features.shape[0]
    n_group = link.n_group
    low = height // 2
    side = link.pair.astype(F32)
    width1, width2 = c_in // GROUPS, channels // GROUPS
    slot, item, row, pair, sibling = link.slot, link.item, link.row, link.pair, link.sibling
    has_up = (row > 0).astype(F32)
    has_down = (row < n_row - 1).astype(F32)
    factor = channels ** (-0.5)
    zero1 = jnp.zeros((8, c_in), F32)
    zero2 = jnp.zeros((8, channels), F32)
    rows_t, cols_t = ref.token.shape
    now = SimpleNamespace()

    def lanes(mask, width):
        if width <= mask.shape[1]:
            return mask[:, 0:width]
        return jnp.concatenate([mask] * (width // mask.shape[1]), axis=1)

    def wide_mask(y):
        return lanes(ref.mask[y], channels)

    def inner(y):
        return ((y > 0) & (y < height + 1)).astype(F32)

    def exists(y):
        return jnp.where(y == 0, has_up, jnp.where(y == height + 1, has_down, 1.0))

    def slot_sum(slots):
        value = slots[0]
        for other in range(1, n_group):
            value = value + slots[other]
        return value

    def land_line(line):
        place = iota((span, span), 0)
        place = jnp.where(place < half, 2 * place, 2 * (place - half) + 1)
        line = jnp.broadcast_to(line.astype(F32), (span, span))
        line = jnp.where(place == iota((span, span), 1), line, 0.0).astype(BF16)
        return mm(line, jnp.ones((span, 128), BF16))

    def token_mask(flags):
        chosen = iota((rows_t, cols_t, rows_t), 0) == iota((rows_t, cols_t, rows_t), 2)
        lines = mm(chosen.reshape(tokens, rows_t).astype(BF16), flags)
        keep = (iota((rows_t, cols_t, cols_t), 1) == iota((rows_t, cols_t, cols_t), 2)).reshape(tokens, cols_t)
        return mm(jnp.where(keep, lines, 0.0).astype(BF16), jnp.ones((cols_t, 128), BF16))

    def split_row(y, line):
        ref.line[...] = line.astype(F32)
        even = ref.line[pl.ds(0, half, stride=2), :]
        odd = ref.line[pl.ds(1, half, stride=2), :]
        ref.normed1[y, 0:half] = even
        ref.normed1[y, half:span] = odd
        return even, odd

    def write_shifted(target, y, even, odd, edge, size):
        top = iota((half, size), 0) == 0
        end = iota((half, size), 0) == half - 1
        before = jnp.where(top, edge * side, pltpu.roll(odd, 1, 0)).astype(BF16)
        after = jnp.where(end, edge * (1.0 - side), pltpu.roll(even, half - 1, 0)).astype(BF16)
        even, odd = even.astype(BF16), odd.astype(BF16)
        target[y, 0:half, 0:size] = before
        target[y, 0:half, size : 2 * size] = even
        target[y, 0:half, 2 * size : 3 * size] = odd
        target[y, half:span, 0:size] = even
        target[y, half:span, size : 2 * size] = odd
        target[y, half:span, 2 * size : 3 * size] = after

    def set_edges(target, edges):
        size = channels

        def body(y, carry):
            edge = edges[pl.ds(y, 1), :]

            @pl.when(pair == 1)
            def _():
                tile = target[y, 0:16, 0:size].astype(F32)
                target[y, 0:16, 0:size] = jnp.where(iota((16, size), 0) == 0, edge, tile).astype(BF16)

            @pl.when(pair == 0)
            def _():
                tile = target[y, span - 16 : span, 2 * size : 3 * size].astype(F32)
                tile = jnp.where(iota((16, size), 0) == 15, edge, tile).astype(BF16)
                target[y, span - 16 : span, 2 * size : 3 * size] = tile

            return carry

        lax.fori_loop(0, height + 2, body, 0)

    def put(target, start, stride, value):
        count = value.shape[0] // 16
        for lane in range(value.shape[1] // 128):
            piece = value[:, lane * 128 : (lane + 1) * 128].astype(BF16)
            target[pl.ds(start + lane * stride, count)] = piece.reshape(count, 16, 128)

    rows_a, rows_b, rows_c = 9 * channels // 16, channels // 16, 10 * c_in // 16

    def local():
        def land_row(y, carry):
            ref.mask[y + 1] = land_line(ref.land[pl.ds(y, 1), :])
            return carry

        lax.fori_loop(0, height, land_row, 0)
        ref.token_mask[...] = token_mask(ref.token[...].astype(F32).astype(BF16))

        def image_row(y, carry):
            sums, squares, count = carry
            even, odd = split_row(y + 2, ref.image[y])
            value = jnp.concatenate([even, odd], axis=0)
            ref.image_low[y] = value.astype(BF16)
            ref.column1[pl.ds(y, 1), :] = jnp.where(side > 0.5, even[0:1], odd[half - 1 : half])
            mask = ref.mask[y + 1]
            masked = value * mask
            return sums + fold(masked), squares + fold(masked * value), count + fold(mask)

        sums, squares, count = lax.fori_loop(0, height, image_row, (zero1, zero1, jnp.zeros((8, 128), F32)))
        raw = ref.features[...].astype(F32)
        tmask = ref.token_mask[...]
        masked = raw * lanes(tmask, channels)
        ref.stats1[slot, 0:1, 0:c_in] = total(sums)
        ref.stats1[slot, 0:1, c_in:channels] = total(squares)
        ref.stats1[slot, 1:2, :] = total(masked)
        ref.stats1[slot, 2:3, :] = total(masked * raw)
        ref.stats1[slot, 3:4, 0:128] = total(count)
        ref.stats1[slot, 3:4, 128:256] = total(tmask)
        now.gpre_sum = zero2
        for i in range(low):
            value = (ref.gpool[i].astype(F32) * 0.25 * math.sqrt(0.5)).astype(BF16)
            ref.gpre[i] = value
            ref.gpre_t[:, i * half : (i + 1) * half] = value.T
            wide = value.astype(F32)
            ref.column2[i : i + 1, :] = jnp.where(side > 0.5, wide[0:1], wide[half - 1 : half])
            now.gpre_sum = now.gpre_sum + fold(wide)
        ref.flags[slot, 0:rows_t] = ref.token[...].astype(F32).astype(BF16)
        ref.raw[slot] = ref.features[...]

    class Gather:
        def __init__(self, slots):
            self.slots, self.base = slots, link.new_recv(n_group)
            self.pass_on(row, True, row < n_row - 1, row > 0)
            self.across(row)

        def send(self, block, device, when=None):
            index = block * 2 + pair
            link.send(self.slots.at[index], self.slots.at[index], device, self.base + index, when)

        def pass_on(self, block, there, up, down):
            if up is not None:
                self.send(block, link.at(row=row + 1), there & up)
            if down is not None:
                self.send(block, link.at(row=row - 1), there & down)

        def across(self, block, there=None):
            self.send(block, link.at(pair=sibling), there)

        def step(self, step):
            below, above = row - step, row + step
            for block, there in ((below, below >= 0), (above, above < n_row)):
                index = block * 2 + pair
                link.arrived(self.slots.at[index], self.base + index, there)
            if step < n_row - 1:
                self.pass_on(below, below >= 0, row < n_row - 1, None)
                self.pass_on(above, above < n_row, None, row > 0)
            self.across(below, below >= 0)
            self.across(above, above < n_row)

        def from_sibling(self, index):
            link.arrived(self.slots.at[index], self.base + index)

    def first_sends():
        now.wait_stats1 = link.share(ref.stats1)
        now.wait_pool_columns = link.edge_columns(ref.column2, ref.columns2)
        now.wait_image_columns = link.edge_columns(ref.column1, ref.columns1)
        now.wait_pool_rows = link.edge_rows(ref.gpool.at[0], ref.gpool.at[low - 1], ref.pool_up, ref.pool_down)
        now.wait_image_rows = link.edge_rows(
            ref.image.at[pl.ds(0, 2)], ref.image.at[pl.ds(height - 2, 2)], ref.image_up, ref.image_down
        )
        now.wait_land_rows = link.edge_rows(ref.land, ref.land, ref.land_up, ref.land_down)
        now.wait_token = link.share(ref.flags)
        now.raw = Gather(ref.raw)

    def raw_step(step):
        now.raw.step(step)

    def gres_first():
        ref.gres_all[slot] = ref.gres[...]
        now.gres = Gather(ref.gres_all)

    def gres_step(step):
        now.gres.step(step)

    coarse = ref.probs if n_group >= 8 and tokens >= 2 * channels else ref.coarse

    def coarse_taps():
        for copy in fetches:
            copy.wait()
        upper, lower = {0: (2,), 1: (1, 2)}, {0: (0, 1), 1: (0,)}
        for u in range(2):
            for line, row_taps in enumerate((upper[u], lower[u])):
                tall = []
                for b in range(3):
                    at = slice(b * channels, (b + 1) * channels)
                    tall.append(sum(ref.kernel2[a, at, :].astype(F32) for a in row_taps))
                for v in range(2):
                    for place_x, column_taps in enumerate((upper[v], lower[v])):
                        tile = sum(tall[b] for b in column_taps)
                        at = slice(place_x * channels, (place_x + 1) * channels)
                        coarse[u * 4 + v * 2 + line, 0:channels, at] = tile.astype(BF16)

    def back2():
        now.wait_pool_rows()
        now.wait_pool_columns()
        first_row = iota((half, channels), 0) == 0
        last_row = iota((half, channels), 0) == half - 1
        for i in range(low + 2):
            if i == 0:
                value, edge = ref.pool_up[...], ref.columns2[0, low - 1 : low, :]
            elif i == low + 1:
                value, edge = ref.pool_down[...], ref.columns2[2, 0:1, :]
            else:
                value, edge = ref.gpre[i - 1], ref.columns2[1, i - 1 : i, :]
            if i in (0, low + 1):
                value = (value.astype(F32) * 0.25 * math.sqrt(0.5)).astype(BF16)
            wide = value.astype(F32)
            left = jnp.where(first_row, edge * side, pltpu.roll(wide, 1, 0))
            right = jnp.where(last_row, edge * (1.0 - side), pltpu.roll(wide, half - 1, 0))
            ref.padded_g[i, :, 0:channels] = left.astype(BF16)
            ref.padded_g[i, :, channels : 2 * channels] = value
            ref.padded_g[i, :, 2 * channels : 3 * channels] = right.astype(BF16)
        for u in range(2):
            for v in range(2):
                value = 0.0
                for line in range(2):
                    rows = ref.padded_g[line : line + low + 1, :, v * channels : (v + 2) * channels]
                    taps = coarse[u * 4 + v * 2 + line, 0:channels, 0 : 2 * channels]
                    value = value + mm_t(rows.reshape((low + 1) * half, 2 * channels), taps)
                for i in range(low + 1):
                    ref.grad2[2 * i + 1 - u, v * half : (v + 1) * half, :] = value[i * half : (i + 1) * half]

    def norm1():
        now.wait_stats1()
        stats = slot_sum(ref.stats1)
        now.stats1 = stats
        now.count_land = lanes(stats[3:4, 0:128], channels)
        now.count_token = lanes(stats[3:4, 128:256], channels)
        mean, inv, now.size1 = norm_terms(
            stats[0:1, 0:c_in], stats[0:1, c_in:channels], now.count_land[:, 0:c_in], width1
        )
        now.inv1 = inv
        now.mean3, now.inv3, now.size3 = norm_terms(stats[1:2], stats[2:3], now.count_token, width2)
        gain, shift = ref.gain1[...], ref.shift1[...]

        def act1(value):
            normed = (value - mean) * inv
            affine = normed * gain + shift
            return normed, affine, sigmoid(affine)

        def edge_act(rows):
            _, affine, gate = act1(rows)
            return affine * gate

        now.wait_image_columns()
        ref.columns1[0] = edge_act(ref.columns1[0]) * has_up
        ref.columns1[1] = edge_act(ref.columns1[1])
        ref.columns1[2] = edge_act(ref.columns1[2]) * has_down

        def edge_row(y, edge, there):
            _, affine, gate = act1(ref.normed1[y])
            act = affine * gate * there
            write_shifted(ref.padded1, y, act[0:half], act[half:span], edge, c_in)

        def act1_row(y, carry):
            normed, affine, gate = act1(ref.normed1[y + 2])
            act = affine * gate
            ref.normed1[y + 2] = normed
            ref.slope1[y] = gate * (1.0 + affine * (1.0 - gate))
            write_shifted(ref.padded1, y + 2, act[0:half], act[half:span], ref.columns1[1, pl.ds(y, 1), :], c_in)
            return carry

        lax.fori_loop(0, height, act1_row, 0)
        now.wait_image_rows()
        for k in range(2):
            split_row(k, ref.image_up[k])
            split_row(height + 2 + k, ref.image_down[k])
        for k in range(2):
            edge_row(k, ref.columns1[0, height - 2 + k : height - 1 + k, :], has_up)
            edge_row(height + 2 + k, ref.columns1[2, k : k + 1, :], has_down)

    def conv1():
        now.wait_land_rows()
        ref.mask[0] = land_line(ref.land_up[height - 1 : height, :])
        ref.mask[height + 1] = land_line(ref.land_down[0:1, :])

        def conv1_row(y, carry):
            sums, squares = carry
            value = mm(ref.padded1[y], ref.kernel1[0])
            value = value + mm(ref.padded1[y + 1], ref.kernel1[1])
            value = value + mm(ref.padded1[y + 2], ref.kernel1[2])
            value = value + ref.bias1[...]
            ref.hidden[y] = value
            masked = value * wide_mask(y)
            keep = inner(y)
            return sums + fold(masked) * keep, squares + fold(masked * value) * keep

        sums, squares = lax.fori_loop(0, height + 2, conv1_row, (zero2, zero2))
        ref.stats2[slot, 0:1, :] = total(sums)
        ref.stats2[slot, 1:2, :] = total(squares)
        now.wait_stats2 = link.share(ref.stats2)

    def normalize(index):
        scale = now.inv3 * ref.gain3[...]
        value = ((ref.raw[index].astype(F32) - now.mean3) * scale + ref.shift3[...]).astype(BF16)
        ref.tokens[index] = value
        ref.tokens_t[index] = value.T

    def weights(k):
        return ref.mix_w[:, k * channels : (k + 1) * channels]

    def queries():
        now.wait_token()
        normalize(slot)
        mine = ref.tokens[slot]
        now.alive = (now.count_token > 0.0).astype(F32) * factor
        query_of(slot, ref.query)
        ref.query_t[...] = (mm_t(weights(1), ref.query[...]) * (factor * LOG2E)).astype(BF16)
        ref.mix_vo[...] = mm(weights(2), ref.out_w[...]).astype(BF16)
        ref.key[...] = (mm(mine, weights(1)) * (factor * LOG2E)).astype(BF16)
        ref.value[...] = mm(mine, ref.mix_vo[...]).astype(BF16)
        ref.grad_att[...] = mm_t(ref.gres[...], ref.out_w[...]).astype(BF16)
        ref.grad_low_t[...] = mm_t(ref.mix_vo[...], ref.gres[...]).astype(BF16)
        ref.mixed_t[...] = jnp.zeros((channels, tokens), F32)
        ref.top[...] = jnp.full((8, tokens), -3e38, F32)
        ref.norm[...] = jnp.zeros((8, tokens), F32)

    def query_of(index, target):
        target[...] = (mm(ref.tokens[index], weights(0)) + ref.mix_b[:, 0:channels]).astype(BF16)

    arrivals = arrival_order(n_row)

    def blocks_at(position):
        block = pick([order[position] for order in arrivals], row)
        return block * 2 + pair, block * 2 + sibling

    def attend(position):
        blocks = blocks_at(position)
        if position > 0:
            normalize(blocks[0])
        now.raw.from_sibling(blocks[1])
        normalize(blocks[1])
        old = new = ref.top[0:1]
        scores = []
        for index in blocks:
            mask = lanes(token_mask(ref.flags[index, 0:rows_t]), tokens)
            score = mm(ref.tokens[index], ref.query_t[...])
            score = jnp.where(mask > 0.5, score, MASKED * LOG2E)
            best = jnp.max(score.reshape(tokens // 8, 8, tokens), axis=0)
            new = jnp.maximum(new, jnp.max(best, axis=0, keepdims=True))
            scores.append(score)
        shrink = jnp.exp2(old - new)
        norm = ref.norm[0:1] * shrink
        mixed = ref.mixed_t[...] * shrink
        for index, score in zip(blocks, scores):
            probs = jnp.exp2(score - new)
            low_probs = probs.astype(BF16)
            ref.probs[index] = low_probs
            ref.tops[index, 0:1] = new
            norm = norm + total(fold(probs))
            mixed = mixed + mm(ref.tokens_t[index], low_probs)
        ref.top[0:1] = new
        ref.norm[0:1] = norm
        ref.mixed_t[...] = mixed

    def film():
        lines = jnp.broadcast_to(ref.embedding[...], (8, ref.embedding.shape[-1]))
        value = mm(lines, ref.film_w[...])[0:1] + ref.film_b[...]
        now.film_scale = 1.0 + value[:, 0:channels]
        now.slope_m = ref.gain2[...] * now.film_scale
        now.shift_m = ref.shift2[...] * now.film_scale + value[:, channels:]

    def mid():
        now.wait_stats2()
        stats = slot_sum(ref.stats2)
        mean, inv, now.size2 = norm_terms(stats[0:1], stats[1:2], now.count_land, width2)
        now.inv2 = inv
        slope_m, shift_m = now.slope_m, now.shift_m

        def mid_row(y, carry):
            grad_sum, grad_dot = carry
            normed = (ref.hidden[y] - mean) * inv
            affine = normed * slope_m + shift_m
            gate = sigmoid(affine)
            act = affine * gate
            grad = ref.grad2[y] * (gate * (1.0 + affine * (1.0 - gate)))
            ref.hidden[y] = normed
            ref.grad2[y] = grad
            act = act * exists(y)
            write_shifted(ref.padded2, y, act[0:half], act[half:span], 0.0, channels)
            ref.column3[pl.ds(y, 1), :] = jnp.where(side > 0.5, act[0:1], act[span - 1 : span])
            keep = inner(y)
            return grad_sum + fold(grad) * keep, grad_dot + fold(grad * normed) * keep

        grad_sum, grad_dot = lax.fori_loop(0, height + 2, mid_row, (zero2, zero2))
        ref.stats3[slot, 0:1, :] = total(grad_sum)
        ref.stats3[slot, 1:2, :] = total(grad_dot)
        now.wait_stats3 = link.share(ref.stats3)
        now.wait_act_column = link.send_all([(ref.column3, ref.edge3, link.at(pair=sibling))], ref.edge3)

    def kernel2_grad():
        now.wait_act_column()
        set_edges(ref.padded2, ref.edge3)

        def box_row(i, carry):
            for a in range(3):
                value = 0.0
                for dy in range(2):
                    for side_x in range(2):
                        line = ref.padded2[2 * i + a + dy, side_x * half : (side_x + 1) * half, :]
                        value = value + line.astype(F32)
                at = a * (low // 2) + lax.div(i, 2)
                ref.padded3[at, pl.ds(lax.rem(i, 2) * half, half), :] = value.astype(BF16)
            return carry

        lax.fori_loop(0, low, box_row, 0)

        def body(a, carry):
            boxes = ref.padded3[pl.ds(a * (low // 2), low // 2)].reshape(low * half, 3 * channels)
            value = mm(ref.gpre_t[...], boxes).T
            put(ref.part_a, a * (rows_a // 3), rows_a, value)
            return carry

        lax.fori_loop(0, 3, body, 0)
        now.sum_a = link.all_sum(ref.part_a, ref.recv1_a, ref.recv2_a, ref.recv3_a, ref.sum_a)

    def hidden():
        now.wait_stats3()
        stats = slot_sum(ref.stats3)
        now.grad_sum2, now.grad_dot2 = stats[0:1], stats[1:2]
        slope_m, inv = now.slope_m, now.inv2
        grouped = group_total(jnp.concatenate([now.grad_sum2 * slope_m, now.grad_dot2 * slope_m], axis=0), width2)
        first, second = grouped[0:1] / now.size2, grouped[1:2] / now.size2

        def hidden_row(y, carry):
            normed = ref.hidden[y]
            grad = ref.grad2[y] * slope_m - wide_mask(y) * (first + normed * second)
            grad = (grad * (inv * exists(y))).astype(BF16)
            wide = grad.astype(F32)
            write_shifted(ref.padded3, y, wide[0:half], wide[half:span], 0.0, channels)
            ref.column4[pl.ds(y, 1), :] = jnp.where(side > 0.5, wide[0:1], wide[span - 1 : span])

            @pl.when((y > 0) & (y < height + 1))
            def _():
                ref.grad_hidden_t[y - 1] = grad.T

            return carry + fold(wide) * inner(y)

        now.bias1_sum = lax.fori_loop(0, height + 2, hidden_row, zero2)
        now.wait_hidden_column = link.send_all([(ref.column4, ref.edge4, link.at(pair=sibling))], ref.edge4)

    def image_boxes():
        for i in range(low):
            value = 0.0
            for dy in range(2):
                for side_x in range(2):
                    at = slice(side_x * half, (side_x + 1) * half)
                    value = value + ref.image_low[2 * i + dy, at, :].astype(F32)
            ref.image_box[i] = value.astype(BF16)
        value = mm(ref.gpre_t[...], ref.image_box[...].reshape(low * half, c_in)).T
        put(ref.part_c, 9 * c_in // 16, rows_c, value)

    def kernel1_grad():
        def body(a, carry):
            value = 0.0
            for y in range(height):
                value = value + mm(ref.grad_hidden_t[y], ref.padded1[a + y + 1])
            put(ref.part_c, a * (3 * c_in // 16), rows_c, value.T)
            return carry

        lax.fori_loop(0, 3, body, 0)
        now.sum_c = link.all_sum(ref.part_c, ref.recv1_c, ref.recv2_c, ref.recv3_c, ref.sum_c)

    def attended():
        norm = 1.0 / ref.norm[0:1]
        mixed_t = ref.mixed_t[...] * norm
        ref.mixed_t[...] = mixed_t
        ref.query_stats[slot, 0:1] = ref.top[0:1]
        ref.query_stats[slot, 1:2] = norm
        ref.query_stats[slot, 2:3] = total(ref.grad_low_t[...].astype(F32) * mixed_t)
        ref.grad_query_t[...] = jnp.zeros((channels, tokens), F32)
        ref.key_grad[...] = jnp.zeros((tokens, channels), F32)
        ref.value_grad[...] = jnp.zeros((tokens, channels), F32)
        now.wait_query_stats = link.share(ref.query_stats)

    def query_back(first, last):
        top, norm, delta = (ref.query_stats[slot, k : k + 1] for k in range(3))

        def body(step, carry):
            value = ref.grad_query_t[...]
            for index in (2 * step, 2 * step + 1):
                probs = ref.probs[index].astype(F32) * (jnp.exp2(ref.tops[index, 0:1] - top) * norm)
                grad = mm(ref.tokens[index], ref.grad_low_t[...])
                grad = (probs * (grad - delta)).astype(BF16)
                value = value + mm(ref.tokens_t[index], grad)
            ref.grad_query_t[...] = value
            return carry

        lax.fori_loop(first, last, body, 0)

    def key_back(position):
        blocks = blocks_at(position)
        if position == 0:
            now.wait_query_stats()
        now.gres.from_sibling(blocks[1])
        key_sum, value_sum = ref.key_grad[...], ref.value_grad[...]
        for lane, index in enumerate(blocks):
            top, norm, delta = (ref.query_stats[index, k : k + 1] for k in range(3))
            query = ref.query_all.at[lane]
            query_of(index, query)
            scores = mm_t(ref.key[...], query[...])
            scores = jnp.where(lanes(ref.token_mask[...], tokens) > 0.5, scores, MASKED * LOG2E)
            probs = jnp.exp2(scores - top) * norm
            grad = mm_t(ref.value[...], ref.gres_all[index])
            grad = (probs * (grad - delta)).astype(BF16)
            key_sum = key_sum + mm(grad, query[...])
            value_sum = value_sum + mm(probs.astype(BF16), ref.gres_all[index])
        ref.key_grad[...] = key_sum
        ref.value_grad[...] = value_sum

    def mix_grads():
        grad_query_t = (ref.grad_query_t[...] * now.alive[0:1, 0:1]).astype(BF16)
        now.grad_query = mm(grad_query_t.T, weights(1)).astype(BF16)
        mixed_t = ref.mixed_t[...]
        now.attended = (mm(mixed_t.T.astype(BF16), weights(2)) + ref.mix_b[:, channels:]).astype(BF16)
        put(ref.part_b, 6 * rows_b, rows_b, mm(now.attended.T, ref.gres[...]))
        put(ref.part_b, 4 * rows_b, rows_b, mm(mixed_t.astype(BF16), ref.grad_att[...]))
        put(ref.part_b, 0, rows_b, mm(ref.tokens_t[slot], now.grad_query))
        put(ref.part_b, 2 * rows_b, rows_b, mm(grad_query_t, ref.query[...]))
        now.sum_b = link.all_sum(ref.part_b, ref.recv1_b, ref.recv2_b, ref.recv3_b, ref.sum_b)

    def result():
        update = mm(now.attended, ref.out_w[...]) + ref.out_b[...]
        raw = ref.features[...].astype(F32)
        value = raw + update
        ref.result[...] = value.astype(BF16)
        store("result")
        tmask2 = lanes(ref.token_mask[...], channels)
        now.update_sum = fold(update * update * tmask2)
        now.result_sum = fold(value * value * tmask2)

    def own_grad():
        value = mm_t(now.grad_query, weights(0))
        value = value + mm_t((ref.key_grad[...] * now.alive).astype(BF16), weights(1))
        value = value + mm_t(ref.value_grad[...].astype(BF16), ref.mix_vo[...])
        ref.grad_own[...] = value
        now.grad_sum3 = total(fold(value))
        now.grad_dot3 = total(fold(value * ref.features[...].astype(F32)))

    def conv2():
        def conv2_rows(i, carry):
            branch_sum, stream_sum = carry
            pooled = 0.0
            for u in range(2):
                y = 2 * i + u
                branch = mm(ref.padded2[y], ref.kernel2[0])
                branch = branch + mm(ref.padded2[y + 1], ref.kernel2[1])
                branch = branch + mm(ref.padded2[y + 2], ref.kernel2[2])
                branch = branch + ref.bias2[...]
                stream = (branch + mm(ref.image_low[y], ref.skip_w[...]) + ref.skip_b[...]) * math.sqrt(0.5)
                mask = wide_mask(y + 1)
                branch_sum = branch_sum + fold(branch * branch * mask)
                stream_sum = stream_sum + fold(stream * stream * mask)
                pooled = pooled + stream[0:half] + stream[half:span]
            ref.pooled[i] = (pooled * 0.25).astype(BF16)
            return branch_sum, stream_sum

        now.branch_sum, now.stream_sum = lax.fori_loop(0, low, conv2_rows, (zero2, zero2))
        store("pooled")

    def taps1():
        for a in range(3):
            for b in range(3):
                at = slice((2 - b) * channels, (3 - b) * channels)
                ref.kernel1_t[2 - a, :, at] = ref.kernel1[a, b * c_in : (b + 1) * c_in, :]

    def back1():
        now.wait_hidden_column()
        set_edges(ref.padded3, ref.edge4)

        def back1_row(y, carry):
            grad_sum, grad_dot = carry
            value = mm_t(ref.padded3[y], ref.kernel1_t[0])
            value = value + mm_t(ref.padded3[y + 1], ref.kernel1_t[1])
            value = value + mm_t(ref.padded3[y + 2], ref.kernel1_t[2])
            value = value * ref.slope1[y]
            ref.slope1[y] = value
            return grad_sum + fold(value), grad_dot + fold(value * ref.normed1[y + 2])

        now.grad_sum1, now.grad_dot1 = lax.fori_loop(0, height, back1_row, (zero1, zero1))

    def last_share():
        ref.stats4[slot, 11:12, 0:c_in] = total(now.grad_dot1)
        ref.stats4[slot, 11:12, c_in:channels] = total(now.grad_sum1)
        for index, value in enumerate((
            now.grad_sum3,
            (now.grad_dot3 - now.mean3 * now.grad_sum3) * now.inv3,
            total(now.bias1_sum),
            4.0 * total(now.gpre_sum),
            total(fold(ref.gres[...].astype(F32))),
            total(fold(now.grad_query.astype(F32))),
            total(fold(ref.grad_att[...].astype(F32))),
            total(now.branch_sum),
            total(now.stream_sum),
            total(now.update_sum),
            total(now.result_sum),
        )):
            ref.stats4[slot, index : index + 1, :] = value
        now.wait_stats4 = link.share(ref.stats4)

    def last_sums():
        now.wait_stats4()
        stats = slot_sum(ref.stats4)
        now.stats4 = stats
        ref.vectors[item, 0:12, :] = stats
        ref.vectors[item, 12:13, :] = now.grad_dot2 * now.film_scale
        ref.vectors[item, 13:14, :] = now.grad_sum2 * now.film_scale
        ref.vectors[item, 14:15, :] = now.grad_dot2 * ref.gain2[...] + now.grad_sum2 * ref.shift2[...]
        ref.vectors[item, 15:16, :] = now.grad_sum2
        ref.vectors[item, 16:17, :] = ref.embedding[:, 0:channels].astype(F32)
        ref.vectors[item, 17:18, :] = ref.embedding[:, channels : 2 * channels].astype(F32)
        ref.vectors[item, 18:19, :] = now.stats1[0:1]
        ref.vectors[item, 19:20, :] = now.stats1[3:4]
        mine = ref.vectors.at[item]
        now.wait_vectors = link.send_all(
            [(mine, mine, device) for _, device in link.others_in_item()], ref.vectors.at[pl.ds(0, n_item - 1)]
        )

    def image_grad():
        stats = now.stats4
        gain, inv = ref.gain1[...], now.inv1
        grad_sum, grad_dot = stats[11:12, c_in:channels], stats[11:12, 0:c_in]
        grouped = group_total(jnp.concatenate([grad_sum * gain, grad_dot * gain], axis=0), width1)
        first, second = grouped[0:1] / now.size1, grouped[1:2] / now.size1

        def body(i, carry):
            skip = mm_t(ref.gpre[i], ref.skip_w[...])
            skip = jnp.concatenate([skip, skip], axis=0)
            for u in range(2):
                y = 2 * i + u
                value = ref.slope1[y] * gain - ref.mask[y + 1] * (first + ref.normed1[y + 2] * second)
                value = value * inv + skip
                ref.line[pl.ds(0, half, stride=2), :] = value[0:half]
                ref.line[pl.ds(1, half, stride=2), :] = value[half:span]
                ref.image_grad[y] = ref.line[...].astype(BF16)
            return carry

        lax.fori_loop(0, low, body, 0)
        store("image_grad")

    def features_grad():
        stats, gain = now.stats4, ref.gain3[...]
        grouped = group_total(jnp.concatenate([stats[0:1] * gain, stats[1:2] * gain], axis=0), width2)
        first, second = grouped[0:1] / now.size3, grouped[1:2] / now.size3
        normed = (ref.features[...].astype(F32) - now.mean3) * now.inv3
        value = ref.grad_own[...] * gain - lanes(ref.token_mask[...], channels) * (first + normed * second)
        ref.features_grad[...] = (ref.gres[...].astype(F32) + value * now.inv3).astype(BF16)
        store("features_grad")

    def step(name):
        stage = getattr(now, name)
        setattr(now, name, stage() if stage is not None else None)

    def step_a():
        step("sum_a")

    def step_b():
        step("sum_b")

    def step_c():
        step("sum_c")

    met = link.greet()
    local()
    met()
    first_sends()
    coarse_taps()
    back2()
    norm1()
    conv1()
    raw_step(1)
    gres_first()
    queries()
    film()
    attend(0)
    mid()
    for k in range(2, min(3, n_row)): raw_step(k)
    kernel2_grad()
    taps1()
    step_a()
    attend(1)
    hidden()
    gres_step(1)
    image_boxes()
    kernel1_grad()
    for k in range(3, n_row): raw_step(k)
    for k in range(2, min(3, n_row)): attend(k)
    step_c()
    for k in range(3, n_row): attend(k)
    step_a()
    attended()
    for k in range(2, min(3, n_row)): gres_step(k)
    query_back(0, n_row)
    mix_grads()
    step_a()
    step_c()
    key_back(0)
    step_b()
    key_back(1)
    for k in range(3, n_row): gres_step(k)
    for k in range(2, min(3, n_row)): key_back(k)
    step_a()
    step_b()
    for k in range(3, n_row): key_back(k)
    step_c()
    result()
    conv2()
    step_b()
    step_c()
    back1()
    own_grad()
    last_share()
    step_a()
    step_b()
    step_c()
    last_sums()
    step_b()
    image_grad()
    features_grad()
    steps = [now.sum_a, now.sum_c, now.sum_b, now.wait_vectors]
    while steps:
        steps = [stage() for stage in steps if stage is not None]
    for name in ("sum_a", "sum_b", "sum_c", "vectors"):
        store(name)
    link.finish()
    for copy in stores:
        copy.wait()
    assert link.sends <= ref.send_sem.shape[0] and link.recvs <= ref.recv_sem.shape[0], (link.sends, link.recvs)


class Scratch(NamedTuple):
    send_sem: Any
    recv_sem: Any
    flags: Any
    raw: Any
    image_up: Any
    image_down: Any
    land_up: Any
    land_down: Any
    pool_up: Any
    pool_down: Any
    mask: Any
    token_mask: Any
    line: Any
    normed1: Any
    image_low: Any
    column1: Any
    columns1: Any
    stats1: Any
    gpre: Any
    gpre_t: Any
    column2: Any
    columns2: Any
    coarse: Any
    padded_g: Any
    grad2: Any
    slope1: Any
    padded1: Any
    hidden: Any
    stats2: Any
    tokens: Any
    tokens_t: Any
    query: Any
    query_t: Any
    grad_att: Any
    column3: Any
    edge3: Any
    stats3: Any
    kernel1_t: Any
    grad_hidden_t: Any
    column4: Any
    edge4: Any
    padded2: Any
    image_box: Any
    part_a: Any
    recv1_a: Any
    recv2_a: Any
    recv3_a: Any
    part_b: Any
    recv1_b: Any
    recv2_b: Any
    recv3_b: Any
    part_c: Any
    recv1_c: Any
    recv2_c: Any
    recv3_c: Any
    padded3: Any
    stats4: Any
    top: Any
    tops: Any
    norm: Any
    probs: Any
    mixed_t: Any
    grad_low_t: Any
    grad_query_t: Any
    grad_own: Any
    gres_all: Any
    query_stats: Any
    mix_vo: Any
    key: Any
    value: Any
    key_grad: Any
    value_grad: Any
    query_all: Any
    local_sem: Any


SCRATCH = Scratch._fields + tuple(name + "_in" for name in FETCHED) + tuple(name + "_out" for name in RESULTS)


class LastOut(NamedTuple):
    gain1: Any
    shift1: Any
    kernel1: Any
    bias1: Any
    film_w: Any
    film_b: Any
    gain2: Any
    shift2: Any
    kernel2: Any
    bias2: Any
    skip_w: Any
    skip_b: Any
    gain3: Any
    shift3: Any
    mix_w: Any
    mix_b: Any
    out_w: Any
    out_b: Any
    rms: Any


LAST_OUT = LastOut._fields
LAST_BIG = ("kernel1", "film_w", "kernel2", "skip_w", "mix_w", "out_w")


def last_kernel(n_item, *refs):
    count = len(RESULTS)
    source = dict(zip(RESULTS, refs))
    target = dict(zip(RESULTS[:4] + LAST_OUT, refs[count:]))
    rest = refs[count + 4 + len(LAST_OUT) :]
    held = dict(zip(RESULTS + LAST_BIG, rest))
    in_sem, out_sem = rest[count + len(LAST_BIG) :]
    arrivals = {}
    for index, name in enumerate(("sum_a", "sum_c", "sum_b", "vectors") + RESULTS[:4]):
        arrivals[name] = pltpu.make_async_copy(source[name], held[name], in_sem.at[index])
        arrivals[name].start()
    leaving = []

    def leave(name):
        copy = pltpu.make_async_copy(held[name], target[name], out_sem.at[len(leaving)])
        copy.start()
        leaving.append(copy)

    o = SimpleNamespace(**target)
    channels, c_in = o.bias1.shape[-1], o.gain1.shape[-1]

    def widen(name, blocks, start, stride):
        rows, width = held[name].shape
        for lane in range(width // 128):
            first = start + lane * stride
            piece = held[blocks][first : first + rows // 16].reshape(rows, 128)
            held[name][:, lane * 128 : (lane + 1) * 128] = piece.astype(F32)
        leave(name)

    rows_a, rows_b, rows_c, rows_k = 9 * channels // 16, channels // 16, 10 * c_in // 16, 9 * c_in // 16
    arrivals["sum_a"].wait()
    widen("kernel2", "sum_a", 0, rows_a)
    arrivals["sum_c"].wait()
    widen("kernel1", "sum_c", 0, rows_c)
    widen("skip_w", "sum_c", rows_k, rows_c)
    arrivals["sum_b"].wait()
    widen("mix_w", "sum_b", 0, rows_b)
    widen("out_w", "sum_b", 3 * (channels // 128) * rows_b, rows_b)
    for name in RESULTS[:4]:
        arrivals[name].wait()
        leave(name)
    arrivals["vectors"].wait()
    vectors = held["vectors"]
    value = vectors[0]
    for item in range(1, n_item):
        value = value + vectors[item]
    o.shift3[...] = value[0:1]
    o.gain3[...] = value[1:2]
    o.bias1[...] = value[2:3]
    o.bias2[...] = value[3:4]
    o.skip_b[...] = value[3:4]
    o.out_b[...] = value[4:5]
    o.mix_b[:, 0:channels] = value[5:6]
    o.mix_b[:, channels:] = value[6:7]
    o.gain1[...] = value[11:12, 0:c_in]
    o.shift1[...] = value[11:12, c_in:channels]
    o.gain2[...] = value[12:13]
    o.shift2[...] = value[13:14]
    o.film_b[:, 0:channels] = value[14:15]
    o.film_b[:, channels:] = value[15:16]
    pad = jnp.zeros((8 - n_item, 2 * channels), F32)

    def stacked(first):
        rows = [
            jnp.concatenate([vectors[i, first : first + 1, :], vectors[i, first + 1 : first + 2, :]], axis=1)
            for i in range(n_item)
        ]
        return jnp.concatenate(rows + [pad], axis=0)

    grads, parts = stacked(14), []
    for _ in range(3):
        parts.append(grads.astype(BF16).astype(F32))
        grads = grads - parts[-1]
    parts.append(jnp.zeros_like(grads))
    embedding = jnp.concatenate([stacked(16)] * 4, axis=0).astype(BF16)
    held["film_w"][...] = lax.dot_general(
        embedding, jnp.concatenate(parts, axis=0).astype(BF16), (((0,), (0,)), ((), ())), preferred_element_type=F32
    )
    leave("film_w")

    def lane_sum(row):
        return jnp.sum(row, axis=1, keepdims=True)

    land = jnp.maximum(value[19:20, 0:1], 1.0)
    token = jnp.maximum(value[19:20, 128:129], 1.0)
    place = iota((1, 5), 1)
    rms = jnp.zeros((1, 5), F32)
    for index, (square, size) in enumerate((
        (lane_sum(value[18:19, c_in:channels]), land * c_in),
        (lane_sum(value[7:8]), land * channels),
        (lane_sum(value[8:9]), land * channels),
        (lane_sum(value[9:10]), token * channels),
        (lane_sum(value[10:11]), token * channels),
    )):
        rms = jnp.where(place == index, jnp.sqrt(square / size), rms)
    o.rms[...] = rms

    for copy in leaving:
        copy.wait()


def on_device(mesh_shape, *args):
    names = INPUTS
    arg = SimpleNamespace(**dict(zip(names, args)))
    n_item, n_row = mesh_shape["item"], mesh_shape["row"]
    n_group = 2 * n_row
    _, height, span, c_in = arg.image.shape
    channels = arg.bias1.shape[-1]
    _, rows_t, cols_t, _ = arg.features.shape
    tokens = rows_t * cols_t
    low, half = height // 2, span // 2
    inputs = [
        arg.image.reshape(height, span, c_in),
        arg.land_mask.reshape(height, span) if hasattr(arg, "land_mask") else arg.land.reshape(height, span),
        arg.embedding,
        arg.gain1.reshape(1, c_in),
        arg.shift1.reshape(1, c_in),
        arg.kernel1.reshape(3, 3 * c_in, channels),
        arg.bias1.reshape(1, channels),
        arg.film_w,
        arg.film_b.reshape(1, 2 * channels),
        arg.gain2.reshape(1, channels),
        arg.shift2.reshape(1, channels),
        arg.kernel2.reshape(3, 3 * channels, channels),
        arg.bias2.reshape(1, channels),
        arg.skip_w,
        arg.skip_b.reshape(1, channels),
        arg.features.reshape(tokens, channels),
        arg.token.reshape(rows_t, cols_t),
        arg.gain3.reshape(1, channels),
        arg.shift3.reshape(1, channels),
        arg.mix_w,
        arg.mix_b.reshape(1, 2 * channels),
        arg.out_w,
        arg.out_b.reshape(1, channels),
        arg.gpool.reshape(low, half, channels),
        arg.gres.reshape(tokens, channels),
    ]
    share = 2 * n_item * n_row
    blocks_a = -(-9 * channels * channels // 2048 // share) * share
    blocks_b = -(-4 * channels * channels // 2048 // share) * share
    blocks_c = -(-10 * c_in * channels // 2048 // share) * share
    vmem = pltpu.VMEM

    def sums(blocks):
        unit = blocks // 2 // n_item
        return [
            vmem((blocks, 16, 128), BF16),
            vmem((blocks // 2, 16, 128), BF16),
            vmem((n_item - 1, unit, 16, 128), BF16),
            vmem((n_row - 1, unit // n_row, 16, 128), BF16),
        ]

    scratch = [
        pltpu.SemaphoreType.DMA((8 * n_row + 33,)),
        pltpu.SemaphoreType.DMA((4 * n_row + 39,)),
        vmem((n_group, -(-rows_t // 16) * 16, cols_t), BF16),
        vmem((n_group, tokens, channels), BF16),
        vmem((2, span, c_in), BF16),
        vmem((2, span, c_in), BF16),
        vmem((height, span), jnp.int32),
        vmem((height, span), jnp.int32),
        vmem((half, channels), BF16),
        vmem((half, channels), BF16),
        vmem((height + 2, span, 128), F32),
        vmem((tokens, 128), F32),
        vmem((span, c_in), F32),
        vmem((height + 4, span, c_in), F32),
        vmem((height, span, c_in), BF16),
        vmem((8, c_in), F32),
        vmem((3, 8, c_in), F32),
        vmem((n_group, 4, channels), F32),
        vmem((low, half, channels), BF16),
        vmem((channels, low * half), BF16),
        vmem((8, channels), F32),
        vmem((3, 8, channels), F32),
        vmem((8, channels, 2 * channels) if n_group < 8 or tokens < 2 * channels else (8, 16, 128), BF16),
        vmem((low + 2, half, 3 * channels), BF16),
        vmem((height + 2, span, channels), F32),
        vmem((height, span, c_in), F32),
        vmem((height + 4, span, 3 * c_in), BF16),
        vmem((height + 2, span, channels), F32),
        vmem((n_group, 2, channels), F32),
        vmem((n_group, tokens, channels), BF16),
        vmem((n_group, channels, tokens), BF16),
        vmem((tokens, channels), BF16),
        vmem((channels, tokens), BF16),
        vmem((tokens, channels), BF16),
        vmem((16, channels), F32),
        vmem((16, channels), F32),
        vmem((n_group, 2, channels), F32),
        vmem((3, c_in, 3 * channels), BF16),
        vmem((height, channels, span), BF16),
        vmem((16, channels), F32),
        vmem((16, channels), F32),
        vmem((height + 2, span, 3 * channels), BF16),
        vmem((low, half, c_in), BF16),
        *sums(blocks_a),
        *sums(blocks_b),
        *sums(blocks_c),
        vmem((height + 2, span, 3 * channels), BF16),
        vmem((n_group, 12, channels), F32),
        vmem((8, tokens), F32),
        vmem((n_group, 8, tokens), F32),
        vmem((8, tokens), F32),
        vmem((n_group, tokens, tokens), BF16),
        vmem((channels, tokens), F32),
        vmem((channels, tokens), BF16),
        vmem((channels, tokens), F32),
        vmem((tokens, channels), F32),
        vmem((n_group, tokens, channels), BF16),
        vmem((n_group, 4, tokens), F32),
        vmem((channels, channels), BF16),
        vmem((tokens, channels), BF16),
        vmem((tokens, channels), BF16),
        vmem((tokens, channels), F32),
        vmem((tokens, channels), F32),
        vmem((2, tokens, channels), BF16),
        pltpu.SemaphoreType.DMA((len(FETCHED) + len(RESULTS),)),
        *[vmem(inputs[INPUTS.index(name)].shape, BF16) for name in FETCHED],
    ]
    shape = jax.ShapeDtypeStruct
    mid = [
        shape((low, half, channels), BF16),
        shape((tokens, channels), BF16),
        shape((height, span, c_in), BF16),
        shape((tokens, channels), BF16),
        shape((blocks_a, 16, 128), BF16),
        shape((blocks_b, 16, 128), BF16),
        shape((blocks_c, 16, 128), BF16),
        shape((n_item, 20, channels), F32),
    ]
    scratch += [vmem(out.shape, out.dtype) for out in mid]
    in_vmem, anywhere = pl.BlockSpec(memory_space=vmem), pl.BlockSpec(memory_space=pl.ANY)
    parts = pl.pallas_call(
        functools.partial(main_kernel, n_item, n_row),
        out_shape=mid,
        in_specs=[anywhere if name in FETCHED else in_vmem for name in INPUTS],
        out_specs=[anywhere] * len(mid),
        scratch_shapes=scratch,
        compiler_params=pltpu.CompilerParams(
            collective_id=0, has_side_effects=True, vmem_limit_bytes=int(63.9 * 1024 * 1024)
        ),
    )(*inputs)
    emb = arg.embedding.shape[-1]
    final = [
        *mid[:4],
        shape((1, c_in), F32),
        shape((1, c_in), F32),
        shape((9 * c_in, channels), F32),
        shape((1, channels), F32),
        shape((emb, 2 * channels), F32),
        shape((1, 2 * channels), F32),
        shape((1, channels), F32),
        shape((1, channels), F32),
        shape((9 * channels, channels), F32),
        shape((1, channels), F32),
        shape((c_in, channels), F32),
        shape((1, channels), F32),
        shape((1, channels), F32),
        shape((1, channels), F32),
        shape((channels, 3 * channels), F32),
        shape((1, 2 * channels), F32),
        shape((channels, channels), F32),
        shape((1, channels), F32),
        shape((1, 5), F32),
    ]
    outs = pl.pallas_call(
        functools.partial(last_kernel, n_item),
        out_shape=final,
        in_specs=[anywhere] * len(mid),
        out_specs=[anywhere] * 4 + [anywhere if name in LAST_BIG else in_vmem for name in LAST_OUT],
        scratch_shapes=[
            *[vmem(out.shape, out.dtype) for out in mid],
            *[vmem(final[4 + LAST_OUT.index(name)].shape, F32) for name in LAST_BIG],
            pltpu.SemaphoreType.DMA((len(mid),)),
            pltpu.SemaphoreType.DMA((4 + len(LAST_BIG),)),
        ],
        compiler_params=pltpu.CompilerParams(vmem_limit_bytes=int(63.9 * 1024 * 1024)),
    )(*parts)
    shapes = (
        (1, low, half, channels),
        (1, rows_t, cols_t, channels),
        (1, height, span, c_in),
        (1, rows_t, cols_t, channels),
        (c_in,),
        (c_in,),
        (3, 3, c_in, channels),
        (channels,),
        (emb, 2 * channels),
        (2 * channels,),
        (channels,),
        (channels,),
        (3, 3, channels, channels),
        (channels,),
        (c_in, channels),
        (channels,),
        (channels,),
        (channels,),
        (channels, 3 * channels),
        (2 * channels,),
        (channels, channels),
        (channels,),
        (5,),
    )
    return tuple(out.reshape(to) for out, to in zip(outs, shapes))


def solution(mesh):
    tiled = P("item", "row", "pair", None)
    mask = P("item", "row", "pair")
    in_specs = [P()] * len(INPUTS)
    for name in ("image", "features", "gpool", "gres"):
        in_specs[INPUTS.index(name)] = tiled
    for name in ("land", "token"):
        in_specs[INPUTS.index(name)] = mask
    in_specs[INPUTS.index("embedding")] = P("item", None)
    return jax.shard_map(
        functools.partial(on_device, dict(mesh.shape)),
        mesh=mesh,
        in_specs=tuple(in_specs),
        out_specs=(tiled,) * 4 + (P(),) * 19,
        check_vma=False,
    )
```
